256 devices in a mesh: inner: 64 (over y, x, z_hi), outer: 2 (over core), dp: 2 (over z_lo).
Axes of the slice: x: 4, y: 4, z: 8 (z_hi: 4, z_lo: 2; z = z_hi * 2 + z_lo), core: 2. Of those that a mesh axis runs over, the one named last changes fastest.
Arguments:
- inputs: bfloat16 [2, 256, 512, 768], P('dp', ('inner', 'outer')), may hold values from -6 to 6
- gate_in: bfloat16 [2, 256, 512, 768], P('dp', ('inner', 'outer')), may hold values from -6 to 6
- grad_out: bfloat16 [2, 256, 512, 768], P('dp', ('inner', 'outer')), may hold values from -6 to 6
- right_factor: bfloat16 [2, 512, 512], replicated, may hold values from -0.25 to 0.25
- left_factor: bfloat16 [2, 256, 256], replicated, may hold values from -0.375 to 0.375
Outputs:
- grad_inputs: bfloat16 [2, 256, 512, 768], P('dp', ('inner', 'outer'))
- grad_gate: bfloat16 [2, 256, 512, 768], P('dp', ('inner', 'outer'))
- grad_right: float32 [2, 512, 512], P('dp')
- grad_left: float32 [2, 256, 256], P('dp')
The draws below stay inside these ranges and needn't reach their ends.
All inputs are finite; a program needn't handle non-finite values.
Results may differ from the reference program's by a relative error of at most 0.018.
Values may be sent and summed in bfloat16 or wider, within the bound.
A program may use at most 64 MiB of HBM per device.

```python
import jax
import jax.numpy as jnp
from jax import lax

P_SIZE = 256
Q = 512
CG = 384
GROUPS = 2
C = 768
BATCH = 2


def block_levels(rng, extent, shards, least, top_value):
    level, own = 1.0, jax.random.fold_in(rng, 6)
    for position, parts in shards:
        draws = jnp.exp(jax.random.uniform(jax.random.fold_in(own, position), (parts,), jnp.float32, least / len(shards), top_value / len(shards)))
        level = level * jnp.repeat(draws, extent[position] // parts).reshape([-1 if axis == position else 1 for axis in range(len(extent))])
    return level


def centred(rng, dims, width, limit, shards=(), kind=jnp.bfloat16):
    entries = jax.random.normal(rng, dims, jnp.float32) * width
    if len(shards) > 0:
        entries = block_levels(rng, dims, shards, -0.22, 0.18) * entries
    return jnp.clip(entries, min=-limit, max=limit).astype(kind)


def setup_inputs(seed: int = 0) -> dict:
    key_of = jax.random.split(jax.random.key(seed), 6)
    inputs = centred(key_of[0], (BATCH, P_SIZE, Q, C), 1.0, 6.0, ((0, 2), (1, 128)))
    gate_in = centred(key_of[1], (BATCH, P_SIZE, Q, C), 1.0, 6.0, ((0, 2), (1, 128)))
    grad_out = centred(key_of[2], (BATCH, P_SIZE, Q, C), 1.0, 6.0, ((0, 2), (1, 128)))
    right_factor = centred(key_of[3], (GROUPS, Q, Q), Q ** -0.5, 0.25)
    left_factor = centred(key_of[4], (GROUPS, P_SIZE, P_SIZE), P_SIZE ** -0.5, 0.375)
    return dict(inputs=inputs, gate_in=gate_in, grad_out=grad_out, right_factor=right_factor, left_factor=left_factor)


def to_bf16_and_back(values):
    return lax.optimization_barrier(values.astype(jnp.bfloat16)).astype(jnp.float32)


def gelu_value(mixed):
    return mixed * (0.5 * (1.0 + jax.scipy.special.erf(mixed * 0.7071067811865476)))


def gelu_slope(mixed):
    normal_cdf = 0.5 * (1.0 + jax.scipy.special.erf(mixed * 0.7071067811865476))
    density = jnp.exp(-0.5 * mixed * mixed) * 0.3989422804014327
    return normal_cdf + mixed * density


def one_sequence(inputs, gate_in, grad_out, right_wide, left_wide):
    groups = right_wide.shape[0]
    x_wide = inputs.astype(jnp.float32).reshape(P_SIZE, Q, groups, CG)
    gate_wide = gate_in.astype(jnp.float32).reshape(P_SIZE, Q, groups, CG)
    grad_wide = grad_out.astype(jnp.float32).reshape(P_SIZE, Q, groups, CG)
    mixed_cols = to_bf16_and_back(jnp.einsum("gab,pbgc->pagc", right_wide, x_wide))
    mixed = jnp.einsum("gpr,rqgc->pqgc", left_wide, mixed_cols)
    mixed_b = to_bf16_and_back(mixed)
    slope = gelu_slope(mixed)
    act = gelu_value(mixed_b)
    grad_gate = (grad_wide * act).astype(jnp.bfloat16)
    weighted = to_bf16_and_back(grad_wide * gate_wide)
    grad_mixed = to_bf16_and_back(weighted * slope)
    grad_left = jnp.einsum("pqgc,rqgc->gpr", grad_mixed, mixed_cols)
    grad_cols = to_bf16_and_back(jnp.einsum("gpr,pqgc->rqgc", left_wide, grad_mixed))
    grad_right = jnp.einsum("pagc,pbgc->gab", grad_cols, x_wide)
    grad_inputs = jnp.einsum("gab,pagc->pbgc", right_wide, grad_cols).astype(jnp.bfloat16)
    return grad_inputs.reshape(P_SIZE, Q, -1), grad_gate.reshape(P_SIZE, Q, -1), grad_right, grad_left


def reference(inputs, gate_in, grad_out, right_factor, left_factor):
    right_wide = right_factor.astype(jnp.float32)
    left_wide = left_factor.astype(jnp.float32)

    def step(carry, items):
        grad_inputs, grad_gate, grad_right, grad_left = one_sequence(items[0], items[1], items[2], right_wide, left_wide)
        return (carry[0] + grad_right, carry[1] + grad_left), (grad_inputs, grad_gate)

    start = (jnp.zeros(right_factor.shape, jnp.float32), jnp.zeros(left_factor.shape, jnp.float32))
    totals, outputs = lax.scan(step, start, (inputs, gate_in, grad_out))
    return outputs[0], outputs[1], totals[0], totals[1]
```

```python
import jax
import jax.numpy as jnp
from jax import lax
from jax.experimental import pallas as pl
from jax.experimental.pallas import tpu as pltpu
from jax.sharding import PartitionSpec as P

MESH = pl.DeviceIdType.MESH
F32 = jnp.float32
BF16 = jnp.bfloat16

INNER = 64
ZH = 4
XY = 16
PEERS = 128
ROWS = 2
CG = 384
LANES = CG // 128
Q = 512
P_ALL = 256
QB = 8
BLK = ROWS * QB
FIRST, SECOND, THIRD = 1, 2, 3


def gelu_value(mixed):
    return mixed * (0.5 * (1.0 + lax.erf(mixed * 0.7071067811865476)))


def gelu_slope(mixed):
    normal_cdf = 0.5 * (1.0 + lax.erf(mixed * 0.7071067811865476))
    density = jnp.exp(-0.5 * mixed * mixed) * 0.3989422804014327
    return normal_cdf + mixed * density


def wait_bytes(ref, sem):
    pltpu.make_async_copy(ref, ref, sem).wait()


def dot(a, b, ca, cb):
    return lax.dot_general(a, b, (((ca,), (cb,)), ((), ())), preferred_element_type=F32)


def kernel(
    x, gate, gout, rf, lf,
    gin_o, ggate_o, gr_o, gl_o,
    s1, s2, r1, r2, t1, t2, b1, b2,
    wide_a, wide_b, slope, colsb, gcb, rt, lt,
    grp, cx, rs_s, rs_r, ls_s, ls_r, share, zrecv, fin,
    a_send, a_recv, m_send, m_recv, q_send, q_recv,
):
    i = lax.axis_index("inner")
    c = lax.axis_index("outer")
    d = lax.axis_index("dp")
    me = i * 2 + c
    zh = i % ZH
    j = i // ZH
    yy = j // 4
    xx = j % 4

    barrier = pltpu.get_barrier_semaphore()

    def greet(k, _):
        s = (me + k) % PEERS
        pl.semaphore_signal(barrier, inc=1, device_id={"inner": s // 2, "outer": s % 2}, device_id_type=MESH)
        return 0

    lax.fori_loop(1, PEERS, greet, 0)

    def greet_z(k, _):
        pl.semaphore_signal(
            barrier, inc=1, device_id={"inner": j * ZH + (zh + k) % ZH, "dp": 1 - d}, device_id_type=MESH
        )
        return 0

    lax.fori_loop(0, ZH, greet_z, 0)

    def right_mix(m, _):
        for g in range(2):
            lhs = rf[g, pl.ds(pl.multiple_of(m * 128, 128), 128), :]
            parts = [
                dot(lhs, x[0, p, :, g * CG:(g + 1) * CG], 1, 0).reshape(16, QB, CG) for p in range(ROWS)
            ]
            s1[g, pl.ds(m * 16, 16)] = jnp.concatenate(parts, axis=1).astype(BF16)
        return 0

    lax.fori_loop(0, 4, right_mix, 0)

    pl.semaphore_wait(barrier, PEERS - 1 + ZH)

    def partner(k, dy):
        jj = ((yy + dy) % 4) * 4 + (xx + k // 8) % 4
        return jj * ZH + (zh + (k // 2) % 4) % ZH, (c + k) % 2

    def send_out(src, dst, n):
        for dy in range(4):
            def step(k, _):
                ii, cc = partner(k, dy)
                pltpu.make_async_remote_copy(
                    src_ref=src.at[cc, ii], dst_ref=dst.at[me], send_sem=a_send.at[n], recv_sem=a_recv.at[n],
                    device_id={"inner": ii, "outer": cc}, device_id_type=MESH,
                ).start()
                return 0

            lax.fori_loop(1 if dy == 0 else 0, 32, step, 0)

    def send_back(src, dst, n, dy):
        def step(k, _):
            ii, cc = partner(k, dy)
            pltpu.make_async_remote_copy(
                src_ref=src.at[ii * 2 + cc], dst_ref=dst.at[c, j, zh], send_sem=a_send.at[n],
                recv_sem=a_recv.at[4 * n - 6 + dy],
                device_id={"inner": ii, "outer": cc}, device_id_type=MESH,
            ).start()
            return 0

        lax.fori_loop(1 if dy == 0 else 0, 32, step, 0)

    def wait_back(n, dy):
        wait_bytes(t1.at[pl.ds(0, 31 if dy == 0 else 32)], a_recv.at[4 * n - 6 + dy])

    send_out(s1, r1, 0)

    def weigh(m, _):
        rows = pl.ds(pl.multiple_of(m * 64, 64), 64)
        for g in range(2):
            parts = []
            for p in range(ROWS):
                a = gout[0, p, rows, g * CG:(g + 1) * CG].astype(F32)
                b = gate[0, p, rows, g * CG:(g + 1) * CG].astype(F32)
                parts.append((a * b).reshape(8, QB, CG))
            s2[g, pl.ds(m * 8, 8)] = jnp.concatenate(parts, axis=1).astype(BF16)
        return 0

    lax.fori_loop(0, 8, weigh, 0)
    send_out(s2, r2, 1)

    r1[me] = s1[c, i]
    r2[me] = s2[c, i]
    lfac = lf[c]
    lt[...] = lfac.astype(F32).T.astype(BF16)
    for g in range(2):
        for h in range(2):
            rt[g, :, h * 256:(h + 1) * 256] = rf[g, h * 256:(h + 1) * 256, :].astype(F32).T.astype(BF16)

    def widen(src):
        def step(m, _):
            v = src[pl.ds(m * 4, 4)].reshape(64, CG).astype(F32)
            for n in range(LANES):
                wide_a[n, pl.ds(pl.multiple_of(m * 64, 64), 64), :] = v[:, n * 128:(n + 1) * 128]
            return 0

        lax.fori_loop(0, 32, step, 0)

    def narrow(dst):
        def step(m, _):
            for n in range(LANES):
                v = wide_b[n, pl.ds(pl.multiple_of(m * 64, 64), 64), :].astype(BF16)
                dst[pl.ds(m * 4, 4), :, n * 128:(n + 1) * 128] = v.reshape(4, BLK, 128)
            return 0

        lax.fori_loop(0, 32, step, 0)

    def column(q):
        return jnp.concatenate([wide_a[n, pl.ds(q, P_ALL, stride=QB), :] for n in range(LANES)], axis=1)

    def put_column(q, v):
        for n in range(LANES):
            wide_b[n, pl.ds(q, P_ALL, stride=QB), :] = v[:, n * 128:(n + 1) * 128]

    wait_bytes(r1.at[pl.ds(0, PEERS - 1)], a_recv.at[0])
    widen(r1)
    for q in range(QB):
        xq = column(q).astype(BF16)
        colsb[q] = xq
        mixed = dot(lfac, xq, 1, 0)
        put_column(q, mixed)
        slope[q] = mixed
    narrow(t1)
    b1[c, j, zh] = t1[me]
    for dy in range(FIRST):
        send_back(t1, b1, 2, dy)

    def slopes(m, _):
        rows = pl.ds(pl.multiple_of((m % 4) * 64, 64), 64)
        slope[m // 4, rows, :] = gelu_slope(slope[m // 4, rows, :])
        return 0

    lax.fori_loop(0, QB * 4, slopes, 0)

    wait_bytes(r2.at[pl.ds(0, PEERS - 1)], a_recv.at[1])
    widen(r2)
    gl_acc = jnp.zeros((P_ALL, P_ALL), F32)
    for q in range(QB):
        gm = (column(q) * slope[q]).astype(BF16)
        put_column(q, dot(lt[...], gm, 1, 0))
        gl_acc = gl_acc + dot(gm, colsb[q], 1, 1)
    narrow(t2)
    b2[c, j, zh] = t2[me]
    for dy in range(4):
        send_back(t2, b2, 3, dy)
    for dy in range(FIRST, SECOND):
        send_back(t1, b1, 2, dy)
    ls_s[...] = gl_acc.astype(BF16).reshape(XY, 16, P_ALL)

    def scatter(src, dst, n, dy):
        y2 = (yy + 4 - dy) % 4

        def step(k, _):
            jj = y2 * 4 + (xx + k) % 4
            pltpu.make_async_remote_copy(
                src_ref=src.at[jj], dst_ref=dst.at[j], send_sem=m_send.at[n], recv_sem=m_recv.at[n],
                device_id={"inner": jj * ZH + zh}, device_id_type=MESH,
            ).start()
            return 0

        lax.fori_loop(1 if dy == 0 else 0, 4, step, 0)

    for dy in range(4):
        scatter(ls_s, ls_r, 0, dy)
    ls_r[j] = ls_s[j]

    def gate_grad(dy):
        wait_back(2, dy)
        y2 = (yy + 4 - dy) % 4

        def step(m, _):
            for g in range(2):
                cols = slice(g * CG, (g + 1) * CG)
                v = b1[g, pl.ds(y2 * 4 + m * 2, 2)].reshape(8, BLK, CG).astype(F32)
                rows = pl.ds(pl.multiple_of(y2 * 128 + m * 64, 64), 64)
                for p in range(ROWS):
                    act = gelu_value(v[:, p * QB:(p + 1) * QB, :].reshape(64, CG))
                    ggate_o[0, p, rows, cols] = (gout[0, p, rows, cols].astype(F32) * act).astype(BF16)
            return 0

        lax.fori_loop(0, 2, step, 0)

    for dy in range(FIRST):
        gate_grad(dy)

    def swap(dy):
        rows = pl.ds(pl.multiple_of(((yy + 4 - dy) % 4) * 128, 128), 128)
        return pltpu.make_async_remote_copy(
            src_ref=grp.at[1 - c, rows], dst_ref=cx.at[rows], send_sem=q_send.at[dy], recv_sem=q_recv.at[dy],
            device_id={"outer": 1 - c}, device_id_type=MESH,
        )

    def finish(dy):
        swap(dy).wait()
        y2 = (yy + 4 - dy) % 4

        def step(m, _):
            rows = pl.ds(pl.multiple_of(y2 * 128 + m * 32, 32), 32)
            rs_s[y2 * 4 + m] = (grp[c, rows, :] + cx[rows, :]).astype(BF16)
            return 0

        lax.fori_loop(0, 4, step, 0)
        scatter(rs_s, rs_r, 2, dy)

    for dy in range(4):
        wait_back(3, dy)
        y2 = (yy + 4 - dy) % 4
        rows = pl.ds(pl.multiple_of(y2 * 128, 128), 128)
        for g in range(2):
            cols = slice(g * CG, (g + 1) * CG)
            v = b2[g, pl.ds(y2 * 4, 4)].reshape(16, BLK, CG).astype(F32)
            total = None
            for p in range(ROWS):
                part = v[:, p * QB:(p + 1) * QB, :].reshape(128, CG).astype(BF16)
                gcb[p, rows, cols] = part
                term = dot(part, x[0, p, :, cols], 1, 1)
                total = term if total is None else total + term
            grp[g, rows, :] = total
        swap(dy).start()
        if dy > 0:
            finish(dy - 1)
    finish(3)
    rs_r[j] = rs_s[j]
    for dy in range(SECOND, THIRD):
        send_back(t1, b1, 2, dy)

    def input_grad(m, _):
        rows = pl.ds(pl.multiple_of(m * 128, 128), 128)
        for g in range(2):
            cols = slice(g * CG, (g + 1) * CG)
            for p in range(ROWS):
                gin_o[0, p, rows, cols] = dot(rt[g, rows, :], gcb[p, :, cols], 1, 0).astype(BF16)
        return 0

    lax.fori_loop(0, 4, input_grad, 0)

    wait_bytes(ls_r.at[pl.ds(0, XY - 1)], m_recv.at[0])
    wait_bytes(rs_r.at[pl.ds(0, XY - 1)], m_recv.at[2])
    gr_sum = rs_r[0].astype(F32)
    gl_sum = ls_r[0].astype(F32)
    for k in range(1, XY):
        gr_sum = gr_sum + rs_r[k].astype(F32)
        gl_sum = gl_sum + ls_r[k].astype(F32)
    share[0:32, :] = gr_sum[:, 0:256].astype(BF16)
    share[32:64, :] = gr_sum[:, 256:512].astype(BF16)
    share[64:80, :] = gl_sum.astype(BF16)

    def to_z(k):
        return pltpu.make_async_remote_copy(
            src_ref=share, dst_ref=zrecv.at[zh * 2 + d], send_sem=m_send.at[3], recv_sem=m_recv.at[3],
            device_id={"inner": j * ZH + (zh + k) % ZH, "dp": c}, device_id_type=MESH,
        )

    for k in range(1, ZH):
        to_z(k).start()

    @pl.when(d != c)
    def _():
        to_z(0).start()

    for dy in range(THIRD, 4):
        send_back(t1, b1, 2, dy)
    for dy in range(FIRST, SECOND):
        gate_grad(dy)

    @pl.when(d == c)
    def _():
        zrecv[zh * 2 + d] = share[...]
        wait_bytes(zrecv.at[pl.ds(0, 7)], m_recv.at[3])
        total = zrecv[0].astype(F32)
        for k in range(1, 8):
            total = total + zrecv[k].astype(F32)
        fin[j] = total.astype(BF16)

        def give(k, _):
            jj = (j + k) % XY
            pltpu.make_async_remote_copy(
                src_ref=fin.at[j], dst_ref=fin.at[j], send_sem=m_send.at[4], recv_sem=m_recv.at[4],
                device_id={"inner": jj * ZH + zh}, device_id_type=MESH,
            ).start()
            return 0

        lax.fori_loop(1, XY, give, 0)

    for dy in range(SECOND, 4):
        gate_grad(dy)

    @pl.when(d == c)
    def _():
        wait_bytes(fin.at[pl.ds(0, XY - 1)], m_recv.at[4])
        over = pltpu.make_async_remote_copy(
            src_ref=fin, dst_ref=fin, send_sem=m_send.at[5], recv_sem=m_recv.at[5],
            device_id={"outer": 1 - c}, device_id_type=MESH,
        )
        over.start()
        wait_bytes(fin.at[pl.ds(0, XY - 1)], m_send.at[4])
        wait_bytes(zrecv.at[pl.ds(0, 3)], m_send.at[3])
        wait_bytes(fin, m_send.at[5])

    @pl.when(d != c)
    def _():
        wait_bytes(zrecv.at[pl.ds(0, 4)], m_send.at[3])
        wait_bytes(fin, m_recv.at[5])

    for k in range(XY):
        gr_o[0, k * 32:(k + 1) * 32, 0:256] = fin[k, 0:32, :].astype(F32)
        gr_o[0, k * 32:(k + 1) * 32, 256:512] = fin[k, 32:64, :].astype(F32)
        gl_o[0, k * 16:(k + 1) * 16, :] = fin[k, 64:80, :].astype(F32)

    for n in range(4):
        wait_bytes(r1.at[pl.ds(0, PEERS - 1)], a_send.at[n])
    wait_bytes(ls_r.at[pl.ds(0, XY - 1)], m_send.at[0])
    wait_bytes(rs_r.at[pl.ds(0, XY - 1)], m_send.at[2])


def body(inputs, gate_in, grad_out, right_factor, left_factor):
    vmem = pl.BlockSpec(memory_space=pltpu.VMEM)
    out_shape = (
        jax.ShapeDtypeStruct((1, ROWS, Q, 2 * CG), BF16),
        jax.ShapeDtypeStruct((1, ROWS, Q, 2 * CG), BF16),
        jax.ShapeDtypeStruct((1, Q, Q), F32),
        jax.ShapeDtypeStruct((1, P_ALL, P_ALL), F32),
    )
    scratch = [
        pltpu.VMEM((2, INNER, BLK, CG), BF16),
        pltpu.VMEM((2, INNER, BLK, CG), BF16),
        pltpu.VMEM((PEERS, BLK, CG), BF16),
        pltpu.VMEM((PEERS, BLK, CG), BF16),
        pltpu.VMEM((PEERS, BLK, CG), BF16),
        pltpu.VMEM((PEERS, BLK, CG), BF16),
        pltpu.VMEM((2, XY, ZH, BLK, CG), BF16),
        pltpu.VMEM((2, XY, ZH, BLK, CG), BF16),
        pltpu.VMEM((LANES, PEERS * BLK, 128), F32),
        pltpu.VMEM((LANES, PEERS * BLK, 128), F32),
        pltpu.VMEM((QB, P_ALL, CG), F32),
        pltpu.VMEM((QB, P_ALL, CG), BF16),
        pltpu.VMEM((ROWS, Q, 2 * CG), BF16),
        pltpu.VMEM((2, Q, Q), BF16),
        pltpu.VMEM((P_ALL, P_ALL), BF16),
        pltpu.VMEM((2, Q, Q), F32),
        pltpu.VMEM((Q, Q), F32),
        pltpu.VMEM((XY, 32, Q), BF16),
        pltpu.VMEM((XY, 32, Q), BF16),
        pltpu.VMEM((XY, 16, P_ALL), BF16),
        pltpu.VMEM((XY, 16, P_ALL), BF16),
        pltpu.VMEM((80, 256), BF16),
        pltpu.VMEM((8, 80, 256), BF16),
        pltpu.VMEM((XY, 80, 256), BF16),
        pltpu.SemaphoreType.DMA((4,)),
        pltpu.SemaphoreType.DMA((10,)),
        pltpu.SemaphoreType.DMA((6,)),
        pltpu.SemaphoreType.DMA((6,)),
        pltpu.SemaphoreType.DMA((4,)),
        pltpu.SemaphoreType.DMA((4,)),
    ]
    return pl.pallas_call(
        kernel,
        out_shape=out_shape,
        in_specs=[vmem] * 5,
        out_specs=(vmem,) * 4,
        scratch_shapes=scratch,
        compiler_params=pltpu.CompilerParams(
            collective_id=0, has_side_effects=True, vmem_limit_bytes=56 * 1024 * 1024
        ),
        cost_estimate=pl.CostEstimate(flops=4 * 10**9, bytes_accessed=12 * 10**6, transcendentals=3 * 10**6),
    )(inputs, gate_in, grad_out, right_factor, left_factor)


def solution(mesh):
    rows = P("dp", ("inner", "outer"), None, None)
    return jax.shard_map(
        body,
        mesh=mesh,
        in_specs=(rows, rows, rows, P(), P()),
        out_specs=(rows, rows, P("dp", None, None), P("dp", None, None)),
        check_vma=False,
    )
```

```python
import jax
import jax.numpy as jnp
from jax import lax
from jax.experimental import pallas as pl
from jax.experimental.pallas import tpu as pltpu
from jax.sharding import PartitionSpec as P

MESH = pl.DeviceIdType.MESH
F32 = jnp.float32
BF16 = jnp.bfloat16

INNER = 64
ZH = 4
XY = 16
PEERS = 128
ROWS = 2
CG = 384
LANES = CG // 128
Q = 512
P_ALL = 256
QB = 8
BLK = ROWS * QB
FIRST, SECOND, THIRD = 1, 2, 3


def gelu_value(mixed):
    return mixed * (0.5 * (1.0 + lax.erf(mixed * 0.7071067811865476)))


def gelu_slope(mixed):
    normal_cdf = 0.5 * (1.0 + lax.erf(mixed * 0.7071067811865476))
    density = jnp.exp(-0.5 * mixed * mixed) * 0.3989422804014327
    return normal_cdf + mixed * density


def wait_bytes(ref, sem):
    pltpu.make_async_copy(ref, ref, sem).wait()


def dot(a, b, ca, cb):
    return lax.dot_general(a, b, (((ca,), (cb,)), ((), ())), preferred_element_type=F32)


def kernel(
    x_h, gate_h, gout_h, rf_h, lf_h,
    gin_o, ggate_o, gr_o, gl_o,
    s1, s2, r1, r2, t1, t2, b1, b2,
    x, gate, gout, rf, lf, gin_v, ggate_v, gr_v, gl_v,
    wide_a, wide_b, slope, colsb, gmb, gcb, rt, lt,
    grp, cx, rs_s, rs_r, ls_s, ls_r, share, zrecv, fin,
    a_send, a_recv, m_send, m_recv, q_send, q_recv, l_sem,
):
    i = lax.axis_index("inner")
    c = lax.axis_index("outer")
    d = lax.axis_index("dp")
    me = i * 2 + c
    zh = i % ZH
    j = i // ZH
    yy = j // 4
    xx = j % 4

    loads = [
        pltpu.make_async_copy(src, dst, l_sem.at[n])
        for n, (src, dst) in enumerate(
            ((x_h.at[0], x), (rf_h, rf), (gate_h.at[0], gate), (gout_h.at[0], gout), (lf_h, lf))
        )
    ]
    for load in loads:
        load.start()

    barrier = pltpu.get_barrier_semaphore()

    def greet(k, _):
        s = (me + k) % PEERS
        pl.semaphore_signal(barrier, inc=1, device_id={"inner": s // 2, "outer": s % 2}, device_id_type=MESH)
        return 0

    lax.fori_loop(1, PEERS, greet, 0)

    def greet_z(k, _):
        pl.semaphore_signal(
            barrier, inc=1, device_id={"inner": j * ZH + (zh + k) % ZH, "dp": 1 - d}, device_id_type=MESH
        )
        return 0

    lax.fori_loop(0, ZH, greet_z, 0)

    loads[0].wait()
    loads[1].wait()

    def right_mix(m, _):
        for g in range(2):
            lhs = rf[g, pl.ds(pl.multiple_of(m * 128, 128), 128), :]
            parts = [
                dot(lhs, x[p, :, g * CG:(g + 1) * CG], 1, 0).reshape(16, QB, CG) for p in range(ROWS)
            ]
            s1[g, pl.ds(m * 16, 16)] = jnp.concatenate(parts, axis=1).astype(BF16)
        return 0

    lax.fori_loop(0, 4, right_mix, 0)

    pl.semaphore_wait(barrier, PEERS - 1 + ZH)

    def place(e, t, sign):
        return ((yy + sign * (e + t) + 8) % 4) * 4 + (xx + sign * t + 4) % 4

    def partner(k, e):
        jj = place(e, k % 4, 1)
        return jj * ZH + (zh + k % 4 + k // 4) % ZH, (c + k // 16) % 2

    def send_out(src, dst, n):
        for e in range(4):
            def step(k, _):
                ii, cc = partner(k, e)
                pltpu.make_async_remote_copy(
                    src_ref=src.at[cc, ii], dst_ref=dst.at[me], send_sem=a_send.at[n], recv_sem=a_recv.at[n],
                    device_id={"inner": ii, "outer": cc}, device_id_type=MESH,
                ).start()
                return 0

            lax.fori_loop(1 if e == 0 else 0, 32, step, 0)

    def send_back(src, dst, n, e):
        def step(k, _):
            ii, cc = partner(k, e)
            pltpu.make_async_remote_copy(
                src_ref=src.at[ii * 2 + cc], dst_ref=dst.at[c, j, zh], send_sem=a_send.at[n],
                recv_sem=a_recv.at[4 * n - 6 + e],
                device_id={"inner": ii, "outer": cc}, device_id_type=MESH,
            ).start()
            return 0

        lax.fori_loop(1 if e == 0 else 0, 32, step, 0)

    def wait_back(n, e):
        wait_bytes(t1.at[pl.ds(0, 31 if e == 0 else 32)], a_recv.at[4 * n - 6 + e])

    send_out(s1, r1, 0)

    loads[2].wait()
    loads[3].wait()

    def weigh(m, _):
        rows = pl.ds(pl.multiple_of(m * 64, 64), 64)
        for g in range(2):
            parts = []
            for p in range(ROWS):
                a = gout[p, rows, g * CG:(g + 1) * CG].astype(F32)
                b = gate[p, rows, g * CG:(g + 1) * CG].astype(F32)
                parts.append((a * b).reshape(8, QB, CG))
            s2[g, pl.ds(m * 8, 8)] = jnp.concatenate(parts, axis=1).astype(BF16)
        return 0

    lax.fori_loop(0, 8, weigh, 0)
    send_out(s2, r2, 1)

    r1[me] = s1[c, i]
    r2[me] = s2[c, i]
    loads[4].wait()
    lfac = lf[c]
    lt[...] = lfac.astype(F32).T.astype(BF16)
    for g in range(2):
        for h in range(2):
            rt[g, :, h * 256:(h + 1) * 256] = rf[g, h * 256:(h + 1) * 256, :].astype(F32).T.astype(BF16)

    def widen(src):
        def step(m, _):
            v = src[pl.ds(m * 4, 4)].reshape(64, CG).astype(F32)
            for n in range(LANES):
                wide_a[n, pl.ds(pl.multiple_of(m * 64, 64), 64), :] = v[:, n * 128:(n + 1) * 128]
            return 0

        lax.fori_loop(0, 32, step, 0)

    def narrow(dst):
        def step(m, _):
            for n in range(LANES):
                v = wide_b[n, pl.ds(pl.multiple_of(m * 64, 64), 64), :].astype(BF16)
                dst[pl.ds(m * 4, 4), :, n * 128:(n + 1) * 128] = v.reshape(4, BLK, 128)
            return 0

        lax.fori_loop(0, 32, step, 0)

    def column(q):
        return jnp.concatenate([wide_a[n, pl.ds(q, P_ALL, stride=QB), :] for n in range(LANES)], axis=1)

    def put_column(q, v):
        for n in range(LANES):
            wide_b[n, pl.ds(q, P_ALL, stride=QB), :] = v[:, n * 128:(n + 1) * 128]

    wait_bytes(r1.at[pl.ds(0, PEERS - 1)], a_recv.at[0])
    widen(r1)
    for q in range(QB):
        xq = column(q).astype(BF16)
        colsb[q] = xq
        mixed = dot(lfac, xq, 1, 0)
        put_column(q, mixed)
        slope[q] = mixed
    narrow(t1)
    b1[c, j, zh] = t1[me]
    for e in range(FIRST):
        send_back(t1, b1, 2, e)

    def slopes(m, _):
        rows = pl.ds(pl.multiple_of((m % 4) * 64, 64), 64)
        slope[m // 4, rows, :] = gelu_slope(slope[m // 4, rows, :])
        return 0

    lax.fori_loop(0, QB * 4, slopes, 0)

    wait_bytes(r2.at[pl.ds(0, PEERS - 1)], a_recv.at[1])
    widen(r2)
    for q in range(QB):
        gm = (column(q) * slope[q]).astype(BF16)
        put_column(q, dot(lt[...], gm, 1, 0))
        gmb[q] = gm
    narrow(t2)
    b2[c, j, zh] = t2[me]
    for e in range(4):
        send_back(t2, b2, 3, e)
    for e in range(FIRST, SECOND):
        send_back(t1, b1, 2, e)
    gl_acc = jnp.zeros((P_ALL, P_ALL), F32)
    for q in range(QB):
        gl_acc = gl_acc + dot(gmb[q], colsb[q], 1, 1)
    ls_s[...] = gl_acc.astype(BF16).reshape(XY, 16, P_ALL)

    def scatter(src, dst, n, e):
        def step(t, _):
            jj = place(e, t, -1)
            pltpu.make_async_remote_copy(
                src_ref=src.at[jj], dst_ref=dst.at[j], send_sem=m_send.at[n], recv_sem=m_recv.at[n],
                device_id={"inner": jj * ZH + zh}, device_id_type=MESH,
            ).start()
            return 0

        lax.fori_loop(1 if e == 0 else 0, 4, step, 0)

    for e in range(4):
        scatter(ls_s, ls_r, 0, e)
    ls_r[j] = ls_s[j]

    def gate_grad(e):
        wait_back(2, e)

        def step(t, _):
            jj = place(e, t, -1)
            rows = pl.ds(pl.multiple_of(jj * 32, 32), 32)
            for g in range(2):
                cols = slice(g * CG, (g + 1) * CG)
                v = b1[g, jj].astype(F32)
                for p in range(ROWS):
                    act = gelu_value(v[:, p * QB:(p + 1) * QB, :].reshape(32, CG))
                    ggate_v[p, rows, cols] = (gout[p, rows, cols].astype(F32) * act).astype(BF16)
            for p in range(ROWS):
                pltpu.make_async_copy(ggate_v.at[p, rows], ggate_o.at[0, p, rows], l_sem.at[6]).start()
            return 0

        lax.fori_loop(0, 4, step, 0)

    for e in range(FIRST):
        gate_grad(e)

    def swap(e):
        return pltpu.make_async_remote_copy(
            src_ref=grp.at[1 - c, e], dst_ref=cx.at[e], send_sem=q_send.at[e], recv_sem=q_recv.at[e],
            device_id={"outer": 1 - c}, device_id_type=MESH,
        )

    def finish(e):
        swap(e).wait()
        for t in range(4):
            rows = slice(t * 32, (t + 1) * 32)
            rs_s[place(e, t, -1)] = (grp[c, e, rows, :] + cx[e, rows, :]).astype(BF16)
        scatter(rs_s, rs_r, 2, e)

    for e in range(4):
        wait_back(3, e)
        for g in range(2):
            cols = slice(g * CG, (g + 1) * CG)
            parts = [[], []]
            for t in range(4):
                jj = place(e, t, -1)
                rows = pl.ds(pl.multiple_of(jj * 32, 32), 32)
                v = b2[g, jj].astype(F32)
                for p in range(ROWS):
                    part = v[:, p * QB:(p + 1) * QB, :].reshape(32, CG).astype(BF16)
                    gcb[p, rows, cols] = part
                    parts[p].append(part)
            total = None
            for p in range(ROWS):
                term = dot(jnp.concatenate(parts[p], axis=0), x[p, :, cols], 1, 1)
                total = term if total is None else total + term
            grp[g, e] = total
        swap(e).start()
        if e > 0:
            finish(e - 1)
    finish(3)
    rs_r[j] = rs_s[j]
    for e in range(SECOND, THIRD):
        send_back(t1, b1, 2, e)

    def input_grad(m, _):
        rows = pl.ds(pl.multiple_of(m * 128, 128), 128)
        for g in range(2):
            cols = slice(g * CG, (g + 1) * CG)
            for p in range(ROWS):
                gin_v[p, rows, cols] = dot(rt[g, rows, :], gcb[p, :, cols], 1, 0).astype(BF16)
        return 0

    lax.fori_loop(0, 4, input_grad, 0)
    gin_out = pltpu.make_async_copy(gin_v, gin_o.at[0], l_sem.at[5])
    gin_out.start()

    wait_bytes(ls_r.at[pl.ds(0, XY - 1)], m_recv.at[0])
    wait_bytes(rs_r.at[pl.ds(0, XY - 1)], m_recv.at[2])
    gr_sum = rs_r[0].astype(F32)
    gl_sum = ls_r[0].astype(F32)
    for k in range(1, XY):
        gr_sum = gr_sum + rs_r[k].astype(F32)
        gl_sum = gl_sum + ls_r[k].astype(F32)
    share[0:32, :] = gr_sum[:, 0:256].astype(BF16)
    share[32:64, :] = gr_sum[:, 256:512].astype(BF16)
    share[64:80, :] = gl_sum.astype(BF16)

    def to_z(k):
        return pltpu.make_async_remote_copy(
            src_ref=share, dst_ref=zrecv.at[zh * 2 + d], send_sem=m_send.at[3], recv_sem=m_recv.at[3],
            device_id={"inner": j * ZH + (zh + k) % ZH, "dp": c}, device_id_type=MESH,
        )

    for k in range(1, ZH):
        to_z(k).start()

    @pl.when(d != c)
    def _():
        to_z(0).start()

    for e in range(THIRD, 4):
        send_back(t1, b1, 2, e)
    for e in range(FIRST, SECOND):
        gate_grad(e)

    @pl.when(d == c)
    def _():
        zrecv[zh * 2 + d] = share[...]
        wait_bytes(zrecv.at[pl.ds(0, 7)], m_recv.at[3])
        total = zrecv[0].astype(F32)
        for k in range(1, 8):
            total = total + zrecv[k].astype(F32)
        fin[j] = total.astype(BF16)

        def give(k, _):
            jj = (j + k) % XY
            pltpu.make_async_remote_copy(
                src_ref=fin.at[j], dst_ref=fin.at[j], send_sem=m_send.at[4], recv_sem=m_recv.at[4],
                device_id={"inner": jj * ZH + zh}, device_id_type=MESH,
            ).start()
            return 0

        lax.fori_loop(1, XY, give, 0)

    for e in range(SECOND, 4):
        gate_grad(e)

    @pl.when(d == c)
    def _():
        wait_bytes(fin.at[pl.ds(0, XY - 1)], m_recv.at[4])
        over = pltpu.make_async_remote_copy(
            src_ref=fin, dst_ref=fin, send_sem=m_send.at[5], recv_sem=m_recv.at[5],
            device_id={"outer": 1 - c}, device_id_type=MESH,
        )
        over.start()
        wait_bytes(fin.at[pl.ds(0, XY - 1)], m_send.at[4])
        wait_bytes(zrecv.at[pl.ds(0, 3)], m_send.at[3])
        wait_bytes(fin, m_send.at[5])

    @pl.when(d != c)
    def _():
        wait_bytes(zrecv.at[pl.ds(0, 4)], m_send.at[3])
        wait_bytes(fin, m_recv.at[5])

    for k in range(XY):
        gr_v[k * 32:(k + 1) * 32, 0:256] = fin[k, 0:32, :].astype(F32)
        gr_v[k * 32:(k + 1) * 32, 256:512] = fin[k, 32:64, :].astype(F32)
        gl_v[k * 16:(k + 1) * 16, :] = fin[k, 64:80, :].astype(F32)

    outs = (
        pltpu.make_async_copy(gr_v, gr_o.at[0], l_sem.at[7]),
        pltpu.make_async_copy(gl_v, gl_o.at[0], l_sem.at[8]),
    )
    for out in outs:
        out.start()
    for n in range(4):
        wait_bytes(r1.at[pl.ds(0, PEERS - 1)], a_send.at[n])
    wait_bytes(ls_r.at[pl.ds(0, XY - 1)], m_send.at[0])
    wait_bytes(rs_r.at[pl.ds(0, XY - 1)], m_send.at[2])
    wait_bytes(ggate_v, l_sem.at[6])
    gin_out.wait()
    for out in outs:
        out.wait()


def body(inputs, gate_in, grad_out, right_factor, left_factor):
    hbm = pl.BlockSpec(memory_space=pl.ANY)
    out_shape = (
        jax.ShapeDtypeStruct((1, ROWS, Q, 2 * CG), BF16),
        jax.ShapeDtypeStruct((1, ROWS, Q, 2 * CG), BF16),
        jax.ShapeDtypeStruct((1, Q, Q), F32),
        jax.ShapeDtypeStruct((1, P_ALL, P_ALL), F32),
    )
    scratch = [
        pltpu.VMEM((2, INNER, BLK, CG), BF16),
        pltpu.VMEM((2, INNER, BLK, CG), BF16),
        pltpu.VMEM((PEERS, BLK, CG), BF16),
        pltpu.VMEM((PEERS, BLK, CG), BF16),
        pltpu.VMEM((PEERS, BLK, CG), BF16),
        pltpu.VMEM((PEERS, BLK, CG), BF16),
        pltpu.VMEM((2, XY, ZH, BLK, CG), BF16),
        pltpu.VMEM((2, XY, ZH, BLK, CG), BF16),
        pltpu.VMEM((ROWS, Q, 2 * CG), BF16),
        pltpu.VMEM((ROWS, Q, 2 * CG), BF16),
        pltpu.VMEM((ROWS, Q, 2 * CG), BF16),
        pltpu.VMEM((2, Q, Q), BF16),
        pltpu.VMEM((2, P_ALL, P_ALL), BF16),
        pltpu.VMEM((ROWS, Q, 2 * CG), BF16),
        pltpu.VMEM((ROWS, Q, 2 * CG), BF16),
        pltpu.VMEM((Q, Q), F32),
        pltpu.VMEM((P_ALL, P_ALL), F32),
        pltpu.VMEM((LANES, PEERS * BLK, 128), F32),
        pltpu.VMEM((LANES, PEERS * BLK, 128), F32),
        pltpu.VMEM((QB, P_ALL, CG), F32),
        pltpu.VMEM((QB, P_ALL, CG), BF16),
        pltpu.VMEM((QB, P_ALL, CG), BF16),
        pltpu.VMEM((ROWS, Q, 2 * CG), BF16),
        pltpu.VMEM((2, Q, Q), BF16),
        pltpu.VMEM((P_ALL, P_ALL), BF16),
        pltpu.VMEM((2, 4, 128, Q), F32),
        pltpu.VMEM((4, 128, Q), F32),
        pltpu.VMEM((XY, 32, Q), BF16),
        pltpu.VMEM((XY, 32, Q), BF16),
        pltpu.VMEM((XY, 16, P_ALL), BF16),
        pltpu.VMEM((XY, 16, P_ALL), BF16),
        pltpu.VMEM((80, 256), BF16),
        pltpu.VMEM((8, 80, 256), BF16),
        pltpu.VMEM((XY, 80, 256), BF16),
        pltpu.SemaphoreType.DMA((4,)),
        pltpu.SemaphoreType.DMA((10,)),
        pltpu.SemaphoreType.DMA((6,)),
        pltpu.SemaphoreType.DMA((6,)),
        pltpu.SemaphoreType.DMA((4,)),
        pltpu.SemaphoreType.DMA((4,)),
        pltpu.SemaphoreType.DMA((9,)),
    ]
    return pl.pallas_call(
        kernel,
        out_shape=out_shape,
        in_specs=[hbm] * 5,
        out_specs=(hbm,) * 4,
        scratch_shapes=scratch,
        compiler_params=pltpu.CompilerParams(
            collective_id=0, has_side_effects=True, vmem_limit_bytes=56 * 1024 * 1024
        ),
        cost_estimate=pl.CostEstimate(flops=4 * 10**9, bytes_accessed=12 * 10**6, transcendentals=3 * 10**6),
    )(inputs, gate_in, grad_out, right_factor, left_factor)


def solution(mesh):
    rows = P("dp", ("inner", "outer"), None, None)
    return jax.shard_map(
        body,
        mesh=mesh,
        in_specs=(rows, rows, rows, P(), P()),
        out_specs=(rows, rows, P("dp", None, None), P("dp", None, None)),
        check_vma=False,
    )
```

```python
import jax
import jax.numpy as jnp
from jax import lax
from jax.experimental import pallas as pl
from jax.experimental.pallas import tpu as pltpu
from jax.sharding import PartitionSpec as P

MESH = pl.DeviceIdType.MESH
F32 = jnp.float32
BF16 = jnp.bfloat16

INNER = 64
ZH = 4
XY = 16
ROWS = 2
CHIP = 4
CG = 384
LANES = CG // 128
Q = 512
P_ALL = 256
QB = 8
BLK = CHIP * QB
FIRST, SECOND, THIRD = 1, 2, 3


def gelu_value(mixed):
    return mixed * (0.5 * (1.0 + lax.erf(mixed * 0.7071067811865476)))


def gelu_slope(mixed):
    normal_cdf = 0.5 * (1.0 + lax.erf(mixed * 0.7071067811865476))
    density = jnp.exp(-0.5 * mixed * mixed) * 0.3989422804014327
    return normal_cdf + mixed * density


def wait_bytes(ref, sem):
    pltpu.make_async_copy(ref, ref, sem).wait()


def dot(a, b, ca, cb):
    return lax.dot_general(a, b, (((ca,), (cb,)), ((), ())), preferred_element_type=F32)


def kernel(
    x_h, gate_h, gout_h, rf_h, lf_h,
    gin_o, ggate_o, gr_o, gl_o,
    s1, s2, r1, r2, t1, t2, b1, b2,
    x, gate, gout, rf, lf, gin_v, ggate_v, gr_v, gl_v,
    wide_a, wide_b, wide_c, colsb, gmb, gcb, rt, lt,
    rs_s, rs_r, ls_s, ls_r, share, zrecv, fin,
    a_send, a_recv, m_send, m_recv, e_send, e_recv, l_sem,
):
    i = lax.axis_index("inner")
    c = lax.axis_index("outer")
    d = lax.axis_index("dp")
    zh = i % ZH
    j = i // ZH
    ys = [(j // 4 + n) % 4 for n in range(4)]
    xs = [(j % 4 + n) % 4 for n in range(4)]
    mine = pl.ds(pl.multiple_of(c * CG, CG), CG)
    theirs = pl.ds(pl.multiple_of((1 - c) * CG, CG), CG)
    my_rows = pl.ds(c * ROWS, ROWS)
    their_rows = pl.ds((1 - c) * ROWS, ROWS)

    def place(e, t, sign):
        return ys[sign * (e + t) % 4] * 4 + xs[sign * t % 4]

    def source(e, t):
        return lax.rem(ys[0] + 8 - e - t, 4) * 4 + lax.rem(xs[0] + 4 - t, 4)

    def each_partner(e, act):
        if e == 0:
            for t in range(1, 4):
                act(place(e, t, 1) * ZH + (zh + t) % ZH)

        def step(u, _):
            for t in range(4):
                act(place(e, t, 1) * ZH + lax.rem(zh + t + u, ZH))
            return 0

        lax.fori_loop(1 if e == 0 else 0, ZH, step, 0)

    arrays = ((x_h, x), (gate_h, gate), (gout_h, gout))
    loads = [
        pltpu.make_async_copy(src.at[0, :, :, mine], dst.at[my_rows], l_sem.at[n])
        for n, (src, dst) in enumerate(arrays)
    ]
    loads.append(pltpu.make_async_copy(rf_h.at[c], rf, l_sem.at[3]))
    loads.append(pltpu.make_async_copy(lf_h.at[c], lf, l_sem.at[4]))
    for n in (0, 3, 1, 2, 4):
        loads[n].start()

    barrier = pltpu.get_barrier_semaphore()

    def greet(ii):
        pl.semaphore_signal(barrier, inc=1, device_id={"inner": ii}, device_id_type=MESH)

    pl.semaphore_signal(barrier, inc=1, device_id={"outer": 1 - c}, device_id_type=MESH)
    for e in range(4):
        each_partner(e, greet)
    for k in range(ZH):
        pl.semaphore_signal(
            barrier, inc=1, device_id={"inner": j * ZH + (zh + k) % ZH, "dp": 1 - d}, device_id_type=MESH
        )

    def right_mix(h):
        def step(m, _):
            lhs = rf[pl.ds(pl.multiple_of(m * 128, 128), 128), :]
            parts = [dot(lhs, x[h * ROWS + p], 1, 0).reshape(16, QB, CG) for p in range(ROWS)]
            half = pl.ds(pl.multiple_of(h * 16, 16), 16)
            s1[pl.ds(m * 16, 16), half, :] = jnp.concatenate(parts, axis=1).astype(BF16)
            return 0

        lax.fori_loop(0, 4, step, 0)

    loads[0].wait()
    loads[3].wait()
    right_mix(c)

    pl.semaphore_wait(barrier, INNER + ZH)
    gifts = [
        pltpu.make_async_remote_copy(
            src_ref=src.at[0, :, :, theirs], dst_ref=dst.at[my_rows], send_sem=e_send.at[n], recv_sem=e_recv.at[n],
            device_id={"outer": 1 - c}, device_id_type=MESH,
        )
        for n, (src, dst) in enumerate(arrays)
    ]
    for gift in gifts:
        gift.start()

    def weigh(e):
        for t in range(4):
            jj = place(e, t, 1)
            rows = pl.ds(pl.multiple_of(jj * 32, 32), 32)
            parts = []
            for p in range(CHIP):
                a = gout[p, rows, :].astype(F32)
                b = gate[p, rows, :].astype(F32)
                parts.append((a * b).reshape(4, QB, CG))
            s2[pl.ds(jj * 4, 4)] = jnp.concatenate(parts, axis=1).astype(BF16)

    def send(src, dst, n, sem, e):
        def act(ii):
            pltpu.make_async_remote_copy(
                src_ref=src.at[ii], dst_ref=dst.at[i], send_sem=a_send.at[n], recv_sem=a_recv.at[sem],
                device_id={"inner": ii}, device_id_type=MESH,
            ).start()

        each_partner(e, act)

    def send_chunk(src, dst, n, e):
        send(src, dst, n, 4 * n - 3 + e, e)

    def wait_chunk(n, e):
        wait_bytes(t1.at[pl.ds(0, 15 if e == 0 else 16)], a_recv.at[4 * n - 3 + e])

    gifts[0].wait_recv()
    right_mix(1 - c)
    for e in range(4):
        send(s1, r1, 0, 0, e)
    loads[1].wait()
    loads[2].wait()
    gifts[1].wait_recv()
    gifts[2].wait_recv()
    for e in range(4):
        weigh(e)
        send_chunk(s2, r2, 1, e)
    r1[i] = s1[i]
    r2[i] = s2[i]
    loads[4].wait()
    lt[...] = lf[...].astype(F32).T.astype(BF16)
    for h in range(2):
        rt[:, h * 256:(h + 1) * 256] = rf[h * 256:(h + 1) * 256, :].astype(F32).T.astype(BF16)

    def column(q):
        return jnp.concatenate([wide_a[n, pl.ds(q, P_ALL, stride=QB), :] for n in range(LANES)], axis=1)

    wait_bytes(t1.at[pl.ds(0, INNER - 1)], a_recv.at[0])

    def widen(m, _):
        v = r1[pl.ds(m * 4, 4)].reshape(128, CG).astype(F32)
        for n in range(LANES):
            wide_a[n, pl.ds(pl.multiple_of(m * 128, 128), 128), :] = v[:, n * 128:(n + 1) * 128]
        return 0

    lax.fori_loop(0, XY, widen, 0)
    for q in range(QB):
        xq = column(q).astype(BF16)
        colsb[q] = xq
        mixed = dot(lf[...], xq, 1, 0)
        for n in range(LANES):
            wide_b[n, pl.ds(q, P_ALL, stride=QB), :] = mixed[:, n * 128:(n + 1) * 128]

    def narrow(m, _):
        for n in range(LANES):
            v = wide_b[n, pl.ds(pl.multiple_of(m * 64, 64), 64), :].astype(BF16)
            t1[pl.ds(m * 2, 2), :, n * 128:(n + 1) * 128] = v.reshape(2, BLK, 128)
        return 0

    lax.fori_loop(0, 32, narrow, 0)
    b1[i] = t1[i]
    for e in range(FIRST):
        send_chunk(t1, b1, 2, e)

    def slopes(m, _):
        rows = pl.ds(pl.multiple_of(m * 64, 64), 64)
        for n in range(LANES):
            wide_b[n, rows, :] = gelu_slope(wide_b[n, rows, :])
        return 0

    lax.fori_loop(0, 32, slopes, 0)

    for e in range(4):
        wait_chunk(1, e)
        for t in range(4):
            jj = place(e, t, -1)
            rows = pl.ds(pl.multiple_of(jj * 128, 128), 128)
            v = r2[pl.ds(jj * 4, 4)].reshape(128, CG).astype(F32)
            for n in range(LANES):
                wide_a[n, rows, :] = v[:, n * 128:(n + 1) * 128] * wide_b[n, rows, :]
    for q in range(QB):
        gmb[q] = column(q).astype(BF16)

    for e in range(4):
        spots = [place(e, t, 1) for t in range(4)]
        lhs = jnp.concatenate([lt[pl.ds(pl.multiple_of(jj * 16, 16), 16), :] for jj in spots], axis=0)
        for q in range(QB):
            v = dot(lhs, gmb[q], 1, 0)
            for t, jj in enumerate(spots):
                for n in range(LANES):
                    wide_c[n, pl.ds(jj * 128 + q, 16, stride=QB), :] = v[t * 16:(t + 1) * 16, n * 128:(n + 1) * 128]
        for jj in spots:
            rows = pl.ds(pl.multiple_of(jj * 128, 128), 128)
            for n in range(LANES):
                v = wide_c[n, rows, :].astype(BF16)
                t2[pl.ds(jj * 4, 4), :, n * 128:(n + 1) * 128] = v.reshape(4, BLK, 128)
        send_chunk(t2, b2, 3, e)
    b2[i] = t2[i]
    for e in range(FIRST, SECOND):
        send_chunk(t1, b1, 2, e)
    gl_acc = jnp.zeros((P_ALL, P_ALL), F32)
    for q in range(QB):
        gl_acc = gl_acc + dot(gmb[q], colsb[q], 1, 1)
    ls_s[...] = gl_acc.astype(BF16).reshape(XY, 16, P_ALL)

    def scatter(src, dst, n, e):
        for t in range(1 if e == 0 else 0, 4):
            jj = place(e, t, -1)
            pltpu.make_async_remote_copy(
                src_ref=src.at[jj], dst_ref=dst.at[j], send_sem=m_send.at[n], recv_sem=m_recv.at[n],
                device_id={"inner": jj * ZH + zh}, device_id_type=MESH,
            ).start()

    for e in range(4):
        scatter(ls_s, ls_r, 0, e)
    ls_r[j] = ls_s[j]

    def hand_out(src, dst, rows, n):
        pltpu.make_async_copy(src.at[my_rows, rows], dst.at[0, :, rows, mine], l_sem.at[n]).start()
        pltpu.make_async_remote_copy(
            src_ref=src.at[their_rows, rows], dst_ref=dst.at[0, :, rows, mine],
            send_sem=e_send.at[n], recv_sem=e_recv.at[n],
            device_id={"outer": 1 - c}, device_id_type=MESH,
        ).start()

    def gate_grad(e):
        wait_chunk(2, e)

        def step(t, _):
            jj = source(e, t)
            rows = pl.ds(pl.multiple_of(jj * 32, 32), 32)
            v = b1[pl.ds(jj * 4, 4)].astype(F32)
            for p in range(CHIP):
                act = gelu_value(v[:, p * QB:(p + 1) * QB, :].reshape(32, CG))
                ggate_v[p, rows, :] = (gout[p, rows, :].astype(F32) * act).astype(BF16)
            hand_out(ggate_v, ggate_o, rows, 6)
            return 0

        lax.fori_loop(0, 4, step, 0)

    for e in range(FIRST):
        gate_grad(e)

    for e in range(4):
        wait_chunk(3, e)
        spots = [place(e, t, -1) for t in range(4)]
        parts = [[] for _ in range(CHIP)]
        for jj in spots:
            rows = pl.ds(pl.multiple_of(jj * 32, 32), 32)
            v = b2[pl.ds(jj * 4, 4)].astype(F32)
            for p in range(CHIP):
                part = v[:, p * QB:(p + 1) * QB, :].reshape(32, CG).astype(BF16)
                gcb[p, rows, :] = part
                parts[p].append(part)
        total = None
        for p in range(CHIP):
            term = dot(jnp.concatenate(parts[p], axis=0), x[p], 1, 1)
            total = term if total is None else total + term
        for t, jj in enumerate(spots):
            rs_s[jj] = total[t * 32:(t + 1) * 32, :].astype(BF16)
        scatter(rs_s, rs_r, 1, e)
    rs_r[j] = rs_s[j]
    for e in range(SECOND, THIRD):
        send_chunk(t1, b1, 2, e)

    def input_grad(m, _):
        rows = pl.ds(pl.multiple_of(m * 128, 128), 128)
        for p in range(CHIP):
            gin_v[p, rows, :] = dot(rt[rows, :], gcb[p], 1, 0).astype(BF16)
        hand_out(gin_v, gin_o, rows, 5)
        return 0

    lax.fori_loop(0, 4, input_grad, 0)

    wait_bytes(ls_r.at[pl.ds(0, XY - 1)], m_recv.at[0])
    wait_bytes(rs_r.at[pl.ds(0, XY - 1)], m_recv.at[1])
    gr_sum = rs_r[0].astype(F32)
    gl_sum = ls_r[0].astype(F32)
    for k in range(1, XY):
        gr_sum = gr_sum + rs_r[k].astype(F32)
        gl_sum = gl_sum + ls_r[k].astype(F32)
    share[0:32, :] = gr_sum[:, 0:256].astype(BF16)
    share[32:64, :] = gr_sum[:, 256:512].astype(BF16)
    share[64:80, :] = gl_sum.astype(BF16)

    def to_z(k):
        return pltpu.make_async_remote_copy(
            src_ref=share, dst_ref=zrecv.at[zh * 2 + d], send_sem=m_send.at[2], recv_sem=m_recv.at[2],
            device_id={"inner": j * ZH + (zh + k) % ZH, "dp": c}, device_id_type=MESH,
        )

    for k in range(1, ZH):
        to_z(k).start()

    @pl.when(d != c)
    def _():
        to_z(0).start()

    for e in range(THIRD, 4):
        send_chunk(t1, b1, 2, e)
    for e in range(FIRST, SECOND):
        gate_grad(e)

    @pl.when(d == c)
    def _():
        zrecv[zh * 2 + d] = share[...]
        wait_bytes(zrecv.at[pl.ds(0, 7)], m_recv.at[2])
        total = zrecv[0].astype(F32)
        for k in range(1, 8):
            total = total + zrecv[k].astype(F32)
        fin[j] = total.astype(BF16)

        def give(k, _):
            jj = (j + k) % XY
            pltpu.make_async_remote_copy(
                src_ref=fin.at[j], dst_ref=fin.at[j], send_sem=m_send.at[3], recv_sem=m_recv.at[3],
                device_id={"inner": jj * ZH + zh}, device_id_type=MESH,
            ).start()
            return 0

        lax.fori_loop(1, XY, give, 0)

    for e in range(SECOND, 4):
        gate_grad(e)

    @pl.when(d == c)
    def _():
        wait_bytes(fin.at[pl.ds(0, XY - 1)], m_recv.at[3])
        pltpu.make_async_remote_copy(
            src_ref=fin, dst_ref=fin, send_sem=m_send.at[4], recv_sem=m_recv.at[4],
            device_id={"outer": 1 - c}, device_id_type=MESH,
        ).start()
        wait_bytes(fin.at[pl.ds(0, XY - 1)], m_send.at[3])
        wait_bytes(zrecv.at[pl.ds(0, 3)], m_send.at[2])
        wait_bytes(fin, m_send.at[4])

    @pl.when(d != c)
    def _():
        wait_bytes(zrecv.at[pl.ds(0, 4)], m_send.at[2])
        wait_bytes(fin, m_recv.at[4])

    for k in range(XY):
        gr_v[k * 32:(k + 1) * 32, 0:256] = fin[k, 0:32, :].astype(F32)
        gr_v[k * 32:(k + 1) * 32, 256:512] = fin[k, 32:64, :].astype(F32)
        gl_v[k * 16:(k + 1) * 16, :] = fin[k, 64:80, :].astype(F32)

    outs = (
        pltpu.make_async_copy(gr_v, gr_o.at[0], l_sem.at[7]),
        pltpu.make_async_copy(gl_v, gl_o.at[0], l_sem.at[8]),
    )
    for out in outs:
        out.start()
    for n in range(4):
        wait_bytes(t1.at[pl.ds(0, INNER - 1)], a_send.at[n])
    wait_bytes(ls_r.at[pl.ds(0, XY - 1)], m_send.at[0])
    wait_bytes(rs_r.at[pl.ds(0, XY - 1)], m_send.at[1])
    for gift in gifts:
        gift.wait_send()
    half = ggate_v.at[pl.ds(0, ROWS)]
    for n in (5, 6):
        wait_bytes(half, l_sem.at[n])
        wait_bytes(half, e_send.at[n])
        wait_bytes(half, e_recv.at[n])
    for out in outs:
        out.wait()


def body(inputs, gate_in, grad_out, right_factor, left_factor):
    hbm = pl.BlockSpec(memory_space=pl.ANY)
    out_shape = (
        jax.ShapeDtypeStruct((1, ROWS, Q, 2 * CG), BF16),
        jax.ShapeDtypeStruct((1, ROWS, Q, 2 * CG), BF16),
        jax.ShapeDtypeStruct((1, Q, Q), F32),
        jax.ShapeDtypeStruct((1, P_ALL, P_ALL), F32),
    )
    blocks = pltpu.VMEM((INNER, BLK, CG), BF16)
    rows = pltpu.VMEM((CHIP, Q, CG), BF16)
    wide = pltpu.VMEM((LANES, INNER * BLK, 128), F32)
    columns = pltpu.VMEM((QB, P_ALL, CG), BF16)
    scratch = [blocks] * 8 + [
        rows, rows, rows,
        pltpu.VMEM((Q, Q), BF16),
        pltpu.VMEM((P_ALL, P_ALL), BF16),
        rows, rows,
        pltpu.VMEM((Q, Q), F32),
        pltpu.VMEM((P_ALL, P_ALL), F32),
        wide, wide, wide,
        columns, columns,
        rows,
        pltpu.VMEM((Q, Q), BF16),
        pltpu.VMEM((P_ALL, P_ALL), BF16),
        pltpu.VMEM((XY, 32, Q), BF16),
        pltpu.VMEM((XY, 32, Q), BF16),
        pltpu.VMEM((XY, 16, P_ALL), BF16),
        pltpu.VMEM((XY, 16, P_ALL), BF16),
        pltpu.VMEM((80, 256), BF16),
        pltpu.VMEM((8, 80, 256), BF16),
        pltpu.VMEM((XY, 80, 256), BF16),
        pltpu.SemaphoreType.DMA((4,)),
        pltpu.SemaphoreType.DMA((13,)),
        pltpu.SemaphoreType.DMA((5,)),
        pltpu.SemaphoreType.DMA((5,)),
        pltpu.SemaphoreType.DMA((7,)),
        pltpu.SemaphoreType.DMA((7,)),
        pltpu.SemaphoreType.DMA((9,)),
    ]
    return pl.pallas_call(
        kernel,
        out_shape=out_shape,
        in_specs=[hbm] * 5,
        out_specs=(hbm,) * 4,
        scratch_shapes=scratch,
        compiler_params=pltpu.CompilerParams(
            collective_id=0, has_side_effects=True, vmem_limit_bytes=48 * 1024 * 1024
        ),
        cost_estimate=pl.CostEstimate(flops=4 * 10**9, bytes_accessed=12 * 10**6, transcendentals=3 * 10**6),
    )(inputs, gate_in, grad_out, right_factor, left_factor)


def solution(mesh):
    rows = P("dp", ("inner", "outer"), None, None)
    return jax.shard_map(
        body,
        mesh=mesh,
        in_specs=(rows, rows, rows, P(), P()),
        out_specs=(rows, rows, P("dp", None, None), P("dp", None, None)),
        check_vma=False,
    )
```

```python
import jax
import jax.numpy as jnp
from jax import lax
from jax.experimental import pallas as pl
from jax.experimental.pallas import tpu as pltpu
from jax.sharding import PartitionSpec as P

MESH = pl.DeviceIdType.MESH
F32 = jnp.float32
BF16 = jnp.bfloat16

INNER = 64
ZH = 4
XY = 16
ROWS = 2
CHIP = 4
CG = 384
LANES = CG // 128
Q = 512
P_ALL = 256
QB = 8
BLK = CHIP * QB

BEFORE_COLS = (0, 1)
AFTER_COLS = (2,)
AFTER_PLANE = (3,)
AFTER_Z = (4, 5)
AFTER_SHARES = (6, 7)


def gelu_value(mixed):
    return mixed * (0.5 * (1.0 + lax.erf(mixed * 0.7071067811865476)))


def gelu_slope(mixed):
    normal_cdf = 0.5 * (1.0 + lax.erf(mixed * 0.7071067811865476))
    density = jnp.exp(-0.5 * mixed * mixed) * 0.3989422804014327
    return normal_cdf + mixed * density


def wait_bytes(ref, sem):
    pltpu.make_async_copy(ref, ref, sem).wait()


def dot(a, b, ca, cb):
    return lax.dot_general(a, b, (((ca,), (cb,)), ((), ())), preferred_element_type=F32)


def kernel(
    x_h, gate_h, gout_h, rf_h, lf_h,
    gin_o, ggate_o, gr_o, gl_o,
    s1, s2, r1, r2, t1, t2, b1, b2,
    x, gate, gout, rf, lf, gin_v, ggate_v,
    wide_a, wide_b, wide_c, colsb, gmb, gcb, rt, lt,
    rs_s, rs_r, ls_s, ls_r, share, zrecv, fin,
    a_send, a_recv, m_send, m_recv, e_send, e_recv, l_sem,
):
    i = lax.axis_index("inner")
    c = lax.axis_index("outer")
    d = lax.axis_index("dp")
    zh = i % ZH
    j = i // ZH
    ys = [(j // 4 + n) % 4 for n in range(4)]
    xs = [(j % 4 + n) % 4 for n in range(4)]
    mine = pl.ds(pl.multiple_of(c * CG, CG), CG)
    theirs = pl.ds(pl.multiple_of((1 - c) * CG, CG), CG)
    my_rows = pl.ds(c * ROWS, ROWS)
    their_rows = pl.ds((1 - c) * ROWS, ROWS)

    def place(e, t, sign):
        return ys[sign * (e + t) % 4] * 4 + xs[sign * t % 4]

    def source(e, t):
        return lax.rem(ys[0] + 8 - e - t, 4) * 4 + lax.rem(xs[0] + 4 - t, 4)

    def each_partner(e, act, first=0, last=ZH):
        if e == 0 and first == 0:
            for t in range(1, 4):
                act(place(e, t, 1) * ZH + (zh + t) % ZH)
            first = 1

        def step(u, _):
            for t in range(4):
                act(place(e, t, 1) * ZH + lax.rem(zh + t + u, ZH))
            return 0

        lax.fori_loop(first, last, step, 0)

    arrays = ((x_h, x), (gate_h, gate), (gout_h, gout))
    loads = [
        pltpu.make_async_copy(src.at[0, :, :, mine], dst.at[my_rows], l_sem.at[n])
        for n, (src, dst) in enumerate(arrays)
    ]
    loads.append(pltpu.make_async_copy(rf_h.at[c], rf, l_sem.at[3]))
    loads.append(pltpu.make_async_copy(lf_h.at[c], lf, l_sem.at[4]))
    for n in (0, 3, 1, 2, 4):
        loads[n].start()

    barrier = pltpu.get_barrier_semaphore()

    def greet(ii):
        pl.semaphore_signal(barrier, inc=1, device_id={"inner": ii}, device_id_type=MESH)

    pl.semaphore_signal(barrier, inc=1, device_id={"outer": 1 - c}, device_id_type=MESH)
    for e in range(4):
        each_partner(e, greet)
    for k in range(ZH):
        pl.semaphore_signal(
            barrier, inc=1, device_id={"inner": j * ZH + (zh + k) % ZH, "dp": 1 - d}, device_id_type=MESH
        )

    def right_mix(h):
        def step(m, _):
            lhs = rf[pl.ds(pl.multiple_of(m * 128, 128), 128), :]
            parts = [dot(lhs, x[h * ROWS + p], 1, 0).reshape(16, QB, CG) for p in range(ROWS)]
            half = pl.ds(pl.multiple_of(h * 16, 16), 16)
            s1[pl.ds(m * 16, 16), half, :] = jnp.concatenate(parts, axis=1).astype(BF16)
            return 0

        lax.fori_loop(0, 4, step, 0)

    loads[0].wait()
    loads[3].wait()
    right_mix(c)

    pl.semaphore_wait(barrier, INNER + ZH)
    gifts = [
        pltpu.make_async_remote_copy(
            src_ref=src.at[0, :, :, theirs], dst_ref=dst.at[my_rows], send_sem=e_send.at[n], recv_sem=e_recv.at[n],
            device_id={"outer": 1 - c}, device_id_type=MESH,
        )
        for n, (src, dst) in enumerate(arrays)
    ]
    gifts[0].start()

    def weigh(e):
        for t in range(4):
            jj = place(e, t, 1)
            rows = pl.ds(pl.multiple_of(jj * 32, 32), 32)
            parts = []
            for p in range(CHIP):
                a = gout[p, rows, :].astype(F32)
                b = gate[p, rows, :].astype(F32)
                parts.append((a * b).reshape(4, QB, CG))
            s2[pl.ds(jj * 4, 4)] = jnp.concatenate(parts, axis=1).astype(BF16)

    def send(src, dst, n, sem, e, first=0, last=ZH):
        def act(ii):
            pltpu.make_async_remote_copy(
                src_ref=src.at[ii], dst_ref=dst.at[i], send_sem=a_send.at[n], recv_sem=a_recv.at[sem],
                device_id={"inner": ii}, device_id_type=MESH,
            ).start()

        each_partner(e, act, first, last)

    def send_chunk(src, dst, n, e):
        send(src, dst, n, 4 * n - 3 + e, e)

    def send_mixed(*pieces):
        for k in pieces:
            send(t1, b1, 2, 5 + k // 2, k // 2, k % 2 * 2, k % 2 * 2 + 2)

    def wait_chunk(n, e):
        wait_bytes(t1.at[pl.ds(0, 15 if e == 0 else 16)], a_recv.at[4 * n - 3 + e])

    gifts[0].wait_recv()
    gifts[1].start()
    gifts[2].start()
    right_mix(1 - c)
    for e in range(4):
        send(s1, r1, 0, 0, e)
    loads[1].wait()
    loads[2].wait()
    gifts[1].wait_recv()
    gifts[2].wait_recv()
    for e in range(4):
        weigh(e)
        send_chunk(s2, r2, 1, e)
    r1[i] = s1[i]
    r2[i] = s2[i]
    loads[4].wait()
    lt[...] = lf[...].astype(F32).T.astype(BF16)
    for h in range(2):
        rt[:, h * 256:(h + 1) * 256] = rf[h * 256:(h + 1) * 256, :].astype(F32).T.astype(BF16)

    def column(q):
        return jnp.concatenate([wide_a[n, pl.ds(q, P_ALL, stride=QB), :] for n in range(LANES)], axis=1)

    wait_bytes(t1.at[pl.ds(0, INNER - 1)], a_recv.at[0])

    def widen(m, _):
        v = r1[pl.ds(m * 4, 4)].reshape(128, CG).astype(F32)
        for n in range(LANES):
            wide_a[n, pl.ds(pl.multiple_of(m * 128, 128), 128), :] = v[:, n * 128:(n + 1) * 128]
        return 0

    lax.fori_loop(0, XY, widen, 0)
    for q in range(QB):
        xq = column(q).astype(BF16)
        colsb[q] = xq
        mixed = dot(lf[...], xq, 1, 0)
        for n in range(LANES):
            wide_b[n, pl.ds(q, P_ALL, stride=QB), :] = mixed[:, n * 128:(n + 1) * 128]

    def narrow(m, _):
        for n in range(LANES):
            v = wide_b[n, pl.ds(pl.multiple_of(m * 64, 64), 64), :].astype(BF16)
            t1[pl.ds(m * 2, 2), :, n * 128:(n + 1) * 128] = v.reshape(2, BLK, 128)
        return 0

    lax.fori_loop(0, 32, narrow, 0)
    b1[i] = t1[i]
    send_mixed(*BEFORE_COLS)

    def slopes(m, _):
        rows = pl.ds(pl.multiple_of(m * 64, 64), 64)
        for n in range(LANES):
            wide_b[n, rows, :] = gelu_slope(wide_b[n, rows, :])
        return 0

    lax.fori_loop(0, 32, slopes, 0)

    for e in range(4):
        wait_chunk(1, e)
        for t in range(4):
            jj = place(e, t, -1)
            rows = pl.ds(pl.multiple_of(jj * 128, 128), 128)
            v = r2[pl.ds(jj * 4, 4)].reshape(128, CG).astype(F32)
            for n in range(LANES):
                wide_a[n, rows, :] = v[:, n * 128:(n + 1) * 128] * wide_b[n, rows, :]
    for q in range(QB):
        gmb[q] = column(q).astype(BF16)

    for e in range(4):
        spots = [place(e, t, 1) for t in range(4)]
        lhs = jnp.concatenate([lt[pl.ds(pl.multiple_of(jj * 16, 16), 16), :] for jj in spots], axis=0)
        for q in range(QB):
            v = dot(lhs, gmb[q], 1, 0)
            for t, jj in enumerate(spots):
                for n in range(LANES):
                    wide_c[n, pl.ds(jj * 128 + q, 16, stride=QB), :] = v[t * 16:(t + 1) * 16, n * 128:(n + 1) * 128]
        for jj in spots:
            rows = pl.ds(pl.multiple_of(jj * 128, 128), 128)
            for n in range(LANES):
                v = wide_c[n, rows, :].astype(BF16)
                t2[pl.ds(jj * 4, 4), :, n * 128:(n + 1) * 128] = v.reshape(4, BLK, 128)
        send_chunk(t2, b2, 3, e)
    b2[i] = t2[i]
    send_mixed(*AFTER_COLS)
    gl_acc = jnp.zeros((P_ALL, P_ALL), F32)
    for q in range(QB):
        gl_acc = gl_acc + dot(gmb[q], colsb[q], 1, 1)
    ls_s[...] = gl_acc.astype(BF16).reshape(XY, 16, P_ALL)

    def scatter(src, dst, n, e):
        for t in range(1 if e == 0 else 0, 4):
            jj = place(e, t, -1)
            pltpu.make_async_remote_copy(
                src_ref=src.at[jj], dst_ref=dst.at[j], send_sem=m_send.at[n], recv_sem=m_recv.at[n],
                device_id={"inner": jj * ZH + zh}, device_id_type=MESH,
            ).start()

    for e in range(4):
        scatter(ls_s, ls_r, 0, e)
    ls_r[j] = ls_s[j]

    def hand_out(src, dst, rows, n):
        pltpu.make_async_copy(src.at[my_rows, rows], dst.at[0, :, rows, mine], l_sem.at[n]).start()
        pltpu.make_async_remote_copy(
            src_ref=src.at[their_rows, rows], dst_ref=dst.at[0, :, rows, mine],
            send_sem=e_send.at[n], recv_sem=e_recv.at[n],
            device_id={"outer": 1 - c}, device_id_type=MESH,
        ).start()

    def gate_grad(e):
        wait_chunk(2, e)

        def step(t, _):
            jj = source(e, t)
            rows = pl.ds(pl.multiple_of(jj * 32, 32), 32)
            v = b1[pl.ds(jj * 4, 4)].astype(F32)
            for p in range(CHIP):
                act = gelu_value(v[:, p * QB:(p + 1) * QB, :].reshape(32, CG))
                ggate_v[p, rows, :] = (gout[p, rows, :].astype(F32) * act).astype(BF16)
            hand_out(ggate_v, ggate_o, rows, 6)
            return 0

        lax.fori_loop(0, 4, step, 0)

    gate_grad(0)

    for e in range(4):
        wait_chunk(3, e)
        spots = [place(e, t, -1) for t in range(4)]
        parts = [[] for _ in range(CHIP)]
        for jj in spots:
            rows = pl.ds(pl.multiple_of(jj * 32, 32), 32)
            v = b2[pl.ds(jj * 4, 4)].astype(F32)
            for p in range(CHIP):
                part = v[:, p * QB:(p + 1) * QB, :].reshape(32, CG).astype(BF16)
                gcb[p, rows, :] = part
                parts[p].append(part)
        total = None
        for p in range(CHIP):
            term = dot(jnp.concatenate(parts[p], axis=0), x[p], 1, 1)
            total = term if total is None else total + term
        for t, jj in enumerate(spots):
            rs_s[jj] = total[t * 32:(t + 1) * 32, :].astype(BF16)
        scatter(rs_s, rs_r, 1, e)
    rs_r[j] = rs_s[j]
    send_mixed(*AFTER_PLANE)

    def input_grad(m, _):
        rows = pl.ds(pl.multiple_of(m * 128, 128), 128)
        for p in range(CHIP):
            gin_v[p, rows, :] = dot(rt[rows, :], gcb[p], 1, 0).astype(BF16)
        hand_out(gin_v, gin_o, rows, 5)
        return 0

    lax.fori_loop(0, 4, input_grad, 0)

    wait_bytes(ls_r.at[pl.ds(0, XY - 1)], m_recv.at[0])
    wait_bytes(rs_r.at[pl.ds(0, XY - 1)], m_recv.at[1])
    gr_sum = rs_r[0].astype(F32)
    gl_sum = ls_r[0].astype(F32)
    for k in range(1, XY):
        gr_sum = gr_sum + rs_r[k].astype(F32)
        gl_sum = gl_sum + ls_r[k].astype(F32)
    share[0:32, :] = gr_sum[:, 0:256].astype(BF16)
    share[32:64, :] = gr_sum[:, 256:512].astype(BF16)
    share[64:80, :] = gl_sum.astype(BF16)

    def to_z(k):
        return pltpu.make_async_remote_copy(
            src_ref=share, dst_ref=zrecv.at[zh * 2 + d], send_sem=m_send.at[2], recv_sem=m_recv.at[2],
            device_id={"inner": j * ZH + (zh + k) % ZH, "dp": c}, device_id_type=MESH,
        )

    for k in range(1, ZH):
        to_z(k).start()

    @pl.when(d != c)
    def _():
        to_z(0).start()

    send_mixed(*AFTER_Z)
    gate_grad(1)

    @pl.when(d == c)
    def _():
        zrecv[zh * 2 + d] = share[...]
        wait_bytes(zrecv.at[pl.ds(0, 7)], m_recv.at[2])
        total = zrecv[0].astype(F32)
        for k in range(1, 8):
            total = total + zrecv[k].astype(F32)
        fin[j] = total.astype(BF16)

        def give(k, _):
            jj = (j + k) % XY
            pltpu.make_async_remote_copy(
                src_ref=fin.at[j], dst_ref=fin.at[j], send_sem=m_send.at[3], recv_sem=m_recv.at[3],
                device_id={"inner": jj * ZH + zh}, device_id_type=MESH,
            ).start()
            return 0

        lax.fori_loop(1, XY, give, 0)

    send_mixed(*AFTER_SHARES)
    gate_grad(2)

    @pl.when(d == c)
    def _():
        wait_bytes(fin.at[pl.ds(0, XY - 1)], m_recv.at[3])
        pltpu.make_async_remote_copy(
            src_ref=fin, dst_ref=fin, send_sem=m_send.at[4], recv_sem=m_recv.at[4],
            device_id={"outer": 1 - c}, device_id_type=MESH,
        ).start()
        wait_bytes(fin.at[pl.ds(0, XY - 1)], m_send.at[3])
        wait_bytes(zrecv.at[pl.ds(0, 3)], m_send.at[2])
        wait_bytes(fin, m_send.at[4])

    @pl.when(d != c)
    def _():
        wait_bytes(zrecv.at[pl.ds(0, 4)], m_send.at[2])
        wait_bytes(fin, m_recv.at[4])

    for k in range(XY):
        gr_o[0, k * 32:(k + 1) * 32, 0:256] = fin[k, 0:32, :].astype(F32)
        gr_o[0, k * 32:(k + 1) * 32, 256:512] = fin[k, 32:64, :].astype(F32)
        gl_o[0, k * 16:(k + 1) * 16, :] = fin[k, 64:80, :].astype(F32)
    gate_grad(3)

    for n in range(4):
        wait_bytes(t1.at[pl.ds(0, INNER - 1)], a_send.at[n])
    wait_bytes(ls_r.at[pl.ds(0, XY - 1)], m_send.at[0])
    wait_bytes(rs_r.at[pl.ds(0, XY - 1)], m_send.at[1])
    for gift in gifts:
        gift.wait_send()
    half = ggate_v.at[pl.ds(0, ROWS)]
    for n in (5, 6):
        wait_bytes(half, l_sem.at[n])
        wait_bytes(half, e_send.at[n])
        wait_bytes(half, e_recv.at[n])


def body(*operands):
    hbm = pl.BlockSpec(memory_space=pl.ANY)
    out_shape = (
        pltpu.VMEM((1, ROWS, Q, 2 * CG), BF16),
        pltpu.VMEM((1, ROWS, Q, 2 * CG), BF16),
        pltpu.VMEM((1, Q, Q), F32),
        pltpu.VMEM((1, P_ALL, P_ALL), F32),
    )
    blocks = pltpu.VMEM((INNER, BLK, CG), BF16)
    rows = pltpu.VMEM((CHIP, Q, CG), BF16)
    wide = pltpu.VMEM((LANES, INNER * BLK, 128), F32)
    columns = pltpu.VMEM((QB, P_ALL, CG), BF16)
    scratch = [blocks] * 8 + [
        rows, rows, rows,
        pltpu.VMEM((Q, Q), BF16),
        pltpu.VMEM((P_ALL, P_ALL), BF16),
        rows, rows,
        wide, wide, wide,
        columns, columns,
        rows,
        pltpu.VMEM((Q, Q), BF16),
        pltpu.VMEM((P_ALL, P_ALL), BF16),
        pltpu.VMEM((XY, 32, Q), BF16),
        pltpu.VMEM((XY, 32, Q), BF16),
        pltpu.VMEM((XY, 16, P_ALL), BF16),
        pltpu.VMEM((XY, 16, P_ALL), BF16),
        pltpu.VMEM((80, 256), BF16),
        pltpu.VMEM((8, 80, 256), BF16),
        pltpu.VMEM((XY, 80, 256), BF16),
        pltpu.SemaphoreType.DMA((4,)),
        pltpu.SemaphoreType.DMA((13,)),
        pltpu.SemaphoreType.DMA((5,)),
        pltpu.SemaphoreType.DMA((5,)),
        pltpu.SemaphoreType.DMA((7,)),
        pltpu.SemaphoreType.DMA((7,)),
        pltpu.SemaphoreType.DMA((9,)),
    ]
    return pl.pallas_call(
        kernel,
        out_shape=out_shape,
        in_specs=[hbm] * 5,
        out_specs=(pl.BlockSpec(memory_space=pltpu.VMEM),) * 4,
        scratch_shapes=scratch,
        compiler_params=pltpu.CompilerParams(
            collective_id=0, has_side_effects=True, vmem_limit_bytes=52 * 1024 * 1024
        ),
        cost_estimate=pl.CostEstimate(flops=4 * 10**9, bytes_accessed=12 * 10**6, transcendentals=3 * 10**6),
    )(*(pltpu.with_memory_space_constraint(a, pltpu.HBM) for a in operands))


def solution(mesh):
    rows = P("dp", ("inner", "outer"), None, None)
    return jax.shard_map(
        body,
        mesh=mesh,
        in_specs=(rows, rows, rows, P(), P()),
        out_specs=(rows, rows, P("dp", None, None), P("dp", None, None)),
        check_vma=False,
    )
```

```python
import jax
import jax.numpy as jnp
from jax import lax
from jax.experimental import pallas as pl
from jax.experimental.pallas import tpu as pltpu
from jax.sharding import PartitionSpec as P

MESH = pl.DeviceIdType.MESH
F32 = jnp.float32
BF16 = jnp.bfloat16

INNER = 64
ZH = 4
XY = 16
ROWS = 2
CHIP = 4
CG = 384
LANES = CG // 128
Q = 512
P_ALL = 256
QB = 8
BLK = CHIP * QB

BEFORE_COLS = (0, 1)
AFTER_COLS = (2, 3)
AFTER_PLANE = (4, 5)
AFTER_Z = (6,)
AFTER_SHARES = (7,)


def gelu_value(mixed):
    return mixed * (0.5 * (1.0 + lax.erf(mixed * 0.7071067811865476)))


def gelu_slope(mixed):
    normal_cdf = 0.5 * (1.0 + lax.erf(mixed * 0.7071067811865476))
    density = jnp.exp(-0.5 * mixed * mixed) * 0.3989422804014327
    return normal_cdf + mixed * density


def wait_bytes(ref, sem):
    pltpu.make_async_copy(ref, ref, sem).wait()


def dot(a, b, ca, cb):
    return lax.dot_general(a, b, (((ca,), (cb,)), ((), ())), preferred_element_type=F32)


def kernel(
    x_h, gate_h, gout_h, rf_h, lf_h,
    gin_o, ggate_o, gr_o, gl_o,
    s1, s2, r1, r2, t1, t2, b1, b2,
    x, gate, gout, rf, lf, gin_v, ggate_v,
    wide_a, wide_b, wide_c, colsb, gmb, gcb, rt, lt,
    rs_s, rs_r, ls_s, ls_r, share, zrecv, fin,
    a_send, a_recv, m_send, m_recv, e_send, e_recv, l_sem,
):
    i = lax.axis_index("inner")
    c = lax.axis_index("outer")
    d = lax.axis_index("dp")
    zh = i % ZH
    j = i // ZH
    ys = [(j // 4 + n) % 4 for n in range(4)]
    xs = [(j % 4 + n) % 4 for n in range(4)]
    mine = pl.ds(pl.multiple_of(c * CG, CG), CG)
    theirs = pl.ds(pl.multiple_of((1 - c) * CG, CG), CG)
    my_rows = pl.ds(c * ROWS, ROWS)
    their_rows = pl.ds((1 - c) * ROWS, ROWS)

    def place(e, t, sign):
        return ys[sign * (e + t) % 4] * 4 + xs[sign * t % 4]

    def source(e, t):
        return lax.rem(ys[0] + 8 - e - t, 4) * 4 + lax.rem(xs[0] + 4 - t, 4)

    def each_partner(e, act, first=0, last=ZH):
        if e == 0 and first == 0:
            for t in range(1, 4):
                act(place(e, t, 1) * ZH + (zh + t) % ZH)
            first = 1

        def step(u, _):
            for t in range(4):
                act(place(e, t, 1) * ZH + lax.rem(zh + t + u, ZH))
            return 0

        lax.fori_loop(first, last, step, 0)

    arrays = ((x_h, x), (gate_h, gate), (gout_h, gout))
    loads = [
        pltpu.make_async_copy(src.at[0, :, :, mine], dst.at[my_rows], l_sem.at[n])
        for n, (src, dst) in enumerate(arrays)
    ]
    loads.append(pltpu.make_async_copy(rf_h.at[c], rf, l_sem.at[3]))
    loads.append(pltpu.make_async_copy(lf_h.at[c], lf, l_sem.at[4]))
    for n in (0, 3, 1, 2, 4):
        loads[n].start()

    barrier = pltpu.get_barrier_semaphore()

    def greet(ii):
        pl.semaphore_signal(barrier, inc=1, device_id={"inner": ii}, device_id_type=MESH)

    pl.semaphore_signal(barrier, inc=1, device_id={"outer": 1 - c}, device_id_type=MESH)
    for e in range(4):
        each_partner(e, greet)
    for k in range(ZH):
        pl.semaphore_signal(
            barrier, inc=1, device_id={"inner": j * ZH + (zh + k) % ZH, "dp": 1 - d}, device_id_type=MESH
        )

    def right_mix(h):
        def step(m, _):
            lhs = rf[pl.ds(pl.multiple_of(m * 128, 128), 128), :]
            parts = [dot(lhs, x[h * ROWS + p], 1, 0).reshape(16, QB, CG) for p in range(ROWS)]
            half = pl.ds(pl.multiple_of(h * 16, 16), 16)
            s1[pl.ds(m * 16, 16), half, :] = jnp.concatenate(parts, axis=1).astype(BF16)
            return 0

        lax.fori_loop(0, 4, step, 0)

    loads[0].wait()
    loads[3].wait()
    right_mix(c)

    pl.semaphore_wait(barrier, INNER + ZH)
    gifts = [
        pltpu.make_async_remote_copy(
            src_ref=src.at[0, :, :, theirs], dst_ref=dst.at[my_rows], send_sem=e_send.at[n], recv_sem=e_recv.at[n],
            device_id={"outer": 1 - c}, device_id_type=MESH,
        )
        for n, (src, dst) in enumerate(arrays)
    ]
    gifts[0].start()

    def weigh(e):
        for t in range(4):
            jj = place(e, t, 1)
            rows = pl.ds(pl.multiple_of(jj * 32, 32), 32)
            parts = []
            for p in range(CHIP):
                a = gout[p, rows, :].astype(F32)
                b = gate[p, rows, :].astype(F32)
                parts.append((a * b).reshape(4, QB, CG))
            s2[pl.ds(jj * 4, 4)] = jnp.concatenate(parts, axis=1).astype(BF16)

    def send_to(src, dst, n, sem, ii):
        pltpu.make_async_remote_copy(
            src_ref=src.at[ii], dst_ref=dst.at[i], send_sem=a_send.at[n], recv_sem=a_recv.at[sem],
            device_id={"inner": ii}, device_id_type=MESH,
        ).start()

    def send_chunk(src, dst, n, e, first=0, last=ZH):
        each_partner(e, lambda ii: send_to(src, dst, n, 4 * n - 3 + e, ii), first, last)

    def send_mixed(*pieces):
        for k in pieces:
            if k < 6:
                send_chunk(t1, b1, 2, k // 2, k % 2 * 2, k % 2 * 2 + 2)
            else:
                for t in (k % 2 * 2, k % 2 * 2 + 1):
                    def step(u, _):
                        send_to(t1, b1, 2, 13 + t, place(3, t, 1) * ZH + lax.rem(zh + t + u, ZH))
                        return 0

                    lax.fori_loop(0, ZH, step, 0)

    def wait_chunk(n, e):
        wait_bytes(t1.at[pl.ds(0, 15 if e == 0 else 16)], a_recv.at[4 * n - 3 + e])

    def send_half(h):
        half = pl.ds(pl.multiple_of(h * 16, 16), 16)

        def act(ii):
            pltpu.make_async_remote_copy(
                src_ref=s1.at[ii, half], dst_ref=r1.at[i, half], send_sem=a_send.at[0], recv_sem=a_recv.at[0],
                device_id={"inner": ii}, device_id_type=MESH,
            ).start()

        for e in range(4):
            each_partner(e, act)

    send_half(c)
    gifts[0].wait_recv()
    gifts[1].start()
    gifts[2].start()
    right_mix(1 - c)
    send_half(1 - c)
    loads[1].wait()
    loads[2].wait()
    gifts[1].wait_recv()
    gifts[2].wait_recv()
    for e in range(4):
        weigh(e)
        send_chunk(s2, r2, 1, e)
    r1[i] = s1[i]
    r2[i] = s2[i]
    loads[4].wait()
    lt[...] = lf[...].astype(F32).T.astype(BF16)
    for h in range(2):
        rt[:, h * 256:(h + 1) * 256] = rf[h * 256:(h + 1) * 256, :].astype(F32).T.astype(BF16)

    def column(q):
        return jnp.concatenate([wide_a[n, pl.ds(q, P_ALL, stride=QB), :] for n in range(LANES)], axis=1)

    wait_bytes(t1.at[pl.ds(0, INNER - 1)], a_recv.at[0])

    def widen(m, _):
        v = r1[pl.ds(m * 4, 4)].reshape(128, CG).astype(F32)
        for n in range(LANES):
            wide_a[n, pl.ds(pl.multiple_of(m * 128, 128), 128), :] = v[:, n * 128:(n + 1) * 128]
        return 0

    lax.fori_loop(0, XY, widen, 0)
    for q in range(QB):
        xq = column(q).astype(BF16)
        colsb[q] = xq
        mixed = dot(lf[...], xq, 1, 0)
        for n in range(LANES):
            wide_b[n, pl.ds(q, P_ALL, stride=QB), :] = mixed[:, n * 128:(n + 1) * 128]

    def narrow(m, _):
        for n in range(LANES):
            v = wide_b[n, pl.ds(pl.multiple_of(m * 64, 64), 64), :].astype(BF16)
            t1[pl.ds(m * 2, 2), :, n * 128:(n + 1) * 128] = v.reshape(2, BLK, 128)
        return 0

    lax.fori_loop(0, 32, narrow, 0)
    b1[i] = t1[i]
    send_mixed(*BEFORE_COLS)

    def slopes(m, _):
        rows = pl.ds(pl.multiple_of(m * 64, 64), 64)
        for n in range(LANES):
            wide_b[n, rows, :] = gelu_slope(wide_b[n, rows, :])
        return 0

    lax.fori_loop(0, 32, slopes, 0)

    for e in range(4):
        wait_chunk(1, e)
        for t in range(4):
            jj = place(e, t, -1)
            rows = pl.ds(pl.multiple_of(jj * 128, 128), 128)
            v = r2[pl.ds(jj * 4, 4)].reshape(128, CG).astype(F32)
            for n in range(LANES):
                wide_a[n, rows, :] = v[:, n * 128:(n + 1) * 128] * wide_b[n, rows, :]
    for q in range(QB):
        gmb[q] = column(q).astype(BF16)

    for e in range(4):
        spots = [place(e, t, 1) for t in range(4)]
        lhs = jnp.concatenate([lt[pl.ds(pl.multiple_of(jj * 16, 16), 16), :] for jj in spots], axis=0)
        for q in range(QB):
            v = dot(lhs, gmb[q], 1, 0)
            for t, jj in enumerate(spots):
                for n in range(LANES):
                    wide_c[n, pl.ds(jj * 128 + q, 16, stride=QB), :] = v[t * 16:(t + 1) * 16, n * 128:(n + 1) * 128]
        for jj in spots:
            rows = pl.ds(pl.multiple_of(jj * 128, 128), 128)
            for n in range(LANES):
                v = wide_c[n, rows, :].astype(BF16)
                t2[pl.ds(jj * 4, 4), :, n * 128:(n + 1) * 128] = v.reshape(4, BLK, 128)
        send_chunk(t2, b2, 3, e)
    b2[i] = t2[i]
    send_mixed(*AFTER_COLS)
    gl_acc = jnp.zeros((P_ALL, P_ALL), F32)
    for q in range(QB):
        gl_acc = gl_acc + dot(gmb[q], colsb[q], 1, 1)
    ls_s[...] = gl_acc.astype(BF16).reshape(XY, 16, P_ALL)

    def scatter(src, dst, n, e):
        for t in range(1 if e == 0 else 0, 4):
            jj = place(e, t, -1)
            pltpu.make_async_remote_copy(
                src_ref=src.at[jj], dst_ref=dst.at[j], send_sem=m_send.at[n], recv_sem=m_recv.at[n],
                device_id={"inner": jj * ZH + zh}, device_id_type=MESH,
            ).start()

    for e in range(4):
        scatter(ls_s, ls_r, 0, e)
    ls_r[j] = ls_s[j]

    def hand_out(src, dst, rows, n):
        pltpu.make_async_copy(src.at[my_rows, rows], dst.at[0, :, rows, mine], l_sem.at[n]).start()
        pltpu.make_async_remote_copy(
            src_ref=src.at[their_rows, rows], dst_ref=dst.at[0, :, rows, mine],
            send_sem=e_send.at[n], recv_sem=e_recv.at[n],
            device_id={"outer": 1 - c}, device_id_type=MESH,
        ).start()

    def gate_chip(jj):
        rows = pl.ds(pl.multiple_of(jj * 32, 32), 32)
        v = b1[pl.ds(jj * 4, 4)].astype(F32)
        for p in range(CHIP):
            act = gelu_value(v[:, p * QB:(p + 1) * QB, :].reshape(32, CG))
            ggate_v[p, rows, :] = (gout[p, rows, :].astype(F32) * act).astype(BF16)
        hand_out(ggate_v, ggate_o, rows, 6)

    def gate_grad(e):
        wait_chunk(2, e)

        def step(t, _):
            gate_chip(source(e, t))
            return 0

        lax.fori_loop(0, 4, step, 0)

    gate_grad(0)

    for e in range(4):
        wait_chunk(3, e)
        spots = [place(e, t, -1) for t in range(4)]
        parts = [[] for _ in range(CHIP)]
        for jj in spots:
            rows = pl.ds(pl.multiple_of(jj * 32, 32), 32)
            v = b2[pl.ds(jj * 4, 4)].astype(F32)
            for p in range(CHIP):
                part = v[:, p * QB:(p + 1) * QB, :].reshape(32, CG).astype(BF16)
                gcb[p, rows, :] = part
                parts[p].append(part)
        total = None
        for p in range(CHIP):
            term = dot(jnp.concatenate(parts[p], axis=0), x[p], 1, 1)
            total = term if total is None else total + term
        for t, jj in enumerate(spots):
            rs_s[jj] = total[t * 32:(t + 1) * 32, :].astype(BF16)
        scatter(rs_s, rs_r, 1, e)
    rs_r[j] = rs_s[j]
    send_mixed(*AFTER_PLANE)

    def input_grad(m, _):
        rows = pl.ds(pl.multiple_of(m * 128, 128), 128)
        for p in range(CHIP):
            gin_v[p, rows, :] = dot(rt[rows, :], gcb[p], 1, 0).astype(BF16)
        hand_out(gin_v, gin_o, rows, 5)
        return 0

    lax.fori_loop(0, 4, input_grad, 0)

    wait_bytes(ls_r.at[pl.ds(0, XY - 1)], m_recv.at[0])
    wait_bytes(rs_r.at[pl.ds(0, XY - 1)], m_recv.at[1])
    gr_sum = rs_r[0].astype(F32)
    gl_sum = ls_r[0].astype(F32)
    for k in range(1, XY):
        gr_sum = gr_sum + rs_r[k].astype(F32)
        gl_sum = gl_sum + ls_r[k].astype(F32)
    share[0:32, :] = gr_sum[:, 0:256].astype(BF16)
    share[32:64, :] = gr_sum[:, 256:512].astype(BF16)
    share[64:80, :] = gl_sum.astype(BF16)

    def to_z(k):
        return pltpu.make_async_remote_copy(
            src_ref=share, dst_ref=zrecv.at[zh * 2 + d], send_sem=m_send.at[2], recv_sem=m_recv.at[2],
            device_id={"inner": j * ZH + (zh + k) % ZH, "dp": c}, device_id_type=MESH,
        )

    for k in range(1, ZH):
        to_z(k).start()

    @pl.when(d != c)
    def _():
        to_z(0).start()

    send_mixed(*AFTER_Z)
    gate_grad(1)

    @pl.when(d == c)
    def _():
        zrecv[zh * 2 + d] = share[...]
        wait_bytes(zrecv.at[pl.ds(0, 7)], m_recv.at[2])
        total = zrecv[0].astype(F32)
        for k in range(1, 8):
            total = total + zrecv[k].astype(F32)
        fin[j] = total.astype(BF16)

        def give(k, _):
            jj = (j + k) % XY
            pltpu.make_async_remote_copy(
                src_ref=fin.at[j], dst_ref=fin.at[j], send_sem=m_send.at[3], recv_sem=m_recv.at[3],
                device_id={"inner": jj * ZH + zh}, device_id_type=MESH,
            ).start()
            return 0

        lax.fori_loop(1, XY, give, 0)

    send_mixed(*AFTER_SHARES)
    gate_grad(2)

    @pl.when(d == c)
    def _():
        wait_bytes(fin.at[pl.ds(0, XY - 1)], m_recv.at[3])
        pltpu.make_async_remote_copy(
            src_ref=fin, dst_ref=fin, send_sem=m_send.at[4], recv_sem=m_recv.at[4],
            device_id={"outer": 1 - c}, device_id_type=MESH,
        ).start()
        wait_bytes(fin.at[pl.ds(0, XY - 1)], m_send.at[3])
        wait_bytes(zrecv.at[pl.ds(0, 3)], m_send.at[2])
        wait_bytes(fin, m_send.at[4])

    @pl.when(d != c)
    def _():
        wait_bytes(zrecv.at[pl.ds(0, 4)], m_send.at[2])
        wait_bytes(fin, m_recv.at[4])

    for k in range(XY):
        gr_o[0, k * 32:(k + 1) * 32, 0:256] = fin[k, 0:32, :].astype(F32)
        gr_o[0, k * 32:(k + 1) * 32, 256:512] = fin[k, 32:64, :].astype(F32)
        gl_o[0, k * 16:(k + 1) * 16, :] = fin[k, 64:80, :].astype(F32)
    for t in range(4):
        wait_bytes(t1.at[pl.ds(0, ZH)], a_recv.at[13 + t])
        gate_chip(place(3, t, -1))

    for n in range(4):
        wait_bytes(t1.at[pl.ds(0, INNER - 1)], a_send.at[n])
    wait_bytes(ls_r.at[pl.ds(0, XY - 1)], m_send.at[0])
    wait_bytes(rs_r.at[pl.ds(0, XY - 1)], m_send.at[1])
    for gift in gifts:
        gift.wait_send()
    half = ggate_v.at[pl.ds(0, ROWS)]
    for n in (5, 6):
        wait_bytes(half, l_sem.at[n])
        wait_bytes(half, e_send.at[n])
        wait_bytes(half, e_recv.at[n])


def hand_on(*refs):
    results, outputs, sem = refs[:4], refs[4:8], refs[8]
    parts = []
    for src, dst in zip(results[:2], outputs[:2]):
        for p in range(ROWS):
            parts.append((src.at[0, p], dst.at[0, p]))
    parts.extend(zip(results[2:], outputs[2:]))
    copies = [pltpu.make_async_copy(src, dst, sem.at[n]) for n, (src, dst) in enumerate(parts)]
    for copy in copies:
        copy.start()
    for copy in copies:
        copy.wait()


def body(*operands):
    hbm = pl.BlockSpec(memory_space=pl.ANY)
    shapes = (
        ((1, ROWS, Q, 2 * CG), BF16),
        ((1, ROWS, Q, 2 * CG), BF16),
        ((1, Q, Q), F32),
        ((1, P_ALL, P_ALL), F32),
    )
    blocks = pltpu.VMEM((INNER, BLK, CG), BF16)
    rows = pltpu.VMEM((CHIP, Q, CG), BF16)
    wide = pltpu.VMEM((LANES, INNER * BLK, 128), F32)
    columns = pltpu.VMEM((QB, P_ALL, CG), BF16)
    scratch = [blocks] * 8 + [
        rows, rows, rows,
        pltpu.VMEM((Q, Q), BF16),
        pltpu.VMEM((P_ALL, P_ALL), BF16),
        rows, rows,
        wide, wide, wide,
        columns, columns,
        rows,
        pltpu.VMEM((Q, Q), BF16),
        pltpu.VMEM((P_ALL, P_ALL), BF16),
        pltpu.VMEM((XY, 32, Q), BF16),
        pltpu.VMEM((XY, 32, Q), BF16),
        pltpu.VMEM((XY, 16, P_ALL), BF16),
        pltpu.VMEM((XY, 16, P_ALL), BF16),
        pltpu.VMEM((80, 256), BF16),
        pltpu.VMEM((8, 80, 256), BF16),
        pltpu.VMEM((XY, 80, 256), BF16),
        pltpu.SemaphoreType.DMA((4,)),
        pltpu.SemaphoreType.DMA((17,)),
        pltpu.SemaphoreType.DMA((5,)),
        pltpu.SemaphoreType.DMA((5,)),
        pltpu.SemaphoreType.DMA((7,)),
        pltpu.SemaphoreType.DMA((7,)),
        pltpu.SemaphoreType.DMA((9,)),
    ]
    results = pl.pallas_call(
        kernel,
        out_shape=tuple(pltpu.VMEM(*shape) for shape in shapes),
        in_specs=[hbm] * 5,
        out_specs=(pl.BlockSpec(memory_space=pltpu.VMEM),) * 4,
        scratch_shapes=scratch,
        compiler_params=pltpu.CompilerParams(
            collective_id=0, has_side_effects=True, vmem_limit_bytes=52 * 1024 * 1024
        ),
        cost_estimate=pl.CostEstimate(flops=4 * 10**9, bytes_accessed=12 * 10**6, transcendentals=3 * 10**6),
    )(*(pltpu.with_memory_space_constraint(a, pltpu.HBM) for a in operands))
    return pl.pallas_call(
        hand_on,
        out_shape=tuple(jax.ShapeDtypeStruct(*shape) for shape in shapes),
        in_specs=[pl.BlockSpec(memory_space=pltpu.VMEM)] * 4,
        out_specs=(hbm,) * 4,
        scratch_shapes=[pltpu.SemaphoreType.DMA((6,))],
        compiler_params=pltpu.CompilerParams(vmem_limit_bytes=8 * 1024 * 1024),
        cost_estimate=pl.CostEstimate(flops=0, bytes_accessed=9 * 10**6, transcendentals=0),
    )(*(pltpu.with_memory_space_constraint(a, pltpu.VMEM) for a in results))


def solution(mesh):
    rows = P("dp", ("inner", "outer"), None, None)
    return jax.shard_map(
        body,
        mesh=mesh,
        in_specs=(rows, rows, rows, P(), P()),
        out_specs=(rows, rows, P("dp", None, None), P("dp", None, None)),
        check_vma=False,
    )
```

```python
import jax
import jax.numpy as jnp
from jax import lax
from jax.experimental import pallas as pl
from jax.experimental.pallas import tpu as pltpu
from jax.sharding import PartitionSpec as P

MESH = pl.DeviceIdType.MESH
F32 = jnp.float32
BF16 = jnp.bfloat16

INNER = 64
ZH = 4
XY = 16
ROWS = 2
CHIP = 4
CG = 384
LANES = CG // 128
Q = 512
P_ALL = 256
QB = 8
BLK = CHIP * QB

BEFORE_COLS = (0, 1)
AFTER_COLS = (2, 3)
AFTER_PLANE = (4, 5)
AFTER_Z = (6,)
AFTER_SHARES = (7,)


def gelu_value(mixed):
    return mixed * (0.5 * (1.0 + lax.erf(mixed * 0.7071067811865476)))


def gelu_slope(mixed):
    normal_cdf = 0.5 * (1.0 + lax.erf(mixed * 0.7071067811865476))
    density = jnp.exp(-0.5 * mixed * mixed) * 0.3989422804014327
    return normal_cdf + mixed * density


def wait_bytes(ref, sem):
    pltpu.make_async_copy(ref, ref, sem).wait()


def dot(a, b, ca, cb):
    return lax.dot_general(a, b, (((ca,), (cb,)), ((), ())), preferred_element_type=F32)


def kernel(
    x_h, gate_h, gout_h, rf_h, lf_h,
    gin_o, ggate_o, gr_o, gl_o,
    s1, s2, r1, r2, t1, t2, b1, b2,
    x, gate, gout, rf, lf, gin_v, ggate_v,
    wide_a, wide_b, wide_c, colsb, gmb, gcb, rt, lt,
    rs_s, rs_r, ls_s, ls_r, share, zrecv, fin,
    a_send, a_recv, m_send, m_recv, e_send, e_recv, l_sem,
):
    i = lax.axis_index("inner")
    c = lax.axis_index("outer")
    d = lax.axis_index("dp")
    zh = i % ZH
    j = i // ZH
    ys = [(j // 4 + n) % 4 for n in range(4)]
    xs = [(j % 4 + n) % 4 for n in range(4)]
    mine = pl.ds(pl.multiple_of(c * CG, CG), CG)
    theirs = pl.ds(pl.multiple_of((1 - c) * CG, CG), CG)
    my_rows = pl.ds(c * ROWS, ROWS)
    their_rows = pl.ds((1 - c) * ROWS, ROWS)

    def place(e, t, sign):
        return ys[sign * (e + t) % 4] * 4 + xs[sign * t % 4]

    def source(e, t):
        return lax.rem(ys[0] + 8 - e - t, 4) * 4 + lax.rem(xs[0] + 4 - t, 4)

    def each_partner(e, act, first=0, last=ZH):
        def step(u, _):
            for t in range(4):
                act(place(e, t, 1) * ZH + lax.rem(zh + t + u, ZH))
            return 0

        lax.fori_loop(first, last, step, 0)

    arrays = ((x_h, x), (gate_h, gate), (gout_h, gout))
    loads = [
        pltpu.make_async_copy(src.at[0, :, :, mine], dst.at[my_rows], l_sem.at[n])
        for n, (src, dst) in enumerate(arrays)
    ]
    loads.append(pltpu.make_async_copy(rf_h.at[c], rf, l_sem.at[3]))
    loads.append(pltpu.make_async_copy(lf_h.at[c], lf, l_sem.at[4]))
    for n in (0, 3, 1, 2, 4):
        loads[n].start()

    barrier = pltpu.get_barrier_semaphore()

    def greet(ii):
        pl.semaphore_signal(barrier, inc=1, device_id={"inner": ii, "dp": 1 - d}, device_id_type=MESH)

    pl.semaphore_signal(barrier, inc=1, device_id={"outer": 1 - c}, device_id_type=MESH)
    for e in range(4):
        each_partner(e, greet)
    for k in range(1, ZH):
        pl.semaphore_signal(
            barrier, inc=1, device_id={"inner": j * ZH + (zh + k) % ZH}, device_id_type=MESH
        )

    def greet_plane(k, _):
        pl.semaphore_signal(barrier, inc=1, device_id={"inner": lax.rem(j + k, XY) * ZH + zh}, device_id_type=MESH)
        return 0

    lax.fori_loop(1, XY, greet_plane, 0)

    def right_mix(h):
        def step(m, _):
            lhs = rf[pl.ds(pl.multiple_of(m * 128, 128), 128), :]
            parts = [dot(lhs, x[h * ROWS + p], 1, 0).reshape(16, QB, CG) for p in range(ROWS)]
            half = pl.ds(pl.multiple_of(h * 16, 16), 16)
            s1[pl.ds(m * 16, 16), half, :] = jnp.concatenate(parts, axis=1).astype(BF16)
            return 0

        lax.fori_loop(0, 4, step, 0)

    loads[0].wait()
    loads[3].wait()
    right_mix(c)

    pl.semaphore_wait(barrier, 1 + INNER + (ZH - 1) + (XY - 1))
    gifts = [
        pltpu.make_async_remote_copy(
            src_ref=src.at[0, :, :, theirs], dst_ref=dst.at[my_rows], send_sem=e_send.at[n], recv_sem=e_recv.at[n],
            device_id={"outer": 1 - c}, device_id_type=MESH,
        )
        for n, (src, dst) in enumerate(arrays)
    ]
    gifts[0].start()

    def weigh(e):
        for t in range(4):
            jj = place(e, t, 1)
            rows = pl.ds(pl.multiple_of(jj * 32, 32), 32)
            parts = []
            for p in range(CHIP):
                a = gout[p, rows, :].astype(F32)
                b = gate[p, rows, :].astype(F32)
                parts.append((a * b).reshape(4, QB, CG))
            s2[pl.ds(jj * 4, 4)] = jnp.concatenate(parts, axis=1).astype(BF16)

    def send_to(src, dst, n, sem, ii):
        pltpu.make_async_remote_copy(
            src_ref=src.at[ii], dst_ref=dst.at[i], send_sem=a_send.at[n], recv_sem=a_recv.at[sem],
            device_id={"inner": ii, "dp": 1 - d}, device_id_type=MESH,
        ).start()

    def send_chunk(src, dst, n, e, first=0, last=ZH):
        each_partner(e, lambda ii: send_to(src, dst, n, 4 * n - 3 + e, ii), first, last)

    def send_mixed(*pieces):
        for k in pieces:
            if k < 6:
                send_chunk(t1, b1, 2, k // 2, k % 2 * 2, k % 2 * 2 + 2)
            else:
                for t in (k % 2 * 2, k % 2 * 2 + 1):
                    def step(u, _):
                        send_to(t1, b1, 2, 13 + t, place(3, t, 1) * ZH + lax.rem(zh + t + u, ZH))
                        return 0

                    lax.fori_loop(0, ZH, step, 0)

    def wait_chunk(n, e):
        wait_bytes(t1.at[pl.ds(0, XY)], a_recv.at[4 * n - 3 + e])

    def send_half(h):
        half = pl.ds(pl.multiple_of(h * 16, 16), 16)

        def act(ii):
            pltpu.make_async_remote_copy(
                src_ref=s1.at[ii, half], dst_ref=r1.at[i, half], send_sem=a_send.at[0], recv_sem=a_recv.at[0],
                device_id={"inner": ii, "dp": 1 - d}, device_id_type=MESH,
            ).start()

        for e in range(4):
            each_partner(e, act)

    send_half(c)
    gifts[0].wait_recv()
    gifts[1].start()
    gifts[2].start()
    right_mix(1 - c)
    send_half(1 - c)
    loads[1].wait()
    loads[2].wait()
    gifts[1].wait_recv()
    gifts[2].wait_recv()
    for e in range(4):
        weigh(e)
        send_chunk(s2, r2, 1, e)
    loads[4].wait()
    lt[...] = lf[...].astype(F32).T.astype(BF16)
    for h in range(2):
        rt[:, h * 256:(h + 1) * 256] = rf[h * 256:(h + 1) * 256, :].astype(F32).T.astype(BF16)

    def column(q):
        return jnp.concatenate([wide_a[n, pl.ds(q, P_ALL, stride=QB), :] for n in range(LANES)], axis=1)

    wait_bytes(t1, a_recv.at[0])

    def widen(m, _):
        v = r1[pl.ds(m * 4, 4)].reshape(128, CG).astype(F32)
        for n in range(LANES):
            wide_a[n, pl.ds(pl.multiple_of(m * 128, 128), 128), :] = v[:, n * 128:(n + 1) * 128]
        return 0

    lax.fori_loop(0, XY, widen, 0)
    for q in range(QB):
        xq = column(q).astype(BF16)
        colsb[q] = xq
        mixed = dot(lf[...], xq, 1, 0)
        for n in range(LANES):
            wide_b[n, pl.ds(q, P_ALL, stride=QB), :] = mixed[:, n * 128:(n + 1) * 128]

    def narrow(m, _):
        for n in range(LANES):
            v = wide_b[n, pl.ds(pl.multiple_of(m * 64, 64), 64), :].astype(BF16)
            t1[pl.ds(m * 2, 2), :, n * 128:(n + 1) * 128] = v.reshape(2, BLK, 128)
        return 0

    lax.fori_loop(0, 32, narrow, 0)
    send_mixed(*BEFORE_COLS)

    def slopes(m, _):
        rows = pl.ds(pl.multiple_of(m * 64, 64), 64)
        for n in range(LANES):
            wide_b[n, rows, :] = gelu_slope(wide_b[n, rows, :])
        return 0

    lax.fori_loop(0, 32, slopes, 0)

    for e in range(4):
        wait_chunk(1, e)
        for t in range(4):
            jj = place(e, t, -1)
            rows = pl.ds(pl.multiple_of(jj * 128, 128), 128)
            v = r2[pl.ds(jj * 4, 4)].reshape(128, CG).astype(F32)
            for n in range(LANES):
                wide_a[n, rows, :] = v[:, n * 128:(n + 1) * 128] * wide_b[n, rows, :]
    for q in range(QB):
        gmb[q] = column(q).astype(BF16)

    for e in range(4):
        spots = [place(e, t, 1) for t in range(4)]
        lhs = jnp.concatenate([lt[pl.ds(pl.multiple_of(jj * 16, 16), 16), :] for jj in spots], axis=0)
        for q in range(QB):
            v = dot(lhs, gmb[q], 1, 0)
            for t, jj in enumerate(spots):
                for n in range(LANES):
                    wide_c[n, pl.ds(jj * 128 + q, 16, stride=QB), :] = v[t * 16:(t + 1) * 16, n * 128:(n + 1) * 128]
        for jj in spots:
            rows = pl.ds(pl.multiple_of(jj * 128, 128), 128)
            for n in range(LANES):
                v = wide_c[n, rows, :].astype(BF16)
                t2[pl.ds(jj * 4, 4), :, n * 128:(n + 1) * 128] = v.reshape(4, BLK, 128)
        send_chunk(t2, b2, 3, e)
    send_mixed(*AFTER_COLS)
    gl_acc = jnp.zeros((P_ALL, P_ALL), F32)
    for q in range(QB):
        gl_acc = gl_acc + dot(gmb[q], colsb[q], 1, 1)
    ls_s[...] = gl_acc.astype(BF16).reshape(XY, 16, P_ALL)

    def scatter(src, dst, n, e):
        for t in range(1 if e == 0 else 0, 4):
            jj = place(e, t, -1)
            pltpu.make_async_remote_copy(
                src_ref=src.at[jj], dst_ref=dst.at[j], send_sem=m_send.at[n], recv_sem=m_recv.at[n],
                device_id={"inner": jj * ZH + zh}, device_id_type=MESH,
            ).start()

    for e in range(4):
        scatter(ls_s, ls_r, 0, e)
    ls_r[j] = ls_s[j]

    def hand_out(src, dst, rows, n):
        pltpu.make_async_copy(src.at[my_rows, rows], dst.at[0, :, rows, mine], l_sem.at[n]).start()
        pltpu.make_async_remote_copy(
            src_ref=src.at[their_rows, rows], dst_ref=dst.at[0, :, rows, mine],
            send_sem=e_send.at[n], recv_sem=e_recv.at[n],
            device_id={"outer": 1 - c}, device_id_type=MESH,
        ).start()

    def gate_chip(jj):
        rows = pl.ds(pl.multiple_of(jj * 32, 32), 32)
        v = b1[pl.ds(jj * 4, 4)].astype(F32)
        for p in range(CHIP):
            act = gelu_value(v[:, p * QB:(p + 1) * QB, :].reshape(32, CG))
            ggate_v[p, rows, :] = (gout[p, rows, :].astype(F32) * act).astype(BF16)
        hand_out(ggate_v, ggate_o, rows, 6)

    def gate_grad(e):
        wait_chunk(2, e)

        def step(t, _):
            gate_chip(source(e, t))
            return 0

        lax.fori_loop(0, 4, step, 0)

    gate_grad(0)

    for e in range(4):
        wait_chunk(3, e)
        spots = [place(e, t, -1) for t in range(4)]
        parts = [[] for _ in range(CHIP)]
        for jj in spots:
            rows = pl.ds(pl.multiple_of(jj * 32, 32), 32)
            v = b2[pl.ds(jj * 4, 4)].astype(F32)
            for p in range(CHIP):
                part = v[:, p * QB:(p + 1) * QB, :].reshape(32, CG).astype(BF16)
                gcb[p, rows, :] = part
                parts[p].append(part)
        total = None
        for p in range(CHIP):
            term = dot(jnp.concatenate(parts[p], axis=0), x[p], 1, 1)
            total = term if total is None else total + term
        for t, jj in enumerate(spots):
            rs_s[jj] = total[t * 32:(t + 1) * 32, :].astype(BF16)
        scatter(rs_s, rs_r, 1, e)
    rs_r[j] = rs_s[j]
    send_mixed(*AFTER_PLANE)

    def input_grad(m, _):
        rows = pl.ds(pl.multiple_of(m * 128, 128), 128)
        for p in range(CHIP):
            gin_v[p, rows, :] = dot(rt[rows, :], gcb[p], 1, 0).astype(BF16)
        hand_out(gin_v, gin_o, rows, 5)
        return 0

    lax.fori_loop(0, 4, input_grad, 0)

    wait_bytes(ls_r.at[pl.ds(0, XY - 1)], m_recv.at[0])
    wait_bytes(rs_r.at[pl.ds(0, XY - 1)], m_recv.at[1])
    gr_sum = rs_r[0].astype(F32)
    gl_sum = ls_r[0].astype(F32)
    for k in range(1, XY):
        gr_sum = gr_sum + rs_r[k].astype(F32)
        gl_sum = gl_sum + ls_r[k].astype(F32)
    share[0:32, :] = gr_sum[:, 0:256].astype(BF16)
    share[32:64, :] = gr_sum[:, 256:512].astype(BF16)
    share[64:80, :] = gl_sum.astype(BF16)

    def to_z(k):
        return pltpu.make_async_remote_copy(
            src_ref=share, dst_ref=zrecv.at[zh * 2 + d], send_sem=m_send.at[2], recv_sem=m_recv.at[2],
            device_id={"inner": j * ZH + (zh + k) % ZH, "dp": c}, device_id_type=MESH,
        )

    for k in range(1, ZH):
        to_z(k).start()

    @pl.when(d != c)
    def _():
        to_z(0).start()

    send_mixed(*AFTER_Z)
    gate_grad(1)

    @pl.when(d == c)
    def _():
        zrecv[zh * 2 + d] = share[...]
        wait_bytes(zrecv.at[pl.ds(0, 7)], m_recv.at[2])
        total = zrecv[0].astype(F32)
        for k in range(1, 8):
            total = total + zrecv[k].astype(F32)
        fin[j] = total.astype(BF16)

        def give(k, _):
            jj = (j + k) % XY
            pltpu.make_async_remote_copy(
                src_ref=fin.at[j], dst_ref=fin.at[j], send_sem=m_send.at[3], recv_sem=m_recv.at[3],
                device_id={"inner": jj * ZH + zh}, device_id_type=MESH,
            ).start()
            return 0

        lax.fori_loop(1, XY, give, 0)

    send_mixed(*AFTER_SHARES)
    gate_grad(2)

    @pl.when(d == c)
    def _():
        wait_bytes(fin.at[pl.ds(0, XY - 1)], m_recv.at[3])
        pltpu.make_async_remote_copy(
            src_ref=fin, dst_ref=fin, send_sem=m_send.at[4], recv_sem=m_recv.at[4],
            device_id={"outer": 1 - c}, device_id_type=MESH,
        ).start()
        wait_bytes(fin.at[pl.ds(0, XY - 1)], m_send.at[3])
        wait_bytes(zrecv.at[pl.ds(0, 3)], m_send.at[2])
        wait_bytes(fin, m_send.at[4])

    @pl.when(d != c)
    def _():
        wait_bytes(zrecv.at[pl.ds(0, 4)], m_send.at[2])
        wait_bytes(fin, m_recv.at[4])

    for k in range(XY):
        gr_o[0, k * 32:(k + 1) * 32, 0:256] = fin[k, 0:32, :].astype(F32)
        gr_o[0, k * 32:(k + 1) * 32, 256:512] = fin[k, 32:64, :].astype(F32)
        gl_o[0, k * 16:(k + 1) * 16, :] = fin[k, 64:80, :].astype(F32)
    for t in range(4):
        wait_bytes(t1.at[pl.ds(0, ZH)], a_recv.at[13 + t])
        gate_chip(place(3, t, -1))

    for n in range(4):
        wait_bytes(t1, a_send.at[n])
    wait_bytes(ls_r.at[pl.ds(0, XY - 1)], m_send.at[0])
    wait_bytes(rs_r.at[pl.ds(0, XY - 1)], m_send.at[1])
    for gift in gifts:
        gift.wait_send()
    half = ggate_v.at[pl.ds(0, ROWS)]
    for n in (5, 6):
        wait_bytes(half, l_sem.at[n])
        wait_bytes(half, e_send.at[n])
        wait_bytes(half, e_recv.at[n])


def hand_on(*refs):
    results, outputs, sem = refs[:4], refs[4:8], refs[8]
    parts = []
    for src, dst in zip(results[:2], outputs[:2]):
        for p in range(ROWS):
            parts.append((src.at[0, p], dst.at[0, p]))
    parts.extend(zip(results[2:], outputs[2:]))
    copies = [pltpu.make_async_copy(src, dst, sem.at[n]) for n, (src, dst) in enumerate(parts)]
    for copy in copies:
        copy.start()
    for copy in copies:
        copy.wait()


def body(*operands):
    hbm = pl.BlockSpec(memory_space=pl.ANY)
    shapes = (
        ((1, ROWS, Q, 2 * CG), BF16),
        ((1, ROWS, Q, 2 * CG), BF16),
        ((1, Q, Q), F32),
        ((1, P_ALL, P_ALL), F32),
    )
    blocks = pltpu.VMEM((INNER, BLK, CG), BF16)
    rows = pltpu.VMEM((CHIP, Q, CG), BF16)
    wide = pltpu.VMEM((LANES, INNER * BLK, 128), F32)
    columns = pltpu.VMEM((QB, P_ALL, CG), BF16)
    scratch = [blocks] * 8 + [
        rows, rows, rows,
        pltpu.VMEM((Q, Q), BF16),
        pltpu.VMEM((P_ALL, P_ALL), BF16),
        rows, rows,
        wide, wide, wide,
        columns, columns,
        rows,
        pltpu.VMEM((Q, Q), BF16),
        pltpu.VMEM((P_ALL, P_ALL), BF16),
        pltpu.VMEM((XY, 32, Q), BF16),
        pltpu.VMEM((XY, 32, Q), BF16),
        pltpu.VMEM((XY, 16, P_ALL), BF16),
        pltpu.VMEM((XY, 16, P_ALL), BF16),
        pltpu.VMEM((80, 256), BF16),
        pltpu.VMEM((8, 80, 256), BF16),
        pltpu.VMEM((XY, 80, 256), BF16),
        pltpu.SemaphoreType.DMA((4,)),
        pltpu.SemaphoreType.DMA((17,)),
        pltpu.SemaphoreType.DMA((5,)),
        pltpu.SemaphoreType.DMA((5,)),
        pltpu.SemaphoreType.DMA((7,)),
        pltpu.SemaphoreType.DMA((7,)),
        pltpu.SemaphoreType.DMA((9,)),
    ]
    results = pl.pallas_call(
        kernel,
        out_shape=tuple(pltpu.VMEM(*shape) for shape in shapes),
        in_specs=[hbm] * 5,
        out_specs=(pl.BlockSpec(memory_space=pltpu.VMEM),) * 4,
        scratch_shapes=scratch,
        compiler_params=pltpu.CompilerParams(
            collective_id=0, has_side_effects=True, vmem_limit_bytes=52 * 1024 * 1024
        ),
        cost_estimate=pl.CostEstimate(flops=4 * 10**9, bytes_accessed=12 * 10**6, transcendentals=3 * 10**6),
    )(*(pltpu.with_memory_space_constraint(a, pltpu.HBM) for a in operands))
    return pl.pallas_call(
        hand_on,
        out_shape=tuple(jax.ShapeDtypeStruct(*shape) for shape in shapes),
        in_specs=[pl.BlockSpec(memory_space=pltpu.VMEM)] * 4,
        out_specs=(hbm,) * 4,
        scratch_shapes=[pltpu.SemaphoreType.DMA((6,))],
        compiler_params=pltpu.CompilerParams(vmem_limit_bytes=8 * 1024 * 1024),
        cost_estimate=pl.CostEstimate(flops=0, bytes_accessed=9 * 10**6, transcendentals=0),
    )(*(pltpu.with_memory_space_constraint(a, pltpu.VMEM) for a in results))


def solution(mesh):
    rows = P("dp", ("inner", "outer"), None, None)
    return jax.shard_map(
        body,
        mesh=mesh,
        in_specs=(rows, rows, rows, P(), P()),
        out_specs=(rows, rows, P("dp", None, None), P("dp", None, None)),
        check_vma=False,
    )
```

```python
import jax
import jax.numpy as jnp
from jax import lax
from jax.experimental import pallas as pl
from jax.experimental.pallas import tpu as pltpu
from jax.sharding import PartitionSpec as P

MESH = pl.DeviceIdType.MESH
F32 = jnp.float32
BF16 = jnp.bfloat16

INNER = 64
ZH = 4
XY = 16
ROWS = 2
CHIP = 4
CG = 384
LANES = CG // 128
Q = 512
P_ALL = 256
QB = 8
BLK = CHIP * QB

BEFORE_COLS = (0, 1, 2)
AFTER_COLS = (3, 4)
AFTER_PLANE = (5,)
AFTER_Z = (6,)
AFTER_SHARES = (7,)


def gelu_value(mixed):
    return mixed * (0.5 * (1.0 + lax.erf(mixed * 0.7071067811865476)))


def gelu_slope(mixed):
    normal_cdf = 0.5 * (1.0 + lax.erf(mixed * 0.7071067811865476))
    density = jnp.exp(-0.5 * mixed * mixed) * 0.3989422804014327
    return normal_cdf + mixed * density


def wait_bytes(ref, sem):
    pltpu.make_async_copy(ref, ref, sem).wait()


def dot(a, b, ca, cb):
    return lax.dot_general(a, b, (((ca,), (cb,)), ((), ())), preferred_element_type=F32)


def kernel(
    x_h, gate_h, gout_h, rf_h, lf_h,
    gin_o, ggate_o, gr_o, gl_o,
    s1, s2, r1, r2, t1, t2, b1, b2,
    x, gate, gout, rf, lf, gin_v, ggate_v,
    wide_a, wide_b, wide_c, colsb, gmb, gcb, rt, lt,
    rs_s, rs_r, ls_s, ls_r, share, zrecv, fin,
    a_send, a_recv, m_send, m_recv, e_send, e_recv, l_sem,
):
    i = lax.axis_index("inner")
    c = lax.axis_index("outer")
    d = lax.axis_index("dp")
    zh = i % ZH
    j = i // ZH
    ys = [(j // 4 + n) % 4 for n in range(4)]
    xs = [(j % 4 + n) % 4 for n in range(4)]
    mine = pl.ds(pl.multiple_of(c * CG, CG), CG)
    theirs = pl.ds(pl.multiple_of((1 - c) * CG, CG), CG)
    my_rows = pl.ds(c * ROWS, ROWS)
    their_rows = pl.ds((1 - c) * ROWS, ROWS)

    def place(e, t, sign):
        return ys[sign * (e + t) % 4] * 4 + xs[sign * t % 4]

    def source(e, t):
        return lax.rem(ys[0] + 8 - e - t, 4) * 4 + lax.rem(xs[0] + 4 - t, 4)

    yc = [(j // 4 + n + 2 * c) % 4 for n in range(4)]
    xc = [(j % 4 + n + 2 * c) % 4 for n in range(4)]

    def each_partner(e, act, first=0, last=ZH):
        def step(u, _):
            for t in range(4):
                act((yc[(e + t) % 4] * 4 + xc[t]) * ZH + lax.rem(zh + t + u, ZH))
            return 0

        lax.fori_loop(first, last, step, 0)

    arrays = ((x_h, x), (gate_h, gate), (gout_h, gout))
    loads = [
        pltpu.make_async_copy(src.at[0, :, :, mine], dst.at[my_rows], l_sem.at[n])
        for n, (src, dst) in enumerate(arrays)
    ]
    loads.append(pltpu.make_async_copy(rf_h.at[c], rf, l_sem.at[3]))
    loads.append(pltpu.make_async_copy(lf_h.at[c], lf, l_sem.at[4]))
    for n in (0, 3, 1, 2, 4):
        loads[n].start()

    barrier = pltpu.get_barrier_semaphore()

    def greet(ii):
        pl.semaphore_signal(barrier, inc=1, device_id={"inner": ii, "dp": 1 - d}, device_id_type=MESH)

    pl.semaphore_signal(barrier, inc=1, device_id={"outer": 1 - c}, device_id_type=MESH)
    for e in range(4):
        each_partner(e, greet)
    for k in range(1, ZH):
        pl.semaphore_signal(
            barrier, inc=1, device_id={"inner": j * ZH + (zh + k) % ZH}, device_id_type=MESH
        )

    def greet_plane(k, _):
        pl.semaphore_signal(barrier, inc=1, device_id={"inner": lax.rem(j + k, XY) * ZH + zh}, device_id_type=MESH)
        return 0

    lax.fori_loop(1, XY, greet_plane, 0)

    def right_mix(h):
        def step(m, _):
            lhs = rf[pl.ds(pl.multiple_of(m * 128, 128), 128), :]
            parts = [dot(lhs, x[h * ROWS + p], 1, 0).reshape(16, QB, CG) for p in range(ROWS)]
            half = pl.ds(pl.multiple_of(h * 16, 16), 16)
            s1[pl.ds(m * 16, 16), half, :] = jnp.concatenate(parts, axis=1).astype(BF16)
            return 0

        lax.fori_loop(0, 4, step, 0)

    loads[0].wait()
    loads[3].wait()
    right_mix(c)

    pl.semaphore_wait(barrier, 1 + INNER + (ZH - 1) + (XY - 1))
    gifts = [
        pltpu.make_async_remote_copy(
            src_ref=src.at[0, :, :, theirs], dst_ref=dst.at[my_rows], send_sem=e_send.at[n], recv_sem=e_recv.at[n],
            device_id={"outer": 1 - c}, device_id_type=MESH,
        )
        for n, (src, dst) in enumerate(arrays)
    ]
    gifts[0].start()

    def weigh(e):
        for t in range(4):
            jj = place(e, t, 1)
            rows = pl.ds(pl.multiple_of(jj * 32, 32), 32)
            parts = []
            for p in range(CHIP):
                a = gout[p, rows, :].astype(F32)
                b = gate[p, rows, :].astype(F32)
                parts.append((a * b).reshape(4, QB, CG))
            s2[pl.ds(jj * 4, 4)] = jnp.concatenate(parts, axis=1).astype(BF16)

    def send_to(src, dst, n, sem, ii):
        pltpu.make_async_remote_copy(
            src_ref=src.at[ii], dst_ref=dst.at[i], send_sem=a_send.at[n], recv_sem=a_recv.at[sem],
            device_id={"inner": ii, "dp": 1 - d}, device_id_type=MESH,
        ).start()

    def send_chunk(src, dst, n, e, first=0, last=ZH):
        each_partner(e, lambda ii: send_to(src, dst, n, 4 * n - 3 + e, ii), first, last)

    def send_mixed(*pieces):
        for k in pieces:
            if k < 6:
                send_chunk(t1, b1, 2, k // 2, k % 2 * 2, k % 2 * 2 + 2)
            else:
                for t in (k % 2 * 2, k % 2 * 2 + 1):
                    def step(u, _):
                        send_to(t1, b1, 2, 13 + t, place(3, t, 1) * ZH + lax.rem(zh + t + u, ZH))
                        return 0

                    lax.fori_loop(0, ZH, step, 0)

    def wait_chunk(n, e):
        wait_bytes(t1.at[pl.ds(0, XY)], a_recv.at[4 * n - 3 + e])

    def send_half(h):
        half = pl.ds(pl.multiple_of(h * 16, 16), 16)

        def act(ii):
            pltpu.make_async_remote_copy(
                src_ref=s1.at[ii, half], dst_ref=r1.at[i, half], send_sem=a_send.at[0], recv_sem=a_recv.at[0],
                device_id={"inner": ii, "dp": 1 - d}, device_id_type=MESH,
            ).start()

        for e in range(4):
            each_partner(e, act)

    send_half(c)
    gifts[0].wait_recv()
    gifts[1].start()
    gifts[2].start()
    right_mix(1 - c)
    send_half(1 - c)
    loads[1].wait()
    loads[2].wait()
    gifts[1].wait_recv()
    gifts[2].wait_recv()
    for e in range(4):
        weigh(e)
        send_chunk(s2, r2, 1, e)
    loads[4].wait()
    lt[...] = lf[...].astype(F32).T.astype(BF16)
    for h in range(2):
        rt[:, h * 256:(h + 1) * 256] = rf[h * 256:(h + 1) * 256, :].astype(F32).T.astype(BF16)

    def column(q):
        return jnp.concatenate([wide_a[n, pl.ds(q, P_ALL, stride=QB), :] for n in range(LANES)], axis=1)

    wait_bytes(t1, a_recv.at[0])

    def widen(m, _):
        v = r1[pl.ds(m * 4, 4)].reshape(128, CG).astype(F32)
        for n in range(LANES):
            wide_a[n, pl.ds(pl.multiple_of(m * 128, 128), 128), :] = v[:, n * 128:(n + 1) * 128]
        return 0

    lax.fori_loop(0, XY, widen, 0)
    for q in range(QB):
        xq = column(q).astype(BF16)
        colsb[q] = xq
        mixed = dot(lf[...], xq, 1, 0)
        for n in range(LANES):
            wide_b[n, pl.ds(q, P_ALL, stride=QB), :] = mixed[:, n * 128:(n + 1) * 128]

    def narrow(m, _):
        for n in range(LANES):
            v = wide_b[n, pl.ds(pl.multiple_of(m * 64, 64), 64), :].astype(BF16)
            t1[pl.ds(m * 2, 2), :, n * 128:(n + 1) * 128] = v.reshape(2, BLK, 128)
        return 0

    lax.fori_loop(0, 32, narrow, 0)
    send_mixed(*BEFORE_COLS)

    def slopes(m, _):
        rows = pl.ds(pl.multiple_of(m * 64, 64), 64)
        for n in range(LANES):
            wide_b[n, rows, :] = gelu_slope(wide_b[n, rows, :])
        return 0

    lax.fori_loop(0, 32, slopes, 0)

    for e in range(4):
        wait_chunk(1, e)
        for t in range(4):
            jj = place(e, t, -1)
            rows = pl.ds(pl.multiple_of(jj * 128, 128), 128)
            v = r2[pl.ds(jj * 4, 4)].reshape(128, CG).astype(F32)
            for n in range(LANES):
                wide_a[n, rows, :] = v[:, n * 128:(n + 1) * 128] * wide_b[n, rows, :]
    for q in range(QB):
        gmb[q] = column(q).astype(BF16)

    for e in range(4):
        spots = [place(e, t, 1) for t in range(4)]
        lhs = jnp.concatenate([lt[pl.ds(pl.multiple_of(jj * 16, 16), 16), :] for jj in spots], axis=0)
        for q in range(QB):
            v = dot(lhs, gmb[q], 1, 0)
            for t, jj in enumerate(spots):
                for n in range(LANES):
                    wide_c[n, pl.ds(jj * 128 + q, 16, stride=QB), :] = v[t * 16:(t + 1) * 16, n * 128:(n + 1) * 128]
        for jj in spots:
            rows = pl.ds(pl.multiple_of(jj * 128, 128), 128)
            for n in range(LANES):
                v = wide_c[n, rows, :].astype(BF16)
                t2[pl.ds(jj * 4, 4), :, n * 128:(n + 1) * 128] = v.reshape(4, BLK, 128)
        send_chunk(t2, b2, 3, e)
    send_mixed(*AFTER_COLS)
    gl_acc = jnp.zeros((P_ALL, P_ALL), F32)
    for q in range(QB):
        gl_acc = gl_acc + dot(gmb[q], colsb[q], 1, 1)
    ls_s[...] = gl_acc.astype(BF16).reshape(XY, 16, P_ALL)

    def scatter(src, dst, n, e):
        for t in range(1 if e == 0 else 0, 4):
            jj = place(e, t, -1)
            pltpu.make_async_remote_copy(
                src_ref=src.at[jj], dst_ref=dst.at[j], send_sem=m_send.at[n], recv_sem=m_recv.at[n],
                device_id={"inner": jj * ZH + zh}, device_id_type=MESH,
            ).start()

    for e in range(4):
        scatter(ls_s, ls_r, 0, e)
    ls_r[j] = ls_s[j]

    def hand_out(src, dst, rows, n):
        pltpu.make_async_copy(src.at[my_rows, rows], dst.at[0, :, rows, mine], l_sem.at[n]).start()
        pltpu.make_async_remote_copy(
            src_ref=src.at[their_rows, rows], dst_ref=dst.at[0, :, rows, mine],
            send_sem=e_send.at[n], recv_sem=e_recv.at[n],
            device_id={"outer": 1 - c}, device_id_type=MESH,
        ).start()

    def gate_chip(jj):
        rows = pl.ds(pl.multiple_of(jj * 32, 32), 32)
        v = b1[pl.ds(jj * 4, 4)].astype(F32)
        for p in range(CHIP):
            act = gelu_value(v[:, p * QB:(p + 1) * QB, :].reshape(32, CG))
            ggate_v[p, rows, :] = (gout[p, rows, :].astype(F32) * act).astype(BF16)
        hand_out(ggate_v, ggate_o, rows, 6)

    def gate_grad(e):
        wait_chunk(2, e)

        def step(t, _):
            gate_chip(source(e, t))
            return 0

        lax.fori_loop(0, 4, step, 0)

    gate_grad(0)

    for e in range(4):
        wait_chunk(3, e)
        spots = [place(e, t, -1) for t in range(4)]
        parts = [[] for _ in range(CHIP)]
        for jj in spots:
            rows = pl.ds(pl.multiple_of(jj * 32, 32), 32)
            v = b2[pl.ds(jj * 4, 4)].astype(F32)
            for p in range(CHIP):
                part = v[:, p * QB:(p + 1) * QB, :].reshape(32, CG).astype(BF16)
                gcb[p, rows, :] = part
                parts[p].append(part)
        total = None
        for p in range(CHIP):
            term = dot(jnp.concatenate(parts[p], axis=0), x[p], 1, 1)
            total = term if total is None else total + term
        for t, jj in enumerate(spots):
            rs_s[jj] = total[t * 32:(t + 1) * 32, :].astype(BF16)
        scatter(rs_s, rs_r, 1, e)
    rs_r[j] = rs_s[j]
    send_mixed(*AFTER_PLANE)

    def input_grad(m, _):
        rows = pl.ds(pl.multiple_of(m * 128, 128), 128)
        for p in range(CHIP):
            gin_v[p, rows, :] = dot(rt[rows, :], gcb[p], 1, 0).astype(BF16)
        hand_out(gin_v, gin_o, rows, 5)
        return 0

    lax.fori_loop(0, 4, input_grad, 0)

    wait_bytes(ls_r.at[pl.ds(0, XY - 1)], m_recv.at[0])
    wait_bytes(rs_r.at[pl.ds(0, XY - 1)], m_recv.at[1])
    gr_sum = rs_r[0].astype(F32)
    gl_sum = ls_r[0].astype(F32)
    for k in range(1, XY):
        gr_sum = gr_sum + rs_r[k].astype(F32)
        gl_sum = gl_sum + ls_r[k].astype(F32)
    share[0:32, :] = gr_sum[:, 0:256].astype(BF16)
    share[32:64, :] = gr_sum[:, 256:512].astype(BF16)
    share[64:80, :] = gl_sum.astype(BF16)

    def to_z(k):
        return pltpu.make_async_remote_copy(
            src_ref=share, dst_ref=zrecv.at[zh * 2 + d], send_sem=m_send.at[2], recv_sem=m_recv.at[2],
            device_id={"inner": j * ZH + (zh + k) % ZH, "dp": c}, device_id_type=MESH,
        )

    for k in range(1, ZH):
        to_z(k).start()

    @pl.when(d != c)
    def _():
        to_z(0).start()

    send_mixed(*AFTER_Z)
    gate_grad(1)

    @pl.when(d == c)
    def _():
        zrecv[zh * 2 + d] = share[...]
        wait_bytes(zrecv.at[pl.ds(0, 7)], m_recv.at[2])
        total = zrecv[0].astype(F32)
        for k in range(1, 8):
            total = total + zrecv[k].astype(F32)
        fin[j] = total.astype(BF16)

        def give(k, _):
            jj = (j + k) % XY
            pltpu.make_async_remote_copy(
                src_ref=fin.at[j], dst_ref=fin.at[j], send_sem=m_send.at[3], recv_sem=m_recv.at[3],
                device_id={"inner": jj * ZH + zh}, device_id_type=MESH,
            ).start()
            return 0

        lax.fori_loop(1, XY, give, 0)

    send_mixed(*AFTER_SHARES)
    gate_grad(2)

    @pl.when(d == c)
    def _():
        wait_bytes(fin.at[pl.ds(0, XY - 1)], m_recv.at[3])
        pltpu.make_async_remote_copy(
            src_ref=fin, dst_ref=fin, send_sem=m_send.at[4], recv_sem=m_recv.at[4],
            device_id={"outer": 1 - c}, device_id_type=MESH,
        ).start()
        wait_bytes(fin.at[pl.ds(0, XY - 1)], m_send.at[3])
        wait_bytes(zrecv.at[pl.ds(0, 3)], m_send.at[2])
        wait_bytes(fin, m_send.at[4])

    @pl.when(d != c)
    def _():
        wait_bytes(zrecv.at[pl.ds(0, 4)], m_send.at[2])
        wait_bytes(fin, m_recv.at[4])

    for k in range(XY):
        gr_o[0, k * 32:(k + 1) * 32, 0:256] = fin[k, 0:32, :].astype(F32)
        gr_o[0, k * 32:(k + 1) * 32, 256:512] = fin[k, 32:64, :].astype(F32)
        gl_o[0, k * 16:(k + 1) * 16, :] = fin[k, 64:80, :].astype(F32)
    for t in range(4):
        wait_bytes(t1.at[pl.ds(0, ZH)], a_recv.at[13 + t])
        gate_chip(place(3, t, -1))

    for n in range(4):
        wait_bytes(t1, a_send.at[n])
    wait_bytes(ls_r.at[pl.ds(0, XY - 1)], m_send.at[0])
    wait_bytes(rs_r.at[pl.ds(0, XY - 1)], m_send.at[1])
    for gift in gifts:
        gift.wait_send()
    half = ggate_v.at[pl.ds(0, ROWS)]
    for n in (5, 6):
        wait_bytes(half, l_sem.at[n])
        wait_bytes(half, e_send.at[n])
        wait_bytes(half, e_recv.at[n])


def hand_on(*refs):
    results, outputs, sem = refs[:4], refs[4:8], refs[8]
    parts = []
    for src, dst in zip(results[:2], outputs[:2]):
        for p in range(ROWS):
            parts.append((src.at[0, p], dst.at[0, p]))
    parts.extend(zip(results[2:], outputs[2:]))
    copies = [pltpu.make_async_copy(src, dst, sem.at[n]) for n, (src, dst) in enumerate(parts)]
    for copy in copies:
        copy.start()
    for copy in copies:
        copy.wait()


def body(*operands):
    hbm = pl.BlockSpec(memory_space=pl.ANY)
    shapes = (
        ((1, ROWS, Q, 2 * CG), BF16),
        ((1, ROWS, Q, 2 * CG), BF16),
        ((1, Q, Q), F32),
        ((1, P_ALL, P_ALL), F32),
    )
    blocks = pltpu.VMEM((INNER, BLK, CG), BF16)
    rows = pltpu.VMEM((CHIP, Q, CG), BF16)
    wide = pltpu.VMEM((LANES, INNER * BLK, 128), F32)
    columns = pltpu.VMEM((QB, P_ALL, CG), BF16)
    scratch = [blocks] * 8 + [
        rows, rows, rows,
        pltpu.VMEM((Q, Q), BF16),
        pltpu.VMEM((P_ALL, P_ALL), BF16),
        rows, rows,
        wide, wide, wide,
        columns, columns,
        rows,
        pltpu.VMEM((Q, Q), BF16),
        pltpu.VMEM((P_ALL, P_ALL), BF16),
        pltpu.VMEM((XY, 32, Q), BF16),
        pltpu.VMEM((XY, 32, Q), BF16),
        pltpu.VMEM((XY, 16, P_ALL), BF16),
        pltpu.VMEM((XY, 16, P_ALL), BF16),
        pltpu.VMEM((80, 256), BF16),
        pltpu.VMEM((8, 80, 256), BF16),
        pltpu.VMEM((XY, 80, 256), BF16),
        pltpu.SemaphoreType.DMA((4,)),
        pltpu.SemaphoreType.DMA((17,)),
        pltpu.SemaphoreType.DMA((5,)),
        pltpu.SemaphoreType.DMA((5,)),
        pltpu.SemaphoreType.DMA((7,)),
        pltpu.SemaphoreType.DMA((7,)),
        pltpu.SemaphoreType.DMA((9,)),
    ]
    results = pl.pallas_call(
        kernel,
        out_shape=tuple(pltpu.VMEM(*shape) for shape in shapes),
        in_specs=[hbm] * 5,
        out_specs=(pl.BlockSpec(memory_space=pltpu.VMEM),) * 4,
        scratch_shapes=scratch,
        compiler_params=pltpu.CompilerParams(
            collective_id=0, has_side_effects=True, vmem_limit_bytes=52 * 1024 * 1024
        ),
        cost_estimate=pl.CostEstimate(flops=4 * 10**9, bytes_accessed=12 * 10**6, transcendentals=3 * 10**6),
    )(*(pltpu.with_memory_space_constraint(a, pltpu.HBM) for a in operands))
    return pl.pallas_call(
        hand_on,
        out_shape=tuple(jax.ShapeDtypeStruct(*shape) for shape in shapes),
        in_specs=[pl.BlockSpec(memory_space=pltpu.VMEM)] * 4,
        out_specs=(hbm,) * 4,
        scratch_shapes=[pltpu.SemaphoreType.DMA((6,))],
        compiler_params=pltpu.CompilerParams(vmem_limit_bytes=8 * 1024 * 1024),
        cost_estimate=pl.CostEstimate(flops=0, bytes_accessed=9 * 10**6, transcendentals=0),
    )(*(pltpu.with_memory_space_constraint(a, pltpu.VMEM) for a in results))


def solution(mesh):
    rows = P("dp", ("inner", "outer"), None, None)
    return jax.shard_map(
        body,
        mesh=mesh,
        in_specs=(rows, rows, rows, P(), P()),
        out_specs=(rows, rows, P("dp", None, None), P("dp", None, None)),
        check_vma=False,
    )
```

```python
import jax
import jax.numpy as jnp
from jax import lax
from jax.experimental import pallas as pl
from jax.experimental.pallas import tpu as pltpu
from jax.sharding import PartitionSpec as P

MESH = pl.DeviceIdType.MESH
F32 = jnp.float32
BF16 = jnp.bfloat16

INNER = 64
ZH = 4
XY = 16
ROWS = 2
CHIP = 4
CG = 384
LANES = CG // 128
Q = 512
P_ALL = 256
QB = 8
BLK = CHIP * QB

BEFORE_COLS = (0, 1, 2)
AFTER_COLS = (3, 4)
AFTER_PLANE = (5,)
AFTER_Z = (6,)
AFTER_SHARES = (7,)


def gelu_value(mixed):
    return mixed * (0.5 * (1.0 + lax.erf(mixed * 0.7071067811865476)))


def gelu_slope(mixed):
    normal_cdf = 0.5 * (1.0 + lax.erf(mixed * 0.7071067811865476))
    density = jnp.exp(-0.5 * mixed * mixed) * 0.3989422804014327
    return normal_cdf + mixed * density


def wait_bytes(ref, sem):
    pltpu.make_async_copy(ref, ref, sem).wait()


def dot(a, b, ca, cb):
    return lax.dot_general(a, b, (((ca,), (cb,)), ((), ())), preferred_element_type=F32)


def kernel(
    x_h, gate_h, gout_h, rf_h, lf_h,
    gin_o, ggate_o, gr_o, gl_o,
    s1, s2, r1, r2, t1, t2, b1, b2,
    x, gate, gout, rf, lf, gin_v, ggate_v,
    wide_a, wide_b, wide_c, colsb, gmb, gcb, rt, lt,
    rs_s, rs_r, ls_s, ls_r, share, zrecv, fin,
    a_send, a_recv, m_send, m_recv, e_send, e_recv, l_sem,
):
    i = lax.axis_index("inner")
    c = lax.axis_index("outer")
    d = lax.axis_index("dp")
    zh = i % ZH
    j = i // ZH
    ys = [(j // 4 + n) % 4 for n in range(4)]
    xs = [(j % 4 + n) % 4 for n in range(4)]
    mine = pl.ds(pl.multiple_of(c * CG, CG), CG)
    theirs = pl.ds(pl.multiple_of((1 - c) * CG, CG), CG)
    my_rows = pl.ds(c * ROWS, ROWS)
    their_rows = pl.ds((1 - c) * ROWS, ROWS)

    def place(e, t, sign):
        return ys[sign * (e + t) % 4] * 4 + xs[sign * t % 4]

    def source(e, t):
        return lax.rem(ys[0] + 8 - e - t, 4) * 4 + lax.rem(xs[0] + 4 - t, 4)

    yc = [(j // 4 + n + 2 * c) % 4 for n in range(4)]
    xc = [(j % 4 + n + 2 * c) % 4 for n in range(4)]

    def along_z(n):
        n = n % 4
        dz = (1 - 2 * c) * (1 - 2 * (n % 2)) * (3 - 2 * (n // 2))
        return (zh + d + (dz + 7) // 2) % ZH

    def each_partner(e, act, first=0, last=ZH):
        def step(u, _):
            for t in range(4):
                act((yc[(e + t) % 4] * 4 + xc[t]) * ZH + along_z(t + u))
            return 0

        lax.fori_loop(first, last, step, 0)

    arrays = ((x_h, x), (gate_h, gate), (gout_h, gout))
    loads = [
        pltpu.make_async_copy(src.at[0, :, :, mine], dst.at[my_rows], l_sem.at[n])
        for n, (src, dst) in enumerate(arrays)
    ]
    loads.append(pltpu.make_async_copy(rf_h.at[c], rf, l_sem.at[3]))
    loads.append(pltpu.make_async_copy(lf_h.at[c], lf, l_sem.at[4]))
    for n in (0, 3, 1, 2, 4):
        loads[n].start()

    barrier = pltpu.get_barrier_semaphore()

    def greet(ii):
        pl.semaphore_signal(barrier, inc=1, device_id={"inner": ii, "dp": 1 - d}, device_id_type=MESH)

    pl.semaphore_signal(barrier, inc=1, device_id={"outer": 1 - c}, device_id_type=MESH)
    for e in range(4):
        each_partner(e, greet)
    for k in range(1, ZH):
        pl.semaphore_signal(
            barrier, inc=1, device_id={"inner": j * ZH + (zh + k) % ZH}, device_id_type=MESH
        )

    def greet_plane(k, _):
        pl.semaphore_signal(barrier, inc=1, device_id={"inner": lax.rem(j + k, XY) * ZH + zh}, device_id_type=MESH)
        return 0

    lax.fori_loop(1, XY, greet_plane, 0)

    def right_mix(h):
        def step(m, _):
            lhs = rf[pl.ds(pl.multiple_of(m * 128, 128), 128), :]
            parts = [dot(lhs, x[h * ROWS + p], 1, 0).reshape(16, QB, CG) for p in range(ROWS)]
            half = pl.ds(pl.multiple_of(h * 16, 16), 16)
            s1[pl.ds(m * 16, 16), half, :] = jnp.concatenate(parts, axis=1).astype(BF16)
            return 0

        lax.fori_loop(0, 4, step, 0)

    loads[0].wait()
    loads[3].wait()
    right_mix(c)

    pl.semaphore_wait(barrier, 1 + INNER + (ZH - 1) + (XY - 1))
    gifts = [
        pltpu.make_async_remote_copy(
            src_ref=src.at[0, :, :, theirs], dst_ref=dst.at[my_rows], send_sem=e_send.at[n], recv_sem=e_recv.at[n],
            device_id={"outer": 1 - c}, device_id_type=MESH,
        )
        for n, (src, dst) in enumerate(arrays)
    ]
    gifts[0].start()

    def weigh(e):
        for t in range(4):
            jj = place(e, t, 1)
            rows = pl.ds(pl.multiple_of(jj * 32, 32), 32)
            parts = []
            for p in range(CHIP):
                a = gout[p, rows, :].astype(F32)
                b = gate[p, rows, :].astype(F32)
                parts.append((a * b).reshape(4, QB, CG))
            s2[pl.ds(jj * 4, 4)] = jnp.concatenate(parts, axis=1).astype(BF16)

    def send_to(src, dst, n, sem, ii):
        pltpu.make_async_remote_copy(
            src_ref=src.at[ii], dst_ref=dst.at[i], send_sem=a_send.at[n], recv_sem=a_recv.at[sem],
            device_id={"inner": ii, "dp": 1 - d}, device_id_type=MESH,
        ).start()

    def send_chunk(src, dst, n, e, first=0, last=ZH):
        each_partner(e, lambda ii: send_to(src, dst, n, 4 * n - 3 + e, ii), first, last)

    def send_mixed(*pieces):
        for k in pieces:
            if k < 6:
                send_chunk(t1, b1, 2, k // 2, k % 2 * 2, k % 2 * 2 + 2)
            else:
                for t in (k % 2 * 2, k % 2 * 2 + 1):
                    def step(u, _):
                        send_to(t1, b1, 2, 13 + t, place(3, t, 1) * ZH + along_z(t + u))
                        return 0

                    lax.fori_loop(0, ZH, step, 0)

    def wait_chunk(n, e):
        wait_bytes(t1.at[pl.ds(0, XY)], a_recv.at[4 * n - 3 + e])

    def send_half(h):
        half = pl.ds(pl.multiple_of(h * 16, 16), 16)

        def act(ii):
            pltpu.make_async_remote_copy(
                src_ref=s1.at[ii, half], dst_ref=r1.at[i, half], send_sem=a_send.at[0], recv_sem=a_recv.at[0],
                device_id={"inner": ii, "dp": 1 - d}, device_id_type=MESH,
            ).start()

        for e in range(4):
            each_partner(e, act)

    send_half(c)
    gifts[0].wait_recv()
    gifts[1].start()
    gifts[2].start()
    right_mix(1 - c)
    send_half(1 - c)
    loads[1].wait()
    loads[2].wait()
    gifts[1].wait_recv()
    gifts[2].wait_recv()
    for e in range(4):
        weigh(e)
        send_chunk(s2, r2, 1, e)
    loads[4].wait()
    lt[...] = lf[...].astype(F32).T.astype(BF16)
    for h in range(2):
        rt[:, h * 256:(h + 1) * 256] = rf[h * 256:(h + 1) * 256, :].astype(F32).T.astype(BF16)

    def column(q):
        return jnp.concatenate([wide_a[n, pl.ds(q, P_ALL, stride=QB), :] for n in range(LANES)], axis=1)

    wait_bytes(t1, a_recv.at[0])

    def widen(m, _):
        v = r1[pl.ds(m * 4, 4)].reshape(128, CG).astype(F32)
        for n in range(LANES):
            wide_a[n, pl.ds(pl.multiple_of(m * 128, 128), 128), :] = v[:, n * 128:(n + 1) * 128]
        return 0

    lax.fori_loop(0, XY, widen, 0)
    for q in range(QB):
        xq = column(q).astype(BF16)
        colsb[q] = xq
        mixed = dot(lf[...], xq, 1, 0)
        for n in range(LANES):
            wide_b[n, pl.ds(q, P_ALL, stride=QB), :] = mixed[:, n * 128:(n + 1) * 128]

    def narrow(m, _):
        for n in range(LANES):
            v = wide_b[n, pl.ds(pl.multiple_of(m * 64, 64), 64), :].astype(BF16)
            t1[pl.ds(m * 2, 2), :, n * 128:(n + 1) * 128] = v.reshape(2, BLK, 128)
        return 0

    lax.fori_loop(0, 32, narrow, 0)
    send_mixed(*BEFORE_COLS)

    def slopes(m, _):
        rows = pl.ds(pl.multiple_of(m * 64, 64), 64)
        for n in range(LANES):
            wide_b[n, rows, :] = gelu_slope(wide_b[n, rows, :])
        return 0

    lax.fori_loop(0, 32, slopes, 0)

    for e in range(4):
        wait_chunk(1, e)
        for t in range(4):
            jj = place(e, t, -1)
            rows = pl.ds(pl.multiple_of(jj * 128, 128), 128)
            v = r2[pl.ds(jj * 4, 4)].reshape(128, CG).astype(F32)
            for n in range(LANES):
                wide_a[n, rows, :] = v[:, n * 128:(n + 1) * 128] * wide_b[n, rows, :]
    for q in range(QB):
        gmb[q] = column(q).astype(BF16)

    for e in range(4):
        spots = [place(e, t, 1) for t in range(4)]
        lhs = jnp.concatenate([lt[pl.ds(pl.multiple_of(jj * 16, 16), 16), :] for jj in spots], axis=0)
        for q in range(QB):
            v = dot(lhs, gmb[q], 1, 0)
            for t, jj in enumerate(spots):
                for n in range(LANES):
                    wide_c[n, pl.ds(jj * 128 + q, 16, stride=QB), :] = v[t * 16:(t + 1) * 16, n * 128:(n + 1) * 128]
        for jj in spots:
            rows = pl.ds(pl.multiple_of(jj * 128, 128), 128)
            for n in range(LANES):
                v = wide_c[n, rows, :].astype(BF16)
                t2[pl.ds(jj * 4, 4), :, n * 128:(n + 1) * 128] = v.reshape(4, BLK, 128)
        send_chunk(t2, b2, 3, e)
    send_mixed(*AFTER_COLS)
    gl_acc = jnp.zeros((P_ALL, P_ALL), F32)
    for q in range(QB):
        gl_acc = gl_acc + dot(gmb[q], colsb[q], 1, 1)
    ls_s[...] = gl_acc.astype(BF16).reshape(XY, 16, P_ALL)

    def scatter(src, dst, n, e):
        for t in range(1 if e == 0 else 0, 4):
            jj = place(e, t, -1)
            pltpu.make_async_remote_copy(
                src_ref=src.at[jj], dst_ref=dst.at[j], send_sem=m_send.at[n], recv_sem=m_recv.at[n],
                device_id={"inner": jj * ZH + zh}, device_id_type=MESH,
            ).start()

    for e in range(4):
        scatter(ls_s, ls_r, 0, e)
    ls_r[j] = ls_s[j]

    def hand_out(src, dst, rows, n):
        pltpu.make_async_copy(src.at[my_rows, rows], dst.at[0, :, rows, mine], l_sem.at[n]).start()
        pltpu.make_async_remote_copy(
            src_ref=src.at[their_rows, rows], dst_ref=dst.at[0, :, rows, mine],
            send_sem=e_send.at[n], recv_sem=e_recv.at[n],
            device_id={"outer": 1 - c}, device_id_type=MESH,
        ).start()

    def gate_chip(jj):
        rows = pl.ds(pl.multiple_of(jj * 32, 32), 32)
        v = b1[pl.ds(jj * 4, 4)].astype(F32)
        for p in range(CHIP):
            act = gelu_value(v[:, p * QB:(p + 1) * QB, :].reshape(32, CG))
            ggate_v[p, rows, :] = (gout[p, rows, :].astype(F32) * act).astype(BF16)
        hand_out(ggate_v, ggate_o, rows, 6)

    def gate_grad(e):
        wait_chunk(2, e)

        def step(t, _):
            gate_chip(source(e, t))
            return 0

        lax.fori_loop(0, 4, step, 0)

    gate_grad(0)

    for e in range(4):
        wait_chunk(3, e)
        spots = [place(e, t, -1) for t in range(4)]
        parts = [[] for _ in range(CHIP)]
        for jj in spots:
            rows = pl.ds(pl.multiple_of(jj * 32, 32), 32)
            v = b2[pl.ds(jj * 4, 4)].astype(F32)
            for p in range(CHIP):
                part = v[:, p * QB:(p + 1) * QB, :].reshape(32, CG).astype(BF16)
                gcb[p, rows, :] = part
                parts[p].append(part)
        total = None
        for p in range(CHIP):
            term = dot(jnp.concatenate(parts[p], axis=0), x[p], 1, 1)
            total = term if total is None else total + term
        for t, jj in enumerate(spots):
            rs_s[jj] = total[t * 32:(t + 1) * 32, :].astype(BF16)
        scatter(rs_s, rs_r, 1, e)
    rs_r[j] = rs_s[j]
    send_mixed(*AFTER_PLANE)

    def input_grad(m, _):
        rows = pl.ds(pl.multiple_of(m * 128, 128), 128)
        for p in range(CHIP):
            gin_v[p, rows, :] = dot(rt[rows, :], gcb[p], 1, 0).astype(BF16)
        hand_out(gin_v, gin_o, rows, 5)
        return 0

    lax.fori_loop(0, 4, input_grad, 0)

    wait_bytes(ls_r.at[pl.ds(0, XY - 1)], m_recv.at[0])
    wait_bytes(rs_r.at[pl.ds(0, XY - 1)], m_recv.at[1])
    gr_sum = rs_r[0].astype(F32)
    gl_sum = ls_r[0].astype(F32)
    for k in range(1, XY):
        gr_sum = gr_sum + rs_r[k].astype(F32)
        gl_sum = gl_sum + ls_r[k].astype(F32)
    share[0:32, :] = gr_sum[:, 0:256].astype(BF16)
    share[32:64, :] = gr_sum[:, 256:512].astype(BF16)
    share[64:80, :] = gl_sum.astype(BF16)

    def to_z(k):
        return pltpu.make_async_remote_copy(
            src_ref=share, dst_ref=zrecv.at[zh * 2 + d], send_sem=m_send.at[2], recv_sem=m_recv.at[2],
            device_id={"inner": j * ZH + (zh + k) % ZH, "dp": c}, device_id_type=MESH,
        )

    for k in range(1, ZH):
        to_z(k).start()

    @pl.when(d != c)
    def _():
        to_z(0).start()

    send_mixed(*AFTER_Z)
    gate_grad(1)

    @pl.when(d == c)
    def _():
        zrecv[zh * 2 + d] = share[...]
        wait_bytes(zrecv.at[pl.ds(0, 7)], m_recv.at[2])
        total = zrecv[0].astype(F32)
        for k in range(1, 8):
            total = total + zrecv[k].astype(F32)
        fin[j] = total.astype(BF16)

        for e in range(4):
            for t in range(1 if e == 0 else 0, 4):
                pltpu.make_async_remote_copy(
                    src_ref=fin.at[j], dst_ref=fin.at[j], send_sem=m_send.at[3], recv_sem=m_recv.at[3 + e],
                    device_id={"inner": place(e, t, 1) * ZH + zh}, device_id_type=MESH,
                ).start()

    send_mixed(*AFTER_SHARES)
    gate_grad(2)

    def last_gate(t):
        wait_bytes(t1.at[pl.ds(0, ZH)], a_recv.at[13 + t])
        gate_chip(place(3, t, -1))

    def unpack():
        for k in range(XY):
            gr_o[0, k * 32:(k + 1) * 32, 0:256] = fin[k, 0:32, :].astype(F32)
            gr_o[0, k * 32:(k + 1) * 32, 256:512] = fin[k, 32:64, :].astype(F32)
            gl_o[0, k * 16:(k + 1) * 16, :] = fin[k, 64:80, :].astype(F32)

    last_gate(0)
    last_gate(1)

    @pl.when(d == c)
    def _():
        for e in range(4):
            wait_bytes(fin.at[pl.ds(0, 3 if e == 0 else 4)], m_recv.at[3 + e])
            for t in range(4):
                jj = place(e, t, -1)
                pltpu.make_async_remote_copy(
                    src_ref=fin.at[jj], dst_ref=fin.at[jj], send_sem=m_send.at[4], recv_sem=m_recv.at[7],
                    device_id={"outer": 1 - c}, device_id_type=MESH,
                ).start()
        unpack()

    last_gate(2)
    last_gate(3)

    @pl.when(d == c)
    def _():
        wait_bytes(fin.at[pl.ds(0, XY - 1)], m_send.at[3])
        wait_bytes(zrecv.at[pl.ds(0, 3)], m_send.at[2])
        wait_bytes(fin, m_send.at[4])

    @pl.when(d != c)
    def _():
        wait_bytes(zrecv.at[pl.ds(0, 4)], m_send.at[2])
        wait_bytes(fin, m_recv.at[7])
        unpack()

    for n in range(4):
        wait_bytes(t1, a_send.at[n])
    wait_bytes(ls_r.at[pl.ds(0, XY - 1)], m_send.at[0])
    wait_bytes(rs_r.at[pl.ds(0, XY - 1)], m_send.at[1])
    for gift in gifts:
        gift.wait_send()
    half = ggate_v.at[pl.ds(0, ROWS)]
    for n in (5, 6):
        wait_bytes(half, l_sem.at[n])
        wait_bytes(half, e_send.at[n])
        wait_bytes(half, e_recv.at[n])


def hand_on(*refs):
    results, outputs, sem = refs[:4], refs[4:8], refs[8]
    parts = []
    for src, dst in zip(results[:2], outputs[:2]):
        for p in range(ROWS):
            parts.append((src.at[0, p], dst.at[0, p]))
    parts.extend(zip(results[2:], outputs[2:]))
    copies = [pltpu.make_async_copy(src, dst, sem.at[n]) for n, (src, dst) in enumerate(parts)]
    for copy in copies:
        copy.start()
    for copy in copies:
        copy.wait()


def body(*operands):
    hbm = pl.BlockSpec(memory_space=pl.ANY)
    shapes = (
        ((1, ROWS, Q, 2 * CG), BF16),
        ((1, ROWS, Q, 2 * CG), BF16),
        ((1, Q, Q), F32),
        ((1, P_ALL, P_ALL), F32),
    )
    blocks = pltpu.VMEM((INNER, BLK, CG), BF16)
    rows = pltpu.VMEM((CHIP, Q, CG), BF16)
    wide = pltpu.VMEM((LANES, INNER * BLK, 128), F32)
    columns = pltpu.VMEM((QB, P_ALL, CG), BF16)
    scratch = [blocks] * 8 + [
        rows, rows, rows,
        pltpu.VMEM((Q, Q), BF16),
        pltpu.VMEM((P_ALL, P_ALL), BF16),
        rows, rows,
        wide, wide, wide,
        columns, columns,
        rows,
        pltpu.VMEM((Q, Q), BF16),
        pltpu.VMEM((P_ALL, P_ALL), BF16),
        pltpu.VMEM((XY, 32, Q), BF16),
        pltpu.VMEM((XY, 32, Q), BF16),
        pltpu.VMEM((XY, 16, P_ALL), BF16),
        pltpu.VMEM((XY, 16, P_ALL), BF16),
        pltpu.VMEM((80, 256), BF16),
        pltpu.VMEM((8, 80, 256), BF16),
        pltpu.VMEM((XY, 80, 256), BF16),
        pltpu.SemaphoreType.DMA((4,)),
        pltpu.SemaphoreType.DMA((17,)),
        pltpu.SemaphoreType.DMA((5,)),
        pltpu.SemaphoreType.DMA((8,)),
        pltpu.SemaphoreType.DMA((7,)),
        pltpu.SemaphoreType.DMA((7,)),
        pltpu.SemaphoreType.DMA((9,)),
    ]
    results = pl.pallas_call(
        kernel,
        out_shape=tuple(pltpu.VMEM(*shape) for shape in shapes),
        in_specs=[hbm] * 5,
        out_specs=(pl.BlockSpec(memory_space=pltpu.VMEM),) * 4,
        scratch_shapes=scratch,
        compiler_params=pltpu.CompilerParams(
            collective_id=0, has_side_effects=True, vmem_limit_bytes=52 * 1024 * 1024
        ),
        cost_estimate=pl.CostEstimate(flops=4 * 10**9, bytes_accessed=12 * 10**6, transcendentals=3 * 10**6),
    )(*(pltpu.with_memory_space_constraint(a, pltpu.HBM) for a in operands))
    return pl.pallas_call(
        hand_on,
        out_shape=tuple(jax.ShapeDtypeStruct(*shape) for shape in shapes),
        in_specs=[pl.BlockSpec(memory_space=pltpu.VMEM)] * 4,
        out_specs=(hbm,) * 4,
        scratch_shapes=[pltpu.SemaphoreType.DMA((6,))],
        compiler_params=pltpu.CompilerParams(vmem_limit_bytes=8 * 1024 * 1024),
        cost_estimate=pl.CostEstimate(flops=0, bytes_accessed=9 * 10**6, transcendentals=0),
    )(*(pltpu.with_memory_space_constraint(a, pltpu.VMEM) for a in results))


def solution(mesh):
    rows = P("dp", ("inner", "outer"), None, None)
    return jax.shard_map(
        body,
        mesh=mesh,
        in_specs=(rows, rows, rows, P(), P()),
        out_specs=(rows, rows, P("dp", None, None), P("dp", None, None)),
        check_vma=False,
    )
```

```python
import jax
import jax.numpy as jnp
from jax import lax
from jax.experimental import pallas as pl
from jax.experimental.pallas import tpu as pltpu
from jax.sharding import PartitionSpec as P

MESH = pl.DeviceIdType.MESH
F32 = jnp.float32
BF16 = jnp.bfloat16

INNER = 64
ZH = 4
XY = 16
ROWS = 2
CHIP = 4
CG = 384
LANES = CG // 128
Q = 512
P_ALL = 256
QB = 8
BLK = CHIP * QB

BEFORE_COLS = (0, 1, 2)
AMID_COLS = (3,)
AFTER_PLANE = (4,)
AFTER_Z = (5, 6)
AFTER_SHARES = (7,)


def gelu_value(mixed):
    return mixed * (0.5 * (1.0 + lax.erf(mixed * 0.7071067811865476)))


def gelu_slope(mixed):
    normal_cdf = 0.5 * (1.0 + lax.erf(mixed * 0.7071067811865476))
    density = jnp.exp(-0.5 * mixed * mixed) * 0.3989422804014327
    return normal_cdf + mixed * density


def wait_bytes(ref, sem):
    pltpu.make_async_copy(ref, ref, sem).wait()


def dot(a, b, ca, cb):
    return lax.dot_general(a, b, (((ca,), (cb,)), ((), ())), preferred_element_type=F32)


def kernel(
    x_h, gate_h, gout_h, rf_h, lf_h,
    gin_o, ggate_o, gr_o, gl_o,
    s1, s2, r1, r2, t1, t2, b1, b2,
    x, gate, gout, rf, lf, gin_v, ggate_v,
    wide_a, wide_b, wide_c, colsb, gmb, gcb, rt, lt,
    rs_s, rs_r, ls_s, ls_r, share, pair, zrecv, fin,
    a_send, a_recv, m_send, m_recv, e_send, e_recv, l_sem,
):
    i = lax.axis_index("inner")
    c = lax.axis_index("outer")
    d = lax.axis_index("dp")
    zh = i % ZH
    j = i // ZH
    ys = [(j // 4 + n) % 4 for n in range(4)]
    xs = [(j % 4 + n) % 4 for n in range(4)]
    mine = pl.ds(pl.multiple_of(c * CG, CG), CG)
    theirs = pl.ds(pl.multiple_of((1 - c) * CG, CG), CG)
    my_rows = pl.ds(c * ROWS, ROWS)
    their_rows = pl.ds((1 - c) * ROWS, ROWS)

    def place(e, t, sign):
        return ys[sign * (e + t) % 4] * 4 + xs[sign * t % 4]

    def source(e, t):
        return lax.rem(ys[0] + 8 - e - t, 4) * 4 + lax.rem(xs[0] + 4 - t, 4)

    yc = [(j // 4 + n + 2 * c) % 4 for n in range(4)]
    xc = [(j % 4 + n + 2 * c) % 4 for n in range(4)]

    def along_z(n):
        n = n % 4
        dz = (1 - 2 * c) * (1 - 2 * (n % 2)) * (3 - 2 * (n // 2))
        return (zh + d + (dz + 7) // 2) % ZH

    def each_partner(e, act, first=0, last=ZH):
        def step(u, _):
            for t in range(4):
                act((yc[(e + t) % 4] * 4 + xc[t]) * ZH + along_z(t + u))
            return 0

        lax.fori_loop(first, last, step, 0)

    arrays = ((x_h, x), (gate_h, gate), (gout_h, gout))
    loads = [
        pltpu.make_async_copy(src.at[0, :, :, mine], dst.at[my_rows], l_sem.at[n])
        for n, (src, dst) in enumerate(arrays)
    ]
    loads.append(pltpu.make_async_copy(rf_h.at[c], rf, l_sem.at[3]))
    loads.append(pltpu.make_async_copy(lf_h.at[c], lf, l_sem.at[4]))
    for n in (0, 3, 1, 2, 4):
        loads[n].start()

    barrier = pltpu.get_barrier_semaphore()

    def greet(ii):
        pl.semaphore_signal(barrier, inc=1, device_id={"inner": ii, "dp": 1 - d}, device_id_type=MESH)

    pl.semaphore_signal(barrier, inc=1, device_id={"outer": 1 - c}, device_id_type=MESH)
    for e in range(4):
        each_partner(e, greet)
    for k in range(1, ZH):
        pl.semaphore_signal(
            barrier, inc=1, device_id={"inner": j * ZH + (zh + k) % ZH}, device_id_type=MESH
        )

    def greet_plane(k, _):
        pl.semaphore_signal(barrier, inc=1, device_id={"inner": lax.rem(j + k, XY) * ZH + zh}, device_id_type=MESH)
        return 0

    lax.fori_loop(1, XY, greet_plane, 0)

    def right_mix(h):
        def step(m, _):
            lhs = rf[pl.ds(pl.multiple_of(m * 128, 128), 128), :]
            parts = [dot(lhs, x[h * ROWS + p], 1, 0).reshape(16, QB, CG) for p in range(ROWS)]
            half = pl.ds(pl.multiple_of(h * 16, 16), 16)
            s1[pl.ds(m * 16, 16), half, :] = jnp.concatenate(parts, axis=1).astype(BF16)
            return 0

        lax.fori_loop(0, 4, step, 0)

    loads[0].wait()
    loads[3].wait()
    right_mix(c)

    pl.semaphore_wait(barrier, 1 + INNER + (ZH - 1) + (XY - 1))
    gifts = [
        pltpu.make_async_remote_copy(
            src_ref=src.at[0, :, :, theirs], dst_ref=dst.at[my_rows], send_sem=e_send.at[n], recv_sem=e_recv.at[n],
            device_id={"outer": 1 - c}, device_id_type=MESH,
        )
        for n, (src, dst) in enumerate(arrays)
    ]
    gifts[0].start()

    def weigh(e):
        for t in range(4):
            jj = place(e, t, 1)
            rows = pl.ds(pl.multiple_of(jj * 32, 32), 32)
            parts = []
            for p in range(CHIP):
                a = gout[p, rows, :].astype(F32)
                b = gate[p, rows, :].astype(F32)
                parts.append((a * b).reshape(4, QB, CG))
            s2[pl.ds(jj * 4, 4)] = jnp.concatenate(parts, axis=1).astype(BF16)

    def send_to(src, dst, n, sem, ii):
        pltpu.make_async_remote_copy(
            src_ref=src.at[ii], dst_ref=dst.at[i], send_sem=a_send.at[n], recv_sem=a_recv.at[sem],
            device_id={"inner": ii, "dp": 1 - d}, device_id_type=MESH,
        ).start()

    def send_chunk(src, dst, n, e, first=0, last=ZH):
        each_partner(e, lambda ii: send_to(src, dst, n, 4 * n - 3 + e, ii), first, last)

    def send_mixed(*pieces):
        for k in pieces:
            if k < 6:
                send_chunk(t1, b1, 2, k // 2, k % 2 * 2, k % 2 * 2 + 2)
            else:
                for t in (k % 2 * 2, k % 2 * 2 + 1):
                    def step(u, _):
                        send_to(t1, b1, 2, 13 + t, place(3, t, 1) * ZH + along_z(t + u))
                        return 0

                    lax.fori_loop(0, ZH, step, 0)

    def wait_chunk(n, e):
        wait_bytes(t1.at[pl.ds(0, XY)], a_recv.at[4 * n - 3 + e])

    def send_half(h):
        half = pl.ds(pl.multiple_of(h * 16, 16), 16)

        def act(ii):
            pltpu.make_async_remote_copy(
                src_ref=s1.at[ii, half], dst_ref=r1.at[i, half], send_sem=a_send.at[0], recv_sem=a_recv.at[0],
                device_id={"inner": ii, "dp": 1 - d}, device_id_type=MESH,
            ).start()

        for e in range(4):
            each_partner(e, act)

    send_half(c)
    gifts[0].wait_recv()
    gifts[1].start()
    gifts[2].start()
    right_mix(1 - c)
    send_half(1 - c)
    loads[1].wait()
    loads[2].wait()
    gifts[1].wait_recv()
    gifts[2].wait_recv()
    for e in range(4):
        weigh(e)
        send_chunk(s2, r2, 1, e)
    loads[4].wait()
    lt[...] = lf[...].astype(F32).T.astype(BF16)
    for h in range(2):
        rt[:, h * 256:(h + 1) * 256] = rf[h * 256:(h + 1) * 256, :].astype(F32).T.astype(BF16)

    def column(q):
        return jnp.concatenate([wide_a[n, pl.ds(q, P_ALL, stride=QB), :] for n in range(LANES)], axis=1)

    wait_bytes(t1, a_recv.at[0])

    def widen(m, _):
        v = r1[pl.ds(m * 4, 4)].reshape(128, CG).astype(F32)
        for n in range(LANES):
            wide_a[n, pl.ds(pl.multiple_of(m * 128, 128), 128), :] = v[:, n * 128:(n + 1) * 128]
        return 0

    lax.fori_loop(0, XY, widen, 0)
    for q in range(QB):
        xq = column(q).astype(BF16)
        colsb[q] = xq
        mixed = dot(lf[...], xq, 1, 0)
        for n in range(LANES):
            wide_b[n, pl.ds(q, P_ALL, stride=QB), :] = mixed[:, n * 128:(n + 1) * 128]

    def narrow(m, _):
        for n in range(LANES):
            v = wide_b[n, pl.ds(pl.multiple_of(m * 64, 64), 64), :].astype(BF16)
            t1[pl.ds(m * 2, 2), :, n * 128:(n + 1) * 128] = v.reshape(2, BLK, 128)
        return 0

    lax.fori_loop(0, 32, narrow, 0)
    send_mixed(*BEFORE_COLS)

    def slopes(m, _):
        rows = pl.ds(pl.multiple_of(m * 64, 64), 64)
        for n in range(LANES):
            wide_b[n, rows, :] = gelu_slope(wide_b[n, rows, :])
        return 0

    lax.fori_loop(0, 32, slopes, 0)

    for e in range(4):
        wait_chunk(1, e)
        for t in range(4):
            jj = place(e, t, -1)
            rows = pl.ds(pl.multiple_of(jj * 128, 128), 128)
            v = r2[pl.ds(jj * 4, 4)].reshape(128, CG).astype(F32)
            for n in range(LANES):
                wide_a[n, rows, :] = v[:, n * 128:(n + 1) * 128] * wide_b[n, rows, :]
    for q in range(QB):
        gmb[q] = column(q).astype(BF16)

    for e in range(4):
        spots = [place(e, t, 1) for t in range(4)]
        lhs = jnp.concatenate([lt[pl.ds(pl.multiple_of(jj * 16, 16), 16), :] for jj in spots], axis=0)
        for q in range(QB):
            v = dot(lhs, gmb[q], 1, 0)
            for t, jj in enumerate(spots):
                for n in range(LANES):
                    wide_c[n, pl.ds(jj * 128 + q, 16, stride=QB), :] = v[t * 16:(t + 1) * 16, n * 128:(n + 1) * 128]
        for jj in spots:
            rows = pl.ds(pl.multiple_of(jj * 128, 128), 128)
            for n in range(LANES):
                v = wide_c[n, rows, :].astype(BF16)
                t2[pl.ds(jj * 4, 4), :, n * 128:(n + 1) * 128] = v.reshape(4, BLK, 128)
        send_chunk(t2, b2, 3, e)
    gl_acc = jnp.zeros((P_ALL, P_ALL), F32)
    for q in range(QB):
        gl_acc = gl_acc + dot(gmb[q], colsb[q], 1, 1)
    ls_s[...] = gl_acc.astype(BF16).reshape(XY, 16, P_ALL)

    def scatter(src, dst, n, e):
        for t in range(1 if e == 0 else 0, 4):
            jj = place(e, t, -1)
            pltpu.make_async_remote_copy(
                src_ref=src.at[jj], dst_ref=dst.at[j], send_sem=m_send.at[n], recv_sem=m_recv.at[n],
                device_id={"inner": jj * ZH + zh}, device_id_type=MESH,
            ).start()

    for e in range(4):
        scatter(ls_s, ls_r, 0, e)
    ls_r[j] = ls_s[j]

    def hand_out(src, dst, rows, n):
        pltpu.make_async_copy(src.at[my_rows, rows], dst.at[0, :, rows, mine], l_sem.at[n]).start()
        pltpu.make_async_remote_copy(
            src_ref=src.at[their_rows, rows], dst_ref=dst.at[0, :, rows, mine],
            send_sem=e_send.at[n], recv_sem=e_recv.at[n],
            device_id={"outer": 1 - c}, device_id_type=MESH,
        ).start()

    def gate_chip(jj):
        rows = pl.ds(pl.multiple_of(jj * 32, 32), 32)
        v = b1[pl.ds(jj * 4, 4)].astype(F32)
        for p in range(CHIP):
            act = gelu_value(v[:, p * QB:(p + 1) * QB, :].reshape(32, CG))
            ggate_v[p, rows, :] = (gout[p, rows, :].astype(F32) * act).astype(BF16)
        hand_out(ggate_v, ggate_o, rows, 6)

    def gate_grad(e):
        wait_chunk(2, e)

        def step(t, _):
            gate_chip(source(e, t))
            return 0

        lax.fori_loop(0, 4, step, 0)

    gate_grad(0)

    for e in range(4):
        wait_chunk(3, e)
        spots = [place(e, t, -1) for t in range(4)]
        parts = [[] for _ in range(CHIP)]
        for jj in spots:
            rows = pl.ds(pl.multiple_of(jj * 32, 32), 32)
            v = b2[pl.ds(jj * 4, 4)].astype(F32)
            for p in range(CHIP):
                part = v[:, p * QB:(p + 1) * QB, :].reshape(32, CG).astype(BF16)
                gcb[p, rows, :] = part
                parts[p].append(part)
        total = None
        for p in range(CHIP):
            term = dot(jnp.concatenate(parts[p], axis=0), x[p], 1, 1)
            total = term if total is None else total + term
        for t, jj in enumerate(spots):
            rs_s[jj] = total[t * 32:(t + 1) * 32, :].astype(BF16)
        scatter(rs_s, rs_r, 1, e)
        if e == 1:
            send_mixed(*AMID_COLS)
    rs_r[j] = rs_s[j]
    send_mixed(*AFTER_PLANE)

    def input_grad(m, _):
        rows = pl.ds(pl.multiple_of(m * 128, 128), 128)
        for p in range(CHIP):
            gin_v[p, rows, :] = dot(rt[rows, :], gcb[p], 1, 0).astype(BF16)
        hand_out(gin_v, gin_o, rows, 5)
        return 0

    lax.fori_loop(0, 4, input_grad, 0)

    wait_bytes(ls_r.at[pl.ds(0, XY - 1)], m_recv.at[0])
    wait_bytes(rs_r.at[pl.ds(0, XY - 1)], m_recv.at[1])
    gr_sum = rs_r[0].astype(F32)
    gl_sum = ls_r[0].astype(F32)
    for k in range(1, XY):
        gr_sum = gr_sum + rs_r[k].astype(F32)
        gl_sum = gl_sum + ls_r[k].astype(F32)
    share[0:32, :] = gr_sum[:, 0:256].astype(BF16)
    share[32:64, :] = gr_sum[:, 256:512].astype(BF16)
    share[64:80, :] = gl_sum.astype(BF16)

    @pl.when(d != c)
    def _():
        pltpu.make_async_remote_copy(
            src_ref=share, dst_ref=pair, send_sem=m_send.at[2], recv_sem=m_recv.at[2],
            device_id={"dp": c}, device_id_type=MESH,
        ).start()

    send_mixed(*AFTER_Z)

    @pl.when(d == c)
    def _():
        wait_bytes(pair, m_recv.at[2])
        zrecv[zh] = (share[...].astype(F32) + pair[...].astype(F32)).astype(BF16)
        for k in range(1, ZH):
            pltpu.make_async_remote_copy(
                src_ref=zrecv.at[zh], dst_ref=zrecv.at[zh], send_sem=m_send.at[5], recv_sem=m_recv.at[8],
                device_id={"inner": j * ZH + (zh + k) % ZH}, device_id_type=MESH,
            ).start()

    gate_grad(1)

    @pl.when(d == c)
    def _():
        wait_bytes(zrecv.at[pl.ds(0, ZH - 1)], m_recv.at[8])
        total = zrecv[0].astype(F32)
        for k in range(1, ZH):
            total = total + zrecv[k].astype(F32)
        fin[j] = total.astype(BF16)
        for e in range(4):
            for t in range(1 if e == 0 else 0, 4):
                pltpu.make_async_remote_copy(
                    src_ref=fin.at[j], dst_ref=fin.at[j], send_sem=m_send.at[3], recv_sem=m_recv.at[3 + e],
                    device_id={"inner": place(e, t, 1) * ZH + zh}, device_id_type=MESH,
                ).start()

    send_mixed(*AFTER_SHARES)
    gate_grad(2)

    def last_gate(t):
        wait_bytes(t1.at[pl.ds(0, ZH)], a_recv.at[13 + t])
        gate_chip(place(3, t, -1))

    def unpack():
        for k in range(XY):
            gr_o[0, k * 32:(k + 1) * 32, 0:256] = fin[k, 0:32, :].astype(F32)
            gr_o[0, k * 32:(k + 1) * 32, 256:512] = fin[k, 32:64, :].astype(F32)
            gl_o[0, k * 16:(k + 1) * 16, :] = fin[k, 64:80, :].astype(F32)

    last_gate(0)
    last_gate(1)

    @pl.when(d == c)
    def _():
        for e in range(4):
            wait_bytes(fin.at[pl.ds(0, 3 if e == 0 else 4)], m_recv.at[3 + e])
            for t in range(4):
                jj = place(e, t, -1)
                pltpu.make_async_remote_copy(
                    src_ref=fin.at[jj], dst_ref=fin.at[jj], send_sem=m_send.at[4], recv_sem=m_recv.at[7],
                    device_id={"outer": 1 - c}, device_id_type=MESH,
                ).start()
        unpack()

    last_gate(2)
    last_gate(3)

    @pl.when(d == c)
    def _():
        wait_bytes(fin.at[pl.ds(0, XY - 1)], m_send.at[3])
        wait_bytes(zrecv.at[pl.ds(0, 3)], m_send.at[5])
        wait_bytes(fin, m_send.at[4])

    @pl.when(d != c)
    def _():
        wait_bytes(share, m_send.at[2])
        wait_bytes(fin, m_recv.at[7])
        unpack()

    for n in range(4):
        wait_bytes(t1, a_send.at[n])
    wait_bytes(ls_r.at[pl.ds(0, XY - 1)], m_send.at[0])
    wait_bytes(rs_r.at[pl.ds(0, XY - 1)], m_send.at[1])
    for gift in gifts:
        gift.wait_send()
    half = ggate_v.at[pl.ds(0, ROWS)]
    for n in (5, 6):
        wait_bytes(half, l_sem.at[n])
        wait_bytes(half, e_send.at[n])
        wait_bytes(half, e_recv.at[n])


def hand_on(*refs):
    results, outputs, sem = refs[:4], refs[4:8], refs[8]
    parts = []
    for src, dst in zip(results[:2], outputs[:2]):
        for p in range(ROWS):
            parts.append((src.at[0, p], dst.at[0, p]))
    parts.extend(zip(results[2:], outputs[2:]))
    copies = [pltpu.make_async_copy(src, dst, sem.at[n]) for n, (src, dst) in enumerate(parts)]
    for copy in copies:
        copy.start()
    for copy in copies:
        copy.wait()


def body(*operands):
    hbm = pl.BlockSpec(memory_space=pl.ANY)
    shapes = (
        ((1, ROWS, Q, 2 * CG), BF16),
        ((1, ROWS, Q, 2 * CG), BF16),
        ((1, Q, Q), F32),
        ((1, P_ALL, P_ALL), F32),
    )
    blocks = pltpu.VMEM((INNER, BLK, CG), BF16)
    rows = pltpu.VMEM((CHIP, Q, CG), BF16)
    wide = pltpu.VMEM((LANES, INNER * BLK, 128), F32)
    columns = pltpu.VMEM((QB, P_ALL, CG), BF16)
    scratch = [blocks] * 8 + [
        rows, rows, rows,
        pltpu.VMEM((Q, Q), BF16),
        pltpu.VMEM((P_ALL, P_ALL), BF16),
        rows, rows,
        wide, wide, wide,
        columns, columns,
        rows,
        pltpu.VMEM((Q, Q), BF16),
        pltpu.VMEM((P_ALL, P_ALL), BF16),
        pltpu.VMEM((XY, 32, Q), BF16),
        pltpu.VMEM((XY, 32, Q), BF16),
        pltpu.VMEM((XY, 16, P_ALL), BF16),
        pltpu.VMEM((XY, 16, P_ALL), BF16),
        pltpu.VMEM((80, 256), BF16),
        pltpu.VMEM((80, 256), BF16),
        pltpu.VMEM((ZH, 80, 256), BF16),
        pltpu.VMEM((XY, 80, 256), BF16),
        pltpu.SemaphoreType.DMA((4,)),
        pltpu.SemaphoreType.DMA((17,)),
        pltpu.SemaphoreType.DMA((6,)),
        pltpu.SemaphoreType.DMA((9,)),
        pltpu.SemaphoreType.DMA((7,)),
        pltpu.SemaphoreType.DMA((7,)),
        pltpu.SemaphoreType.DMA((9,)),
    ]
    results = pl.pallas_call(
        kernel,
        out_shape=tuple(pltpu.VMEM(*shape) for shape in shapes),
        in_specs=[hbm] * 5,
        out_specs=(pl.BlockSpec(memory_space=pltpu.VMEM),) * 4,
        scratch_shapes=scratch,
        compiler_params=pltpu.CompilerParams(
            collective_id=0, has_side_effects=True, vmem_limit_bytes=52 * 1024 * 1024
        ),
        cost_estimate=pl.CostEstimate(flops=4 * 10**9, bytes_accessed=12 * 10**6, transcendentals=3 * 10**6),
    )(*(pltpu.with_memory_space_constraint(a, pltpu.HBM) for a in operands))
    return pl.pallas_call(
        hand_on,
        out_shape=tuple(jax.ShapeDtypeStruct(*shape) for shape in shapes),
        in_specs=[pl.BlockSpec(memory_space=pltpu.VMEM)] * 4,
        out_specs=(hbm,) * 4,
        scratch_shapes=[pltpu.SemaphoreType.DMA((6,))],
        compiler_params=pltpu.CompilerParams(vmem_limit_bytes=8 * 1024 * 1024),
        cost_estimate=pl.CostEstimate(flops=0, bytes_accessed=9 * 10**6, transcendentals=0),
    )(*(pltpu.with_memory_space_constraint(a, pltpu.VMEM) for a in results))


def solution(mesh):
    rows = P("dp", ("inner", "outer"), None, None)
    return jax.shard_map(
        body,
        mesh=mesh,
        in_specs=(rows, rows, rows, P(), P()),
        out_specs=(rows, rows, P("dp", None, None), P("dp", None, None)),
        check_vma=False,
    )
```

```python
import jax
import jax.numpy as jnp
from jax import lax
from jax.experimental import pallas as pl
from jax.experimental.pallas import tpu as pltpu
from jax.sharding import PartitionSpec as P

MESH = pl.DeviceIdType.MESH
F32 = jnp.float32
BF16 = jnp.bfloat16

INNER = 64
ZH = 4
XY = 16
ROWS = 2
CHIP = 4
CG = 384
LANES = CG // 128
Q = 512
P_ALL = 256
QB = 8
BLK = CHIP * QB

BEFORE_COLS = (0, 1, 2)
AFTER_COLS = (3,)
AFTER_PLANE = (4,)
AFTER_PAIR = (5,)
AFTER_Z = (6,)
AFTER_SHARES = (7,)


def gelu_value(mixed):
    return mixed * (0.5 * (1.0 + lax.erf(mixed * 0.7071067811865476)))


def gelu_slope(mixed):
    normal_cdf = 0.5 * (1.0 + lax.erf(mixed * 0.7071067811865476))
    density = jnp.exp(-0.5 * mixed * mixed) * 0.3989422804014327
    return normal_cdf + mixed * density


def wait_bytes(ref, sem):
    pltpu.make_async_copy(ref, ref, sem).wait()


def dot(a, b, ca, cb):
    return lax.dot_general(a, b, (((ca,), (cb,)), ((), ())), preferred_element_type=F32)


def kernel(
    x_h, gate_h, gout_h, rf_h, lf_h,
    gin_o, ggate_o, gr_o, gl_o,
    s1, s2, r1, r2, t1, t2, b1, b2,
    x, gate, gout, rf, lf, gin_v, ggate_v,
    wide_a, wide_b, wide_c, colsb, gmb, gcb, rt, lt,
    rs_s, rs_r, ls_s, ls_r, share, pair, zrecv, fin,
    a_send, a_recv, m_send, m_recv, e_send, e_recv, l_sem,
):
    i = lax.axis_index("inner")
    c = lax.axis_index("outer")
    d = lax.axis_index("dp")
    zh = i % ZH
    j = i // ZH
    ys = [(j // 4 + n) % 4 for n in range(4)]
    xs = [(j % 4 + n) % 4 for n in range(4)]
    mine = pl.ds(pl.multiple_of(c * CG, CG), CG)
    theirs = pl.ds(pl.multiple_of((1 - c) * CG, CG), CG)
    my_rows = pl.ds(c * ROWS, ROWS)
    their_rows = pl.ds((1 - c) * ROWS, ROWS)

    def place(e, t, sign):
        return ys[sign * (e + t) % 4] * 4 + xs[sign * t % 4]

    def source(e, t):
        return lax.rem(ys[0] + 8 - e - t, 4) * 4 + lax.rem(xs[0] + 4 - t, 4)

    yc = [(j // 4 + n + 2 * c) % 4 for n in range(4)]
    xc = [(j % 4 + n + 2 * c) % 4 for n in range(4)]

    def along_z(n):
        n = n % 4
        dz = (1 - 2 * c) * (1 - 2 * (n % 2)) * (3 - 2 * (n // 2))
        return (zh + d + (dz + 7) // 2) % ZH

    def each_partner(e, act, first=0, last=ZH):
        def step(u, _):
            for t in range(4):
                act((yc[(e + t) % 4] * 4 + xc[t]) * ZH + along_z(t + u))
            return 0

        lax.fori_loop(first, last, step, 0)

    arrays = ((x_h, x), (gate_h, gate), (gout_h, gout))
    loads = [
        pltpu.make_async_copy(src.at[0, :, :, mine], dst.at[my_rows], l_sem.at[n])
        for n, (src, dst) in enumerate(arrays)
    ]
    loads.append(pltpu.make_async_copy(rf_h.at[c], rf, l_sem.at[3]))
    loads.append(pltpu.make_async_copy(lf_h.at[c], lf, l_sem.at[4]))
    for n in (0, 3, 1, 2, 4):
        loads[n].start()

    barrier = pltpu.get_barrier_semaphore()

    def greet(ii):
        pl.semaphore_signal(barrier, inc=1, device_id={"inner": ii, "dp": 1 - d}, device_id_type=MESH)

    pl.semaphore_signal(barrier, inc=1, device_id={"outer": 1 - c}, device_id_type=MESH)
    for e in range(4):
        each_partner(e, greet)
    for k in range(1, ZH):
        pl.semaphore_signal(
            barrier, inc=1, device_id={"inner": j * ZH + (zh + k) % ZH}, device_id_type=MESH
        )

    def greet_plane(k, _):
        pl.semaphore_signal(barrier, inc=1, device_id={"inner": lax.rem(j + k, XY) * ZH + zh}, device_id_type=MESH)
        return 0

    lax.fori_loop(1, XY, greet_plane, 0)

    def right_mix(h):
        def step(m, _):
            lhs = rf[pl.ds(pl.multiple_of(m * 128, 128), 128), :]
            parts = [dot(lhs, x[h * ROWS + p], 1, 0).reshape(16, QB, CG) for p in range(ROWS)]
            half = pl.ds(pl.multiple_of(h * 16, 16), 16)
            s1[pl.ds(m * 16, 16), half, :] = jnp.concatenate(parts, axis=1).astype(BF16)
            return 0

        lax.fori_loop(0, 4, step, 0)

    loads[0].wait()
    loads[3].wait()
    right_mix(c)

    pl.semaphore_wait(barrier, 1 + INNER + (ZH - 1) + (XY - 1))
    gifts = [
        pltpu.make_async_remote_copy(
            src_ref=src.at[0, :, :, theirs], dst_ref=dst.at[my_rows], send_sem=e_send.at[n], recv_sem=e_recv.at[n],
            device_id={"outer": 1 - c}, device_id_type=MESH,
        )
        for n, (src, dst) in enumerate(arrays)
    ]
    gifts[0].start()

    def weigh(e):
        for t in range(4):
            jj = place(e, t, 1)
            rows = pl.ds(pl.multiple_of(jj * 32, 32), 32)
            parts = []
            for p in range(CHIP):
                a = gout[p, rows, :].astype(F32)
                b = gate[p, rows, :].astype(F32)
                parts.append((a * b).reshape(4, QB, CG))
            s2[pl.ds(jj * 4, 4)] = jnp.concatenate(parts, axis=1).astype(BF16)

    def send_to(src, dst, n, sem, ii):
        pltpu.make_async_remote_copy(
            src_ref=src.at[ii], dst_ref=dst.at[i], send_sem=a_send.at[n], recv_sem=a_recv.at[sem],
            device_id={"inner": ii, "dp": 1 - d}, device_id_type=MESH,
        ).start()

    def send_chunk(src, dst, n, e, first=0, last=ZH):
        each_partner(e, lambda ii: send_to(src, dst, n, 4 * n - 3 + e, ii), first, last)

    def send_mixed(*pieces):
        for k in pieces:
            if k < 6:
                send_chunk(t1, b1, 2, k // 2, k % 2 * 2, k % 2 * 2 + 2)
            else:
                for t in (k % 2 * 2, k % 2 * 2 + 1):
                    def step(u, _):
                        send_to(t1, b1, 2, 13 + t, place(3, t, 1) * ZH + along_z(t + u))
                        return 0

                    lax.fori_loop(0, ZH, step, 0)

    def wait_chunk(n, e):
        wait_bytes(t1.at[pl.ds(0, XY)], a_recv.at[4 * n - 3 + e])

    def send_half(h):
        half = pl.ds(pl.multiple_of(h * 16, 16), 16)

        def act(ii):
            pltpu.make_async_remote_copy(
                src_ref=s1.at[ii, half], dst_ref=r1.at[i, half], send_sem=a_send.at[0], recv_sem=a_recv.at[0],
                device_id={"inner": ii, "dp": 1 - d}, device_id_type=MESH,
            ).start()

        for e in range(4):
            each_partner(e, act)

    send_half(c)
    gifts[0].wait_recv()
    gifts[1].start()
    gifts[2].start()
    right_mix(1 - c)
    send_half(1 - c)
    loads[1].wait()
    loads[2].wait()
    gifts[1].wait_recv()
    gifts[2].wait_recv()
    for e in range(4):
        weigh(e)
        send_chunk(s2, r2, 1, e)
    loads[4].wait()
    lt[...] = lf[...].astype(F32).T.astype(BF16)
    for h in range(2):
        rt[:, h * 256:(h + 1) * 256] = rf[h * 256:(h + 1) * 256, :].astype(F32).T.astype(BF16)

    def column(q):
        return jnp.concatenate([wide_a[n, pl.ds(q, P_ALL, stride=QB), :] for n in range(LANES)], axis=1)

    wait_bytes(t1, a_recv.at[0])

    def widen(m, _):
        v = r1[pl.ds(m * 4, 4)].reshape(128, CG).astype(F32)
        for n in range(LANES):
            wide_a[n, pl.ds(pl.multiple_of(m * 128, 128), 128), :] = v[:, n * 128:(n + 1) * 128]
        return 0

    lax.fori_loop(0, XY, widen, 0)
    for q in range(QB):
        xq = column(q).astype(BF16)
        colsb[q] = xq
        mixed = dot(lf[...], xq, 1, 0)
        for n in range(LANES):
            wide_b[n, pl.ds(q, P_ALL, stride=QB), :] = mixed[:, n * 128:(n + 1) * 128]

    def narrow(m, _):
        for n in range(LANES):
            v = wide_b[n, pl.ds(pl.multiple_of(m * 64, 64), 64), :].astype(BF16)
            t1[pl.ds(m * 2, 2), :, n * 128:(n + 1) * 128] = v.reshape(2, BLK, 128)
        return 0

    lax.fori_loop(0, 32, narrow, 0)
    send_mixed(*BEFORE_COLS)

    def slopes(m, _):
        rows = pl.ds(pl.multiple_of(m * 64, 64), 64)
        for n in range(LANES):
            wide_b[n, rows, :] = gelu_slope(wide_b[n, rows, :])
        return 0

    lax.fori_loop(0, 32, slopes, 0)

    for e in range(4):
        wait_chunk(1, e)
        for t in range(4):
            jj = place(e, t, -1)
            rows = pl.ds(pl.multiple_of(jj * 128, 128), 128)
            v = r2[pl.ds(jj * 4, 4)].reshape(128, CG).astype(F32)
            for n in range(LANES):
                wide_a[n, rows, :] = v[:, n * 128:(n + 1) * 128] * wide_b[n, rows, :]
    for q in range(QB):
        gmb[q] = column(q).astype(BF16)

    for e in range(4):
        spots = [place(e, t, 1) for t in range(4)]
        lhs = jnp.concatenate([lt[pl.ds(pl.multiple_of(jj * 16, 16), 16), :] for jj in spots], axis=0)
        for q in range(QB):
            v = dot(lhs, gmb[q], 1, 0)
            for t, jj in enumerate(spots):
                for n in range(LANES):
                    wide_c[n, pl.ds(jj * 128 + q, 16, stride=QB), :] = v[t * 16:(t + 1) * 16, n * 128:(n + 1) * 128]
        for jj in spots:
            rows = pl.ds(pl.multiple_of(jj * 128, 128), 128)
            for n in range(LANES):
                v = wide_c[n, rows, :].astype(BF16)
                t2[pl.ds(jj * 4, 4), :, n * 128:(n + 1) * 128] = v.reshape(4, BLK, 128)
        send_chunk(t2, b2, 3, e)
    send_mixed(*AFTER_COLS)
    gl_acc = jnp.zeros((P_ALL, P_ALL), F32)
    for q in range(QB):
        gl_acc = gl_acc + dot(gmb[q], colsb[q], 1, 1)
    ls_s[...] = gl_acc.astype(BF16).reshape(XY, 16, P_ALL)

    def scatter(src, dst, n, e):
        for t in range(1 if e == 0 else 0, 4):
            jj = place(e, t, -1)
            pltpu.make_async_remote_copy(
                src_ref=src.at[jj], dst_ref=dst.at[j], send_sem=m_send.at[n], recv_sem=m_recv.at[n],
                device_id={"inner": jj * ZH + zh}, device_id_type=MESH,
            ).start()

    for e in range(4):
        scatter(ls_s, ls_r, 0, e)
    ls_r[j] = ls_s[j]

    def hand_out(src, dst, rows, n):
        pltpu.make_async_copy(src.at[my_rows, rows], dst.at[0, :, rows, mine], l_sem.at[n]).start()
        pltpu.make_async_remote_copy(
            src_ref=src.at[their_rows, rows], dst_ref=dst.at[0, :, rows, mine],
            send_sem=e_send.at[n], recv_sem=e_recv.at[n],
            device_id={"outer": 1 - c}, device_id_type=MESH,
        ).start()

    def gate_chip(jj):
        rows = pl.ds(pl.multiple_of(jj * 32, 32), 32)
        v = b1[pl.ds(jj * 4, 4)].astype(F32)
        for p in range(CHIP):
            act = gelu_value(v[:, p * QB:(p + 1) * QB, :].reshape(32, CG))
            ggate_v[p, rows, :] = (gout[p, rows, :].astype(F32) * act).astype(BF16)
        hand_out(ggate_v, ggate_o, rows, 6)

    def gate_grad(e):
        wait_chunk(2, e)

        def step(t, _):
            gate_chip(source(e, t))
            return 0

        lax.fori_loop(0, 4, step, 0)

    gate_grad(0)

    for e in range(4):
        wait_chunk(3, e)
        spots = [place(e, t, -1) for t in range(4)]
        parts = [[] for _ in range(CHIP)]
        for jj in spots:
            rows = pl.ds(pl.multiple_of(jj * 32, 32), 32)
            v = b2[pl.ds(jj * 4, 4)].astype(F32)
            for p in range(CHIP):
                part = v[:, p * QB:(p + 1) * QB, :].reshape(32, CG).astype(BF16)
                gcb[p, rows, :] = part
                parts[p].append(part)
        total = None
        for p in range(CHIP):
            term = dot(jnp.concatenate(parts[p], axis=0), x[p], 1, 1)
            total = term if total is None else total + term
        for t, jj in enumerate(spots):
            rs_s[jj] = total[t * 32:(t + 1) * 32, :].astype(BF16)
        scatter(rs_s, rs_r, 1, e)
    rs_r[j] = rs_s[j]
    send_mixed(*AFTER_PLANE)

    def input_grad(m, _):
        rows = pl.ds(pl.multiple_of(m * 128, 128), 128)
        for p in range(CHIP):
            gin_v[p, rows, :] = dot(rt[rows, :], gcb[p], 1, 0).astype(BF16)
        hand_out(gin_v, gin_o, rows, 5)
        return 0

    lax.fori_loop(0, 4, input_grad, 0)

    wait_bytes(ls_r.at[pl.ds(0, XY - 1)], m_recv.at[0])
    wait_bytes(rs_r.at[pl.ds(0, XY - 1)], m_recv.at[1])
    gr_sum = rs_r[0].astype(F32)
    gl_sum = ls_r[0].astype(F32)
    for k in range(1, XY):
        gr_sum = gr_sum + rs_r[k].astype(F32)
        gl_sum = gl_sum + ls_r[k].astype(F32)
    share[0:32, :] = gr_sum[:, 0:256].astype(BF16)
    share[32:64, :] = gr_sum[:, 256:512].astype(BF16)
    share[64:80, :] = gl_sum.astype(BF16)

    @pl.when(d != c)
    def _():
        pltpu.make_async_remote_copy(
            src_ref=share, dst_ref=pair, send_sem=m_send.at[2], recv_sem=m_recv.at[2],
            device_id={"dp": c}, device_id_type=MESH,
        ).start()

    send_mixed(*AFTER_PAIR)

    @pl.when(d == c)
    def _():
        wait_bytes(pair, m_recv.at[2])
        zrecv[zh] = (share[...].astype(F32) + pair[...].astype(F32)).astype(BF16)
        for k in range(1, ZH):
            pltpu.make_async_remote_copy(
                src_ref=zrecv.at[zh], dst_ref=zrecv.at[zh], send_sem=m_send.at[5], recv_sem=m_recv.at[8],
                device_id={"inner": j * ZH + (zh + k) % ZH}, device_id_type=MESH,
            ).start()

    send_mixed(*AFTER_Z)
    gate_grad(1)

    @pl.when(d == c)
    def _():
        wait_bytes(zrecv.at[pl.ds(0, ZH - 1)], m_recv.at[8])
        total = zrecv[0].astype(F32)
        for k in range(1, ZH):
            total = total + zrecv[k].astype(F32)
        fin[j] = total.astype(BF16)
        for e in range(4):
            for t in range(1 if e == 0 else 0, 4):
                pltpu.make_async_remote_copy(
                    src_ref=fin.at[j], dst_ref=fin.at[j], send_sem=m_send.at[3], recv_sem=m_recv.at[3 + e],
                    device_id={"inner": place(e, t, 1) * ZH + zh}, device_id_type=MESH,
                ).start()

    send_mixed(*AFTER_SHARES)
    gate_grad(2)

    def last_gate(t):
        wait_bytes(t1.at[pl.ds(0, ZH)], a_recv.at[13 + t])
        gate_chip(place(3, t, -1))

    def unpack():
        for k in range(XY):
            gr_o[0, k * 32:(k + 1) * 32, 0:256] = fin[k, 0:32, :].astype(F32)
            gr_o[0, k * 32:(k + 1) * 32, 256:512] = fin[k, 32:64, :].astype(F32)
            gl_o[0, k * 16:(k + 1) * 16, :] = fin[k, 64:80, :].astype(F32)

    last_gate(0)
    last_gate(1)

    @pl.when(d == c)
    def _():
        for e in range(4):
            wait_bytes(fin.at[pl.ds(0, 3 if e == 0 else 4)], m_recv.at[3 + e])
            for t in range(4):
                jj = place(e, t, -1)
                pltpu.make_async_remote_copy(
                    src_ref=fin.at[jj], dst_ref=fin.at[jj], send_sem=m_send.at[4], recv_sem=m_recv.at[7],
                    device_id={"outer": 1 - c}, device_id_type=MESH,
                ).start()
        unpack()

    last_gate(2)
    last_gate(3)

    @pl.when(d == c)
    def _():
        wait_bytes(fin.at[pl.ds(0, XY - 1)], m_send.at[3])
        wait_bytes(zrecv.at[pl.ds(0, 3)], m_send.at[5])
        wait_bytes(fin, m_send.at[4])

    @pl.when(d != c)
    def _():
        wait_bytes(share, m_send.at[2])
        wait_bytes(fin, m_recv.at[7])
        unpack()

    for n in range(4):
        wait_bytes(t1, a_send.at[n])
    wait_bytes(ls_r.at[pl.ds(0, XY - 1)], m_send.at[0])
    wait_bytes(rs_r.at[pl.ds(0, XY - 1)], m_send.at[1])
    for gift in gifts:
        gift.wait_send()
    half = ggate_v.at[pl.ds(0, ROWS)]
    for n in (5, 6):
        wait_bytes(half, l_sem.at[n])
        wait_bytes(half, e_send.at[n])
        wait_bytes(half, e_recv.at[n])


def hand_on(*refs):
    results, outputs, sem = refs[:4], refs[4:8], refs[8]
    parts = []
    for src, dst in zip(results[:2], outputs[:2]):
        for p in range(ROWS):
            parts.append((src.at[0, p], dst.at[0, p]))
    parts.extend(zip(results[2:], outputs[2:]))
    copies = [pltpu.make_async_copy(src, dst, sem.at[n]) for n, (src, dst) in enumerate(parts)]
    for copy in copies:
        copy.start()
    for copy in copies:
        copy.wait()


def body(*operands):
    hbm = pl.BlockSpec(memory_space=pl.ANY)
    shapes = (
        ((1, ROWS, Q, 2 * CG), BF16),
        ((1, ROWS, Q, 2 * CG), BF16),
        ((1, Q, Q), F32),
        ((1, P_ALL, P_ALL), F32),
    )
    blocks = pltpu.VMEM((INNER, BLK, CG), BF16)
    rows = pltpu.VMEM((CHIP, Q, CG), BF16)
    wide = pltpu.VMEM((LANES, INNER * BLK, 128), F32)
    columns = pltpu.VMEM((QB, P_ALL, CG), BF16)
    scratch = [blocks] * 8 + [
        rows, rows, rows,
        pltpu.VMEM((Q, Q), BF16),
        pltpu.VMEM((P_ALL, P_ALL), BF16),
        rows, rows,
        wide, wide, wide,
        columns, columns,
        rows,
        pltpu.VMEM((Q, Q), BF16),
        pltpu.VMEM((P_ALL, P_ALL), BF16),
        pltpu.VMEM((XY, 32, Q), BF16),
        pltpu.VMEM((XY, 32, Q), BF16),
        pltpu.VMEM((XY, 16, P_ALL), BF16),
        pltpu.VMEM((XY, 16, P_ALL), BF16),
        pltpu.VMEM((80, 256), BF16),
        pltpu.VMEM((80, 256), BF16),
        pltpu.VMEM((ZH, 80, 256), BF16),
        pltpu.VMEM((XY, 80, 256), BF16),
        pltpu.SemaphoreType.DMA((4,)),
        pltpu.SemaphoreType.DMA((17,)),
        pltpu.SemaphoreType.DMA((6,)),
        pltpu.SemaphoreType.DMA((9,)),
        pltpu.SemaphoreType.DMA((7,)),
        pltpu.SemaphoreType.DMA((7,)),
        pltpu.SemaphoreType.DMA((9,)),
    ]
    results = pl.pallas_call(
        kernel,
        out_shape=tuple(pltpu.VMEM(*shape) for shape in shapes),
        in_specs=[hbm] * 5,
        out_specs=(pl.BlockSpec(memory_space=pltpu.VMEM),) * 4,
        scratch_shapes=scratch,
        compiler_params=pltpu.CompilerParams(
            collective_id=0, has_side_effects=True, vmem_limit_bytes=52 * 1024 * 1024
        ),
        cost_estimate=pl.CostEstimate(flops=4 * 10**9, bytes_accessed=12 * 10**6, transcendentals=3 * 10**6),
    )(*(pltpu.with_memory_space_constraint(a, pltpu.HBM) for a in operands))
    return pl.pallas_call(
        hand_on,
        out_shape=tuple(jax.ShapeDtypeStruct(*shape) for shape in shapes),
        in_specs=[pl.BlockSpec(memory_space=pltpu.VMEM)] * 4,
        out_specs=(hbm,) * 4,
        scratch_shapes=[pltpu.SemaphoreType.DMA((6,))],
        compiler_params=pltpu.CompilerParams(vmem_limit_bytes=8 * 1024 * 1024),
        cost_estimate=pl.CostEstimate(flops=0, bytes_accessed=9 * 10**6, transcendentals=0),
    )(*(pltpu.with_memory_space_constraint(a, pltpu.VMEM) for a in results))


def solution(mesh):
    rows = P("dp", ("inner", "outer"), None, None)
    return jax.shard_map(
        body,
        mesh=mesh,
        in_specs=(rows, rows, rows, P(), P()),
        out_specs=(rows, rows, P("dp", None, None), P("dp", None, None)),
        check_vma=False,
    )
```

```python
import jax
import jax.numpy as jnp
from jax import lax
from jax.experimental import pallas as pl
from jax.experimental.pallas import tpu as pltpu
from jax.sharding import PartitionSpec as P

MESH = pl.DeviceIdType.MESH
F32 = jnp.float32
BF16 = jnp.bfloat16

INNER = 64
ZH = 4
XY = 16
ROWS = 2
CHIP = 4
CG = 384
LANES = CG // 128
Q = 512
P_ALL = 256
QB = 8
BLK = CHIP * QB

BEFORE_COLS = (0, 1)
AFTER_COLS = (2, 3)
AFTER_PLANE = (4, 5)
AFTER_Z = (6,)
AFTER_SHARES = (7,)


def gelu_value(mixed):
    return mixed * (0.5 * (1.0 + lax.erf(mixed * 0.7071067811865476)))


def gelu_slope(mixed):
    normal_cdf = 0.5 * (1.0 + lax.erf(mixed * 0.7071067811865476))
    density = jnp.exp(-0.5 * mixed * mixed) * 0.3989422804014327
    return normal_cdf + mixed * density


def wait_bytes(ref, sem):
    pltpu.make_async_copy(ref, ref, sem).wait()


def dot(a, b, ca, cb):
    return lax.dot_general(a, b, (((ca,), (cb,)), ((), ())), preferred_element_type=F32)


def kernel(
    x_h, gate_h, gout_h, rf_h, lf_h,
    gin_o, ggate_o, gr_o, gl_o,
    s1, s2, r1, r2, t1, t2, b1, b2,
    x, gate, gout, rf, lf, gin_v, ggate_v,
    wide_a, wide_b, wide_c, colsb, gmb, gcb, rt, lt,
    rs_s, rs_r, ls_s, ls_r, share, zrecv, fin,
    a_send, a_recv, m_send, m_recv, e_send, e_recv, l_sem,
):
    i = lax.axis_index("inner")
    c = lax.axis_index("outer")
    d = lax.axis_index("dp")
    zh = i % ZH
    j = i // ZH
    ys = [(j // 4 + n) % 4 for n in range(4)]
    xs = [(j % 4 + n) % 4 for n in range(4)]
    mine = pl.ds(pl.multiple_of(c * CG, CG), CG)
    theirs = pl.ds(pl.multiple_of((1 - c) * CG, CG), CG)
    my_rows = pl.ds(c * ROWS, ROWS)
    their_rows = pl.ds((1 - c) * ROWS, ROWS)

    def place(e, t, sign):
        return ys[sign * (e + t) % 4] * 4 + xs[sign * t % 4]

    def source(e, t):
        return lax.rem(ys[0] + 8 - e - t, 4) * 4 + lax.rem(xs[0] + 4 - t, 4)

    yc = [(j // 4 + n + 2 * c) % 4 for n in range(4)]
    xc = [(j % 4 + n + 2 * c) % 4 for n in range(4)]

    def along_z(n):
        n = n % 4
        dz = (1 - 2 * c) * (1 - 2 * (n % 2)) * (3 - 2 * (n // 2))
        return (zh + d + (dz + 7) // 2) % ZH

    def each_partner(e, act, first=0, last=ZH):
        def step(u, _):
            for t in range(4):
                act((yc[(e + t) % 4] * 4 + xc[t]) * ZH + along_z(t + u))
            return 0

        lax.fori_loop(first, last, step, 0)

    arrays = ((x_h, x), (gate_h, gate), (gout_h, gout))
    loads = [
        pltpu.make_async_copy(src.at[0, :, :, mine], dst.at[my_rows], l_sem.at[n])
        for n, (src, dst) in enumerate(arrays)
    ]
    loads.append(pltpu.make_async_copy(rf_h.at[c], rf, l_sem.at[3]))
    loads.append(pltpu.make_async_copy(lf_h.at[c], lf, l_sem.at[4]))
    for n in (0, 3, 1, 2, 4):
        loads[n].start()

    barrier = pltpu.get_barrier_semaphore()

    def greet(ii):
        pl.semaphore_signal(barrier, inc=1, device_id={"inner": ii, "dp": 1 - d}, device_id_type=MESH)

    pl.semaphore_signal(barrier, inc=1, device_id={"outer": 1 - c}, device_id_type=MESH)
    for e in range(4):
        each_partner(e, greet)
    for k in range(1, ZH):
        pl.semaphore_signal(
            barrier, inc=1, device_id={"inner": j * ZH + (zh + k) % ZH}, device_id_type=MESH
        )

    def greet_plane(k, _):
        pl.semaphore_signal(barrier, inc=1, device_id={"inner": lax.rem(j + k, XY) * ZH + zh}, device_id_type=MESH)
        return 0

    lax.fori_loop(1, XY, greet_plane, 0)

    def right_mix(h):
        def step(m, _):
            lhs = rf[pl.ds(pl.multiple_of(m * 128, 128), 128), :]
            parts = [dot(lhs, x[h * ROWS + p], 1, 0).reshape(16, QB, CG) for p in range(ROWS)]
            half = pl.ds(pl.multiple_of(h * 16, 16), 16)
            s1[pl.ds(m * 16, 16), half, :] = jnp.concatenate(parts, axis=1).astype(BF16)
            return 0

        lax.fori_loop(0, 4, step, 0)

    loads[0].wait()
    loads[3].wait()
    right_mix(c)

    pl.semaphore_wait(barrier, 1 + INNER + (ZH - 1) + (XY - 1))
    gifts = [
        pltpu.make_async_remote_copy(
            src_ref=src.at[0, :, :, theirs], dst_ref=dst.at[my_rows], send_sem=e_send.at[n], recv_sem=e_recv.at[n],
            device_id={"outer": 1 - c}, device_id_type=MESH,
        )
        for n, (src, dst) in enumerate(arrays)
    ]
    gifts[0].start()

    def weigh(e):
        for t in range(4):
            jj = place(e, t, 1)
            rows = pl.ds(pl.multiple_of(jj * 32, 32), 32)
            parts = []
            for p in range(CHIP):
                a = gout[p, rows, :].astype(F32)
                b = gate[p, rows, :].astype(F32)
                parts.append((a * b).reshape(4, QB, CG))
            s2[pl.ds(jj * 4, 4)] = jnp.concatenate(parts, axis=1).astype(BF16)

    def send_to(src, dst, n, sem, ii):
        pltpu.make_async_remote_copy(
            src_ref=src.at[ii], dst_ref=dst.at[i], send_sem=a_send.at[n], recv_sem=a_recv.at[sem],
            device_id={"inner": ii, "dp": 1 - d}, device_id_type=MESH,
        ).start()

    def send_chunk(src, dst, n, e, first=0, last=ZH):
        each_partner(e, lambda ii: send_to(src, dst, n, 4 * n - 3 + e, ii), first, last)

    def send_mixed(*pieces):
        for k in pieces:
            if k < 6:
                send_chunk(t1, b1, 2, k // 2, k % 2 * 2, k % 2 * 2 + 2)
            else:
                for t in (k % 2 * 2, k % 2 * 2 + 1):
                    def step(u, _):
                        send_to(t1, b1, 2, 13 + t, place(3, t, 1) * ZH + along_z(t + u))
                        return 0

                    lax.fori_loop(0, ZH, step, 0)

    def wait_chunk(n, e):
        wait_bytes(t1.at[pl.ds(0, XY)], a_recv.at[4 * n - 3 + e])

    def send_half(h):
        half = pl.ds(pl.multiple_of(h * 16, 16), 16)

        def act(ii):
            pltpu.make_async_remote_copy(
                src_ref=s1.at[ii, half], dst_ref=r1.at[i, half], send_sem=a_send.at[0], recv_sem=a_recv.at[0],
                device_id={"inner": ii, "dp": 1 - d}, device_id_type=MESH,
            ).start()

        for e in range(4):
            each_partner(e, act)

    send_half(c)
    gifts[0].wait_recv()
    gifts[1].start()
    gifts[2].start()
    right_mix(1 - c)
    send_half(1 - c)
    loads[1].wait()
    loads[2].wait()
    gifts[1].wait_recv()
    gifts[2].wait_recv()
    for e in range(4):
        weigh(e)
        send_chunk(s2, r2, 1, e)
    loads[4].wait()
    lt[...] = lf[...].astype(F32).T.astype(BF16)
    for h in range(2):
        rt[:, h * 256:(h + 1) * 256] = rf[h * 256:(h + 1) * 256, :].astype(F32).T.astype(BF16)

    def column(q):
        return jnp.concatenate([wide_a[n, pl.ds(q, P_ALL, stride=QB), :] for n in range(LANES)], axis=1)

    wait_bytes(t1, a_recv.at[0])

    def widen(m, _):
        v = r1[pl.ds(m * 4, 4)].reshape(128, CG).astype(F32)
        for n in range(LANES):
            wide_a[n, pl.ds(pl.multiple_of(m * 128, 128), 128), :] = v[:, n * 128:(n + 1) * 128]
        return 0

    lax.fori_loop(0, XY, widen, 0)
    for q in range(QB):
        xq = column(q).astype(BF16)
        colsb[q] = xq
        mixed = dot(lf[...], xq, 1, 0)
        for n in range(LANES):
            wide_b[n, pl.ds(q, P_ALL, stride=QB), :] = mixed[:, n * 128:(n + 1) * 128]

    def narrow(m, _):
        for n in range(LANES):
            v = wide_b[n, pl.ds(pl.multiple_of(m * 64, 64), 64), :].astype(BF16)
            t1[pl.ds(m * 2, 2), :, n * 128:(n + 1) * 128] = v.reshape(2, BLK, 128)
        return 0

    lax.fori_loop(0, 32, narrow, 0)
    send_mixed(*BEFORE_COLS)

    def slopes(m, _):
        rows = pl.ds(pl.multiple_of(m * 64, 64), 64)
        for n in range(LANES):
            wide_b[n, rows, :] = gelu_slope(wide_b[n, rows, :])
        return 0

    lax.fori_loop(0, 32, slopes, 0)

    for e in range(4):
        wait_chunk(1, e)
        for t in range(4):
            jj = place(e, t, -1)
            rows = pl.ds(pl.multiple_of(jj * 128, 128), 128)
            v = r2[pl.ds(jj * 4, 4)].reshape(128, CG).astype(F32)
            for n in range(LANES):
                wide_a[n, rows, :] = v[:, n * 128:(n + 1) * 128] * wide_b[n, rows, :]
    for q in range(QB):
        gmb[q] = column(q).astype(BF16)

    for e in range(4):
        spots = [place(e, t, 1) for t in range(4)]
        lhs = jnp.concatenate([lt[pl.ds(pl.multiple_of(jj * 16, 16), 16), :] for jj in spots], axis=0)
        for q in range(QB):
            v = dot(lhs, gmb[q], 1, 0)
            for t, jj in enumerate(spots):
                for n in range(LANES):
                    wide_c[n, pl.ds(jj * 128 + q, 16, stride=QB), :] = v[t * 16:(t + 1) * 16, n * 128:(n + 1) * 128]
        for jj in spots:
            rows = pl.ds(pl.multiple_of(jj * 128, 128), 128)
            for n in range(LANES):
                v = wide_c[n, rows, :].astype(BF16)
                t2[pl.ds(jj * 4, 4), :, n * 128:(n + 1) * 128] = v.reshape(4, BLK, 128)
        send_chunk(t2, b2, 3, e)
    send_mixed(*AFTER_COLS)
    gl_acc = jnp.zeros((P_ALL, P_ALL), F32)
    for q in range(QB):
        gl_acc = gl_acc + dot(gmb[q], colsb[q], 1, 1)
    ls_s[...] = gl_acc.astype(BF16).reshape(XY, 16, P_ALL)

    def scatter(src, dst, n, e):
        for t in range(1 if e == 0 else 0, 4):
            jj = place(e, t, -1)
            pltpu.make_async_remote_copy(
                src_ref=src.at[jj], dst_ref=dst.at[j], send_sem=m_send.at[n], recv_sem=m_recv.at[n],
                device_id={"inner": jj * ZH + zh}, device_id_type=MESH,
            ).start()

    for e in range(4):
        scatter(ls_s, ls_r, 0, e)
    ls_r[j] = ls_s[j]

    def hand_out(src, dst, rows, n):
        pltpu.make_async_copy(src.at[my_rows, rows], dst.at[0, :, rows, mine], l_sem.at[n]).start()
        pltpu.make_async_remote_copy(
            src_ref=src.at[their_rows, rows], dst_ref=dst.at[0, :, rows, mine],
            send_sem=e_send.at[n], recv_sem=e_recv.at[n],
            device_id={"outer": 1 - c}, device_id_type=MESH,
        ).start()

    def gate_chip(jj):
        rows = pl.ds(pl.multiple_of(jj * 32, 32), 32)
        v = b1[pl.ds(jj * 4, 4)].astype(F32)
        for p in range(CHIP):
            act = gelu_value(v[:, p * QB:(p + 1) * QB, :].reshape(32, CG))
            ggate_v[p, rows, :] = (gout[p, rows, :].astype(F32) * act).astype(BF16)
        hand_out(ggate_v, ggate_o, rows, 6)

    def gate_grad(e):
        wait_chunk(2, e)

        def step(t, _):
            gate_chip(source(e, t))
            return 0

        lax.fori_loop(0, 4, step, 0)

    gate_grad(0)

    for e in range(4):
        wait_chunk(3, e)
        spots = [place(e, t, -1) for t in range(4)]
        parts = [[] for _ in range(CHIP)]
        for jj in spots:
            rows = pl.ds(pl.multiple_of(jj * 32, 32), 32)
            v = b2[pl.ds(jj * 4, 4)].astype(F32)
            for p in range(CHIP):
                part = v[:, p * QB:(p + 1) * QB, :].reshape(32, CG).astype(BF16)
                gcb[p, rows, :] = part
                parts[p].append(part)
        total = None
        for p in range(CHIP):
            term = dot(jnp.concatenate(parts[p], axis=0), x[p], 1, 1)
            total = term if total is None else total + term
        for t, jj in enumerate(spots):
            rs_s[jj] = total[t * 32:(t + 1) * 32, :].astype(BF16)
        scatter(rs_s, rs_r, 1, e)
    rs_r[j] = rs_s[j]
    send_mixed(*AFTER_PLANE)

    def input_grad(m, _):
        rows = pl.ds(pl.multiple_of(m * 128, 128), 128)
        for p in range(CHIP):
            gin_v[p, rows, :] = dot(rt[rows, :], gcb[p], 1, 0).astype(BF16)
        hand_out(gin_v, gin_o, rows, 5)
        return 0

    lax.fori_loop(0, 4, input_grad, 0)

    wait_bytes(ls_r.at[pl.ds(0, XY - 1)], m_recv.at[0])
    wait_bytes(rs_r.at[pl.ds(0, XY - 1)], m_recv.at[1])
    gr_sum = rs_r[0].astype(F32)
    gl_sum = ls_r[0].astype(F32)
    for k in range(1, XY):
        gr_sum = gr_sum + rs_r[k].astype(F32)
        gl_sum = gl_sum + ls_r[k].astype(F32)
    share[0:32, :] = gr_sum[:, 0:256].astype(BF16)
    share[32:64, :] = gr_sum[:, 256:512].astype(BF16)
    share[64:80, :] = gl_sum.astype(BF16)

    def to_z(k):
        return pltpu.make_async_remote_copy(
            src_ref=share, dst_ref=zrecv.at[zh * 2 + d], send_sem=m_send.at[2], recv_sem=m_recv.at[2],
            device_id={"inner": j * ZH + (zh + k) % ZH, "dp": c}, device_id_type=MESH,
        )

    for k in range(1, ZH):
        to_z(k).start()

    @pl.when(d != c)
    def _():
        to_z(0).start()

    send_mixed(*AFTER_Z)
    gate_grad(1)

    @pl.when(d == c)
    def _():
        zrecv[zh * 2 + d] = share[...]
        wait_bytes(zrecv.at[pl.ds(0, 7)], m_recv.at[2])
        total = zrecv[0].astype(F32)
        for k in range(1, 8):
            total = total + zrecv[k].astype(F32)
        fin[j] = total.astype(BF16)

        for e in range(4):
            for t in range(1 if e == 0 else 0, 4):
                pltpu.make_async_remote_copy(
                    src_ref=fin.at[j], dst_ref=fin.at[j], send_sem=m_send.at[3], recv_sem=m_recv.at[3 + e],
                    device_id={"inner": place(e, t, 1) * ZH + zh}, device_id_type=MESH,
                ).start()

    send_mixed(*AFTER_SHARES)
    gate_grad(2)

    def last_gate(t):
        wait_bytes(t1.at[pl.ds(0, ZH)], a_recv.at[13 + t])
        gate_chip(place(3, t, -1))

    def unpack():
        for k in range(XY):
            gr_o[0, k * 32:(k + 1) * 32, 0:256] = fin[k, 0:32, :].astype(F32)
            gr_o[0, k * 32:(k + 1) * 32, 256:512] = fin[k, 32:64, :].astype(F32)
            gl_o[0, k * 16:(k + 1) * 16, :] = fin[k, 64:80, :].astype(F32)

    last_gate(0)
    last_gate(1)

    @pl.when(d == c)
    def _():
        for e in range(4):
            wait_bytes(fin.at[pl.ds(0, 3 if e == 0 else 4)], m_recv.at[3 + e])
            for t in range(4):
                jj = place(e, t, -1)
                pltpu.make_async_remote_copy(
                    src_ref=fin.at[jj], dst_ref=fin.at[jj], send_sem=m_send.at[4], recv_sem=m_recv.at[7],
                    device_id={"outer": 1 - c}, device_id_type=MESH,
                ).start()
        unpack()

    last_gate(2)
    last_gate(3)

    @pl.when(d == c)
    def _():
        wait_bytes(fin.at[pl.ds(0, XY - 1)], m_send.at[3])
        wait_bytes(zrecv.at[pl.ds(0, 3)], m_send.at[2])
        wait_bytes(fin, m_send.at[4])

    @pl.when(d != c)
    def _():
        wait_bytes(zrecv.at[pl.ds(0, 4)], m_send.at[2])
        wait_bytes(fin, m_recv.at[7])
        unpack()

    for n in range(4):
        wait_bytes(t1, a_send.at[n])
    wait_bytes(ls_r.at[pl.ds(0, XY - 1)], m_send.at[0])
    wait_bytes(rs_r.at[pl.ds(0, XY - 1)], m_send.at[1])
    for gift in gifts:
        gift.wait_send()
    half = ggate_v.at[pl.ds(0, ROWS)]
    for n in (5, 6):
        wait_bytes(half, l_sem.at[n])
        wait_bytes(half, e_send.at[n])
        wait_bytes(half, e_recv.at[n])


def hand_on(*refs):
    results, outputs, sem = refs[:4], refs[4:8], refs[8]
    parts = []
    for src, dst in zip(results[:2], outputs[:2]):
        for p in range(ROWS):
            parts.append((src.at[0, p], dst.at[0, p]))
    parts.extend(zip(results[2:], outputs[2:]))
    copies = [pltpu.make_async_copy(src, dst, sem.at[n]) for n, (src, dst) in enumerate(parts)]
    for copy in copies:
        copy.start()
    for copy in copies:
        copy.wait()


def body(*operands):
    hbm = pl.BlockSpec(memory_space=pl.ANY)
    shapes = (
        ((1, ROWS, Q, 2 * CG), BF16),
        ((1, ROWS, Q, 2 * CG), BF16),
        ((1, Q, Q), F32),
        ((1, P_ALL, P_ALL), F32),
    )
    blocks = pltpu.VMEM((INNER, BLK, CG), BF16)
    rows = pltpu.VMEM((CHIP, Q, CG), BF16)
    wide = pltpu.VMEM((LANES, INNER * BLK, 128), F32)
    columns = pltpu.VMEM((QB, P_ALL, CG), BF16)
    scratch = [blocks] * 8 + [
        rows, rows, rows,
        pltpu.VMEM((Q, Q), BF16),
        pltpu.VMEM((P_ALL, P_ALL), BF16),
        rows, rows,
        wide, wide, wide,
        columns, columns,
        rows,
        pltpu.VMEM((Q, Q), BF16),
        pltpu.VMEM((P_ALL, P_ALL), BF16),
        pltpu.VMEM((XY, 32, Q), BF16),
        pltpu.VMEM((XY, 32, Q), BF16),
        pltpu.VMEM((XY, 16, P_ALL), BF16),
        pltpu.VMEM((XY, 16, P_ALL), BF16),
        pltpu.VMEM((80, 256), BF16),
        pltpu.VMEM((8, 80, 256), BF16),
        pltpu.VMEM((XY, 80, 256), BF16),
        pltpu.SemaphoreType.DMA((4,)),
        pltpu.SemaphoreType.DMA((17,)),
        pltpu.SemaphoreType.DMA((5,)),
        pltpu.SemaphoreType.DMA((8,)),
        pltpu.SemaphoreType.DMA((7,)),
        pltpu.SemaphoreType.DMA((7,)),
        pltpu.SemaphoreType.DMA((9,)),
    ]
    results = pl.pallas_call(
        kernel,
        out_shape=tuple(pltpu.VMEM(*shape) for shape in shapes),
        in_specs=[hbm] * 5,
        out_specs=(pl.BlockSpec(memory_space=pltpu.VMEM),) * 4,
        scratch_shapes=scratch,
        compiler_params=pltpu.CompilerParams(
            collective_id=0, has_side_effects=True, vmem_limit_bytes=52 * 1024 * 1024
        ),
        cost_estimate=pl.CostEstimate(flops=4 * 10**9, bytes_accessed=12 * 10**6, transcendentals=3 * 10**6),
    )(*(pltpu.with_memory_space_constraint(a, pltpu.HBM) for a in operands))
    return pl.pallas_call(
        hand_on,
        out_shape=tuple(jax.ShapeDtypeStruct(*shape) for shape in shapes),
        in_specs=[pl.BlockSpec(memory_space=pltpu.VMEM)] * 4,
        out_specs=(hbm,) * 4,
        scratch_shapes=[pltpu.SemaphoreType.DMA((6,))],
        compiler_params=pltpu.CompilerParams(vmem_limit_bytes=8 * 1024 * 1024),
        cost_estimate=pl.CostEstimate(flops=0, bytes_accessed=9 * 10**6, transcendentals=0),
    )(*(pltpu.with_memory_space_constraint(a, pltpu.VMEM) for a in results))


def solution(mesh):
    rows = P("dp", ("inner", "outer"), None, None)
    return jax.shard_map(
        body,
        mesh=mesh,
        in_specs=(rows, rows, rows, P(), P()),
        out_specs=(rows, rows, P("dp", None, None), P("dp", None, None)),
        check_vma=False,
    )
```

```python
import jax
import jax.numpy as jnp
from jax import lax
from jax.experimental import pallas as pl
from jax.experimental.pallas import tpu as pltpu
from jax.sharding import PartitionSpec as P

MESH = pl.DeviceIdType.MESH
F32 = jnp.float32
BF16 = jnp.bfloat16

INNER = 64
ZH = 4
XY = 16
ROWS = 2
CHIP = 4
CG = 384
LANES = CG // 128
Q = 512
P_ALL = 256
QB = 8
BLK = CHIP * QB

BEFORE_COLS = (0,)
AFTER_COLS = (1, 2)
AFTER_PLANE = (3, 4)
AFTER_Z = (5,)
AFTER_SHARES = (6, 7)


def gelu_value(mixed):
    return mixed * (0.5 * (1.0 + lax.erf(mixed * 0.7071067811865476)))


def gelu_slope(mixed):
    normal_cdf = 0.5 * (1.0 + lax.erf(mixed * 0.7071067811865476))
    density = jnp.exp(-0.5 * mixed * mixed) * 0.3989422804014327
    return normal_cdf + mixed * density


def wait_bytes(ref, sem):
    pltpu.make_async_copy(ref, ref, sem).wait()


def dot(a, b, ca, cb):
    return lax.dot_general(a, b, (((ca,), (cb,)), ((), ())), preferred_element_type=F32)


def kernel(
    x_h, gate_h, gout_h, rf_h, lf_h,
    gin_o, ggate_o, gr_o, gl_o,
    s1, s2, r1, r2, t1, t2, b1, b2,
    x, gate, gout, rf, lf, gin_v, ggate_v,
    wide_a, wide_b, wide_c, colsb, gmb, gcb, rt, lt,
    rs_s, rs_r, ls_s, ls_r, share, zrecv, fin,
    a_send, a_recv, m_send, m_recv, e_send, e_recv, l_sem,
):
    i = lax.axis_index("inner")
    c = lax.axis_index("outer")
    d = lax.axis_index("dp")
    zh = i % ZH
    j = i // ZH
    ys = [(j // 4 + n) % 4 for n in range(4)]
    xs = [(j % 4 + n) % 4 for n in range(4)]
    mine = pl.ds(pl.multiple_of(c * CG, CG), CG)
    theirs = pl.ds(pl.multiple_of((1 - c) * CG, CG), CG)
    my_rows = pl.ds(c * ROWS, ROWS)
    their_rows = pl.ds((1 - c) * ROWS, ROWS)

    def place(e, t, sign):
        return ys[sign * (e + t) % 4] * 4 + xs[sign * t % 4]

    def source(e, t):
        return lax.rem(ys[0] + 8 - e - t, 4) * 4 + lax.rem(xs[0] + 4 - t, 4)

    yc = [(j // 4 + n + 2 * c) % 4 for n in range(4)]
    xc = [(j % 4 + n + 2 * c) % 4 for n in range(4)]

    def along_z(n):
        n = n % 4
        dz = (1 - 2 * c) * (1 - 2 * (n % 2)) * (3 - 2 * (n // 2))
        return (zh + d + (dz + 7) // 2) % ZH

    def each_partner(e, act, first=0, last=ZH):
        def step(u, _):
            for t in range(4):
                act((yc[(e + t) % 4] * 4 + xc[t]) * ZH + along_z(t + u))
            return 0

        lax.fori_loop(first, last, step, 0)

    arrays = ((x_h, x), (gate_h, gate), (gout_h, gout))
    loads = [
        pltpu.make_async_copy(src.at[0, :, :, mine], dst.at[my_rows], l_sem.at[n])
        for n, (src, dst) in enumerate(arrays)
    ]
    loads.append(pltpu.make_async_copy(rf_h.at[c], rf, l_sem.at[3]))
    loads.append(pltpu.make_async_copy(lf_h.at[c], lf, l_sem.at[4]))
    for n in (0, 3, 1, 2, 4):
        loads[n].start()

    barrier = pltpu.get_barrier_semaphore()

    def greet(ii):
        pl.semaphore_signal(barrier, inc=1, device_id={"inner": ii, "dp": 1 - d}, device_id_type=MESH)

    pl.semaphore_signal(barrier, inc=1, device_id={"outer": 1 - c}, device_id_type=MESH)
    for e in range(4):
        each_partner(e, greet)
    for k in range(1, ZH):
        pl.semaphore_signal(
            barrier, inc=1, device_id={"inner": j * ZH + (zh + k) % ZH}, device_id_type=MESH
        )

    def greet_plane(k, _):
        pl.semaphore_signal(barrier, inc=1, device_id={"inner": lax.rem(j + k, XY) * ZH + zh}, device_id_type=MESH)
        return 0

    lax.fori_loop(1, XY, greet_plane, 0)

    def right_mix(h):
        def step(m, _):
            lhs = rf[pl.ds(pl.multiple_of(m * 128, 128), 128), :]
            parts = [dot(lhs, x[h * ROWS + p], 1, 0).reshape(16, QB, CG) for p in range(ROWS)]
            half = pl.ds(pl.multiple_of(h * 16, 16), 16)
            s1[pl.ds(m * 16, 16), half, :] = jnp.concatenate(parts, axis=1).astype(BF16)
            return 0

        lax.fori_loop(0, 4, step, 0)

    loads[0].wait()
    loads[3].wait()
    right_mix(c)

    pl.semaphore_wait(barrier, 1 + INNER + (ZH - 1) + (XY - 1))
    gifts = [
        pltpu.make_async_remote_copy(
            src_ref=src.at[0, :, :, theirs], dst_ref=dst.at[my_rows], send_sem=e_send.at[n], recv_sem=e_recv.at[n],
            device_id={"outer": 1 - c}, device_id_type=MESH,
        )
        for n, (src, dst) in enumerate(arrays)
    ]
    gifts[0].start()

    def weigh(e):
        for t in range(4):
            jj = place(e, t, 1)
            rows = pl.ds(pl.multiple_of(jj * 32, 32), 32)
            parts = []
            for p in range(CHIP):
                a = gout[p, rows, :].astype(F32)
                b = gate[p, rows, :].astype(F32)
                parts.append((a * b).reshape(4, QB, CG))
            s2[pl.ds(jj * 4, 4)] = jnp.concatenate(parts, axis=1).astype(BF16)

    def send_to(src, dst, n, sem, ii):
        pltpu.make_async_remote_copy(
            src_ref=src.at[ii], dst_ref=dst.at[i], send_sem=a_send.at[n], recv_sem=a_recv.at[sem],
            device_id={"inner": ii, "dp": 1 - d}, device_id_type=MESH,
        ).start()

    def send_chunk(src, dst, n, e, first=0, last=ZH):
        each_partner(e, lambda ii: send_to(src, dst, n, 4 * n - 3 + e, ii), first, last)

    def send_mixed(*pieces):
        for k in pieces:
            if k < 6:
                send_chunk(t1, b1, 2, k // 2, k % 2 * 2, k % 2 * 2 + 2)
            else:
                for t in (k % 2 * 2, k % 2 * 2 + 1):
                    def step(u, _):
                        send_to(t1, b1, 2, 13 + t, place(3, t, 1) * ZH + along_z(t + u))
                        return 0

                    lax.fori_loop(0, ZH, step, 0)

    def wait_chunk(n, e):
        wait_bytes(t1.at[pl.ds(0, XY)], a_recv.at[4 * n - 3 + e])

    def send_half(h):
        half = pl.ds(pl.multiple_of(h * 16, 16), 16)

        def act(ii):
            pltpu.make_async_remote_copy(
                src_ref=s1.at[ii, half], dst_ref=r1.at[i, half], send_sem=a_send.at[0], recv_sem=a_recv.at[0],
                device_id={"inner": ii, "dp": 1 - d}, device_id_type=MESH,
            ).start()

        for e in range(4):
            each_partner(e, act)

    send_half(c)
    gifts[0].wait_recv()
    gifts[1].start()
    gifts[2].start()
    right_mix(1 - c)
    send_half(1 - c)
    loads[1].wait()
    loads[2].wait()
    gifts[1].wait_recv()
    gifts[2].wait_recv()
    for e in range(4):
        weigh(e)
        send_chunk(s2, r2, 1, e)
    loads[4].wait()
    lt[...] = lf[...].astype(F32).T.astype(BF16)
    for h in range(2):
        rt[:, h * 256:(h + 1) * 256] = rf[h * 256:(h + 1) * 256, :].astype(F32).T.astype(BF16)

    def column(q):
        return jnp.concatenate([wide_a[n, pl.ds(q, P_ALL, stride=QB), :] for n in range(LANES)], axis=1)

    wait_bytes(t1, a_recv.at[0])

    def widen(m, _):
        v = r1[pl.ds(m * 4, 4)].reshape(128, CG).astype(F32)
        for n in range(LANES):
            wide_a[n, pl.ds(pl.multiple_of(m * 128, 128), 128), :] = v[:, n * 128:(n + 1) * 128]
        return 0

    lax.fori_loop(0, XY, widen, 0)
    for q in range(QB):
        xq = column(q).astype(BF16)
        colsb[q] = xq
        mixed = dot(lf[...], xq, 1, 0)
        for n in range(LANES):
            wide_b[n, pl.ds(q, P_ALL, stride=QB), :] = mixed[:, n * 128:(n + 1) * 128]

    def narrow(m, _):
        for n in range(LANES):
            v = wide_b[n, pl.ds(pl.multiple_of(m * 64, 64), 64), :].astype(BF16)
            t1[pl.ds(m * 2, 2), :, n * 128:(n + 1) * 128] = v.reshape(2, BLK, 128)
        return 0

    lax.fori_loop(0, 32, narrow, 0)
    send_mixed(*BEFORE_COLS)

    def slopes(m, _):
        rows = pl.ds(pl.multiple_of(m * 64, 64), 64)
        for n in range(LANES):
            wide_b[n, rows, :] = gelu_slope(wide_b[n, rows, :])
        return 0

    lax.fori_loop(0, 32, slopes, 0)

    for e in range(4):
        wait_chunk(1, e)
        for t in range(4):
            jj = place(e, t, -1)
            rows = pl.ds(pl.multiple_of(jj * 128, 128), 128)
            v = r2[pl.ds(jj * 4, 4)].reshape(128, CG).astype(F32)
            for n in range(LANES):
                wide_a[n, rows, :] = v[:, n * 128:(n + 1) * 128] * wide_b[n, rows, :]
    for q in range(QB):
        gmb[q] = column(q).astype(BF16)

    for e in range(4):
        spots = [place(e, t, 1) for t in range(4)]
        lhs = jnp.concatenate([lt[pl.ds(pl.multiple_of(jj * 16, 16), 16), :] for jj in spots], axis=0)
        for q in range(QB):
            v = dot(lhs, gmb[q], 1, 0)
            for t, jj in enumerate(spots):
                for n in range(LANES):
                    wide_c[n, pl.ds(jj * 128 + q, 16, stride=QB), :] = v[t * 16:(t + 1) * 16, n * 128:(n + 1) * 128]
        for jj in spots:
            rows = pl.ds(pl.multiple_of(jj * 128, 128), 128)
            for n in range(LANES):
                v = wide_c[n, rows, :].astype(BF16)
                t2[pl.ds(jj * 4, 4), :, n * 128:(n + 1) * 128] = v.reshape(4, BLK, 128)
        send_chunk(t2, b2, 3, e)
    send_mixed(*AFTER_COLS)
    gl_acc = jnp.zeros((P_ALL, P_ALL), F32)
    for q in range(QB):
        gl_acc = gl_acc + dot(gmb[q], colsb[q], 1, 1)
    ls_s[...] = gl_acc.astype(BF16).reshape(XY, 16, P_ALL)

    def scatter(src, dst, n, e):
        for t in range(1 if e == 0 else 0, 4):
            jj = place(e, t, -1)
            pltpu.make_async_remote_copy(
                src_ref=src.at[jj], dst_ref=dst.at[j], send_sem=m_send.at[n], recv_sem=m_recv.at[n],
                device_id={"inner": jj * ZH + zh}, device_id_type=MESH,
            ).start()

    for e in range(4):
        scatter(ls_s, ls_r, 0, e)
    ls_r[j] = ls_s[j]

    def hand_out(src, dst, rows, n):
        pltpu.make_async_copy(src.at[my_rows, rows], dst.at[0, :, rows, mine], l_sem.at[n]).start()
        pltpu.make_async_remote_copy(
            src_ref=src.at[their_rows, rows], dst_ref=dst.at[0, :, rows, mine],
            send_sem=e_send.at[n], recv_sem=e_recv.at[n],
            device_id={"outer": 1 - c}, device_id_type=MESH,
        ).start()

    def gate_chip(jj):
        rows = pl.ds(pl.multiple_of(jj * 32, 32), 32)
        v = b1[pl.ds(jj * 4, 4)].astype(F32)
        for p in range(CHIP):
            act = gelu_value(v[:, p * QB:(p + 1) * QB, :].reshape(32, CG))
            ggate_v[p, rows, :] = (gout[p, rows, :].astype(F32) * act).astype(BF16)
        hand_out(ggate_v, ggate_o, rows, 6)

    def gate_grad(e):
        wait_chunk(2, e)

        def step(t, _):
            gate_chip(source(e, t))
            return 0

        lax.fori_loop(0, 4, step, 0)

    for e in range(4):
        wait_chunk(3, e)
        spots = [place(e, t, -1) for t in range(4)]
        parts = [[] for _ in range(CHIP)]
        for jj in spots:
            rows = pl.ds(pl.multiple_of(jj * 32, 32), 32)
            v = b2[pl.ds(jj * 4, 4)].astype(F32)
            for p in range(CHIP):
                part = v[:, p * QB:(p + 1) * QB, :].reshape(32, CG).astype(BF16)
                gcb[p, rows, :] = part
                parts[p].append(part)
        total = None
        for p in range(CHIP):
            term = dot(jnp.concatenate(parts[p], axis=0), x[p], 1, 1)
            total = term if total is None else total + term
        for t, jj in enumerate(spots):
            rs_s[jj] = total[t * 32:(t + 1) * 32, :].astype(BF16)
        scatter(rs_s, rs_r, 1, e)
    rs_r[j] = rs_s[j]
    send_mixed(*AFTER_PLANE)

    def input_grad(m, _):
        rows = pl.ds(pl.multiple_of(m * 128, 128), 128)
        for p in range(CHIP):
            gin_v[p, rows, :] = dot(rt[rows, :], gcb[p], 1, 0).astype(BF16)
        hand_out(gin_v, gin_o, rows, 5)
        return 0

    lax.fori_loop(0, 4, input_grad, 0)

    gate_grad(0)

    wait_bytes(ls_r.at[pl.ds(0, XY - 1)], m_recv.at[0])
    wait_bytes(rs_r.at[pl.ds(0, XY - 1)], m_recv.at[1])
    gr_sum = rs_r[0].astype(F32)
    gl_sum = ls_r[0].astype(F32)
    for k in range(1, XY):
        gr_sum = gr_sum + rs_r[k].astype(F32)
        gl_sum = gl_sum + ls_r[k].astype(F32)
    share[0:32, :] = gr_sum[:, 0:256].astype(BF16)
    share[32:64, :] = gr_sum[:, 256:512].astype(BF16)
    share[64:80, :] = gl_sum.astype(BF16)

    def to_z(k):
        return pltpu.make_async_remote_copy(
            src_ref=share, dst_ref=zrecv.at[zh * 2 + d], send_sem=m_send.at[2], recv_sem=m_recv.at[2],
            device_id={"inner": j * ZH + (zh + k) % ZH, "dp": c}, device_id_type=MESH,
        )

    for k in range(1, ZH):
        to_z(k).start()

    @pl.when(d != c)
    def _():
        to_z(0).start()

    send_mixed(*AFTER_Z)
    gate_grad(1)

    @pl.when(d == c)
    def _():
        zrecv[zh * 2 + d] = share[...]
        wait_bytes(zrecv.at[pl.ds(0, 7)], m_recv.at[2])
        total = zrecv[0].astype(F32)
        for k in range(1, 8):
            total = total + zrecv[k].astype(F32)
        fin[j] = total.astype(BF16)

        for e in range(4):
            for t in range(1 if e == 0 else 0, 4):
                pltpu.make_async_remote_copy(
                    src_ref=fin.at[j], dst_ref=fin.at[j], send_sem=m_send.at[3], recv_sem=m_recv.at[3 + e],
                    device_id={"inner": place(e, t, 1) * ZH + zh}, device_id_type=MESH,
                ).start()

    send_mixed(*AFTER_SHARES)
    gate_grad(2)

    def last_gate(t):
        wait_bytes(t1.at[pl.ds(0, ZH)], a_recv.at[13 + t])
        gate_chip(place(3, t, -1))

    def unpack():
        for k in range(XY):
            gr_o[0, k * 32:(k + 1) * 32, 0:256] = fin[k, 0:32, :].astype(F32)
            gr_o[0, k * 32:(k + 1) * 32, 256:512] = fin[k, 32:64, :].astype(F32)
            gl_o[0, k * 16:(k + 1) * 16, :] = fin[k, 64:80, :].astype(F32)

    @pl.when(d == c)
    def _():
        for e in range(4):
            wait_bytes(fin.at[pl.ds(0, 3 if e == 0 else 4)], m_recv.at[3 + e])
            for t in range(4):
                jj = place(e, t, -1)
                pltpu.make_async_remote_copy(
                    src_ref=fin.at[jj], dst_ref=fin.at[jj], send_sem=m_send.at[4], recv_sem=m_recv.at[7],
                    device_id={"outer": 1 - c}, device_id_type=MESH,
                ).start()
        unpack()

    for t in range(4):
        last_gate(t)

    @pl.when(d == c)
    def _():
        wait_bytes(fin.at[pl.ds(0, XY - 1)], m_send.at[3])
        wait_bytes(zrecv.at[pl.ds(0, 3)], m_send.at[2])
        wait_bytes(fin, m_send.at[4])

    @pl.when(d != c)
    def _():
        wait_bytes(zrecv.at[pl.ds(0, 4)], m_send.at[2])
        wait_bytes(fin, m_recv.at[7])
        unpack()

    for n in range(4):
        wait_bytes(t1, a_send.at[n])
    wait_bytes(ls_r.at[pl.ds(0, XY - 1)], m_send.at[0])
    wait_bytes(rs_r.at[pl.ds(0, XY - 1)], m_send.at[1])
    for gift in gifts:
        gift.wait_send()
    half = ggate_v.at[pl.ds(0, ROWS)]
    for n in (5, 6):
        wait_bytes(half, l_sem.at[n])
        wait_bytes(half, e_send.at[n])
        wait_bytes(half, e_recv.at[n])


def hand_on(*refs):
    results, outputs, sem = refs[:4], refs[4:8], refs[8]
    parts = []
    for src, dst in zip(results[:2], outputs[:2]):
        for p in range(ROWS):
            parts.append((src.at[0, p], dst.at[0, p]))
    parts.extend(zip(results[2:], outputs[2:]))
    copies = [pltpu.make_async_copy(src, dst, sem.at[n]) for n, (src, dst) in enumerate(parts)]
    for copy in copies:
        copy.start()
    for copy in copies:
        copy.wait()


def body(*operands):
    hbm = pl.BlockSpec(memory_space=pl.ANY)
    shapes = (
        ((1, ROWS, Q, 2 * CG), BF16),
        ((1, ROWS, Q, 2 * CG), BF16),
        ((1, Q, Q), F32),
        ((1, P_ALL, P_ALL), F32),
    )
    blocks = pltpu.VMEM((INNER, BLK, CG), BF16)
    rows = pltpu.VMEM((CHIP, Q, CG), BF16)
    wide = pltpu.VMEM((LANES, INNER * BLK, 128), F32)
    columns = pltpu.VMEM((QB, P_ALL, CG), BF16)
    scratch = [blocks] * 8 + [
        rows, rows, rows,
        pltpu.VMEM((Q, Q), BF16),
        pltpu.VMEM((P_ALL, P_ALL), BF16),
        rows, rows,
        wide, wide, wide,
        columns, columns,
        rows,
        pltpu.VMEM((Q, Q), BF16),
        pltpu.VMEM((P_ALL, P_ALL), BF16),
        pltpu.VMEM((XY, 32, Q), BF16),
        pltpu.VMEM((XY, 32, Q), BF16),
        pltpu.VMEM((XY, 16, P_ALL), BF16),
        pltpu.VMEM((XY, 16, P_ALL), BF16),
        pltpu.VMEM((80, 256), BF16),
        pltpu.VMEM((8, 80, 256), BF16),
        pltpu.VMEM((XY, 80, 256), BF16),
        pltpu.SemaphoreType.DMA((4,)),
        pltpu.SemaphoreType.DMA((17,)),
        pltpu.SemaphoreType.DMA((5,)),
        pltpu.SemaphoreType.DMA((8,)),
        pltpu.SemaphoreType.DMA((7,)),
        pltpu.SemaphoreType.DMA((7,)),
        pltpu.SemaphoreType.DMA((9,)),
    ]
    results = pl.pallas_call(
        kernel,
        out_shape=tuple(pltpu.VMEM(*shape) for shape in shapes),
        in_specs=[hbm] * 5,
        out_specs=(pl.BlockSpec(memory_space=pltpu.VMEM),) * 4,
        scratch_shapes=scratch,
        compiler_params=pltpu.CompilerParams(
            collective_id=0, has_side_effects=True, vmem_limit_bytes=52 * 1024 * 1024
        ),
        cost_estimate=pl.CostEstimate(flops=4 * 10**9, bytes_accessed=12 * 10**6, transcendentals=3 * 10**6),
    )(*(pltpu.with_memory_space_constraint(a, pltpu.HBM) for a in operands))
    return pl.pallas_call(
        hand_on,
        out_shape=tuple(jax.ShapeDtypeStruct(*shape) for shape in shapes),
        in_specs=[pl.BlockSpec(memory_space=pltpu.VMEM)] * 4,
        out_specs=(hbm,) * 4,
        scratch_shapes=[pltpu.SemaphoreType.DMA((6,))],
        compiler_params=pltpu.CompilerParams(vmem_limit_bytes=8 * 1024 * 1024),
        cost_estimate=pl.CostEstimate(flops=0, bytes_accessed=9 * 10**6, transcendentals=0),
    )(*(pltpu.with_memory_space_constraint(a, pltpu.VMEM) for a in results))


def solution(mesh):
    rows = P("dp", ("inner", "outer"), None, None)
    return jax.shard_map(
        body,
        mesh=mesh,
        in_specs=(rows, rows, rows, P(), P()),
        out_specs=(rows, rows, P("dp", None, None), P("dp", None, None)),
        check_vma=False,
    )
```
